32 devices in a mesh: groups: 2 (over y), tiles: 4 (over z), levels: 2 (over x), sub: 2 (over core).
Axes of the slice: x: 2, y: 2, z: 4, core: 2. Of those that a mesh axis runs over, the one named last changes fastest.
Arguments:
- final_adjoint: float32 [6, 18, 16, 720], P('groups', 'levels', 'tiles', 'sub'), parts along dimension 0, may hold values from -6 to 6
- lon_courant: float32 [36, 16, 720], P(('groups', 'levels'), 'tiles', 'sub'), parts along dimension 0, may hold values from 0.02 to 0.24
- lat_courant: float32 [36, 16, 720], P(('groups', 'levels'), 'tiles', 'sub'), parts along dimension 0, may hold values from 0.02 to 0.24
- upwind_flags: int32 [2, 36, 16, 720], P(None, ('groups', 'levels'), 'tiles', 'sub'), parts along dimension 1, may hold values 0 or 1
- vertical_mixing: float32 [36, 16, 720], P(('groups', 'levels'), 'tiles', 'sub'), parts along dimension 0, may hold values from 0.01 to 0.45
- level_profile: float32 [18], P('levels'), may hold values from 0.01 to 0.1
- sounding_owner: int32 [6144, 1], P(('groups', 'tiles', 'sub')), parts along dimension 0, may hold values from 0 to 7; in each aligned block of 384 rows (0 to 383, 384 to 767, ...) at most 128 rows name the same one
- sounding_target: int32 [6144], P(('groups', 'tiles', 'sub')), parts along dimension 0, may hold values from 0 to 8639
- misfit: float32 [3, 6144], P(None, ('groups', 'tiles', 'sub')), parts along dimension 1, may hold values from -6 to 6
- averaging_kernel: float32 [18, 6144], P('levels', ('groups', 'tiles', 'sub')), parts along dimension 1, may hold values from 0.2 to 1.5
Outputs:
- adjoint_state: float32 [6, 18, 16, 720], P('groups', 'levels', 'tiles', 'sub'), parts along dimension 0
- flux_gradient: float32 [6, 16, 720], P('groups', ('tiles', 'levels'), 'sub'), parts along dimension 0
The draws below stay inside these ranges and needn't reach their ends.
There are 2 independent parts, one for each index of `groups`. The reference program is written for one: setup_inputs(seed, part) draws one part's arguments, and reference() takes and returns one part's arrays. A program takes and returns all parts, laid end to end along the dimension named above; an argument that names none is the same for every part. Nothing has to cross between parts.
Inputs may be any that keep to these rules, and one draw needn't show every extreme that they name: `sounding_owner`: in the rows of one device, at most 128 soundings name one owner, a bound that some block reaches of them.
All inputs are finite; a program needn't handle non-finite values. No bound on the sum of `upwind_flags` on one device may be relied on, other than what follows from the above.
Results may differ from the reference program's by a relative error of at most 0.0001.
Values sent between devices are 32-bit elements; how exact they have to be, the bound alone decides.
No kernel may reach another device: no remote copies, remote signals or barrier semaphores. Data moves between devices by JAX's collectives and lax.ppermute only.
A program may use at most 128 MiB of HBM per device.

```python
import math
import jax
import jax.numpy as jnp
import numpy as np

TRACERS = 3
STEPS = 6
CAP = 128
RLAT = 4
CLON = 360
OWNERS = 8
SND_DEV = 384
SOUNDINGS = 3072
LEVELS = 18
LAT = 16
LON = 720
N_SUB = 2


def with_ends(entries, stream_key, low, largest):
    longest = entries.shape.index(max(entries.shape))
    spots = []
    for shift in (0, 1):
        where = [jax.random.randint(jax.random.fold_in(stream_key, axis), (), 0, length) for axis, length in enumerate(entries.shape)]
        where[longest] = (where[longest] + shift) % entries.shape[longest]
        spots.append(tuple(where))
    return entries.at[spots[0]].set(low).at[spots[1]].set(largest)


def steps_of(rng, dims, pieces, low, largest):
    level = 1.0
    for axis_at, shards_of in pieces:
        heights = jax.random.uniform(jax.random.fold_in(jax.random.fold_in(rng, 6), axis_at), (shards_of,), jnp.float32, low / len(pieces), largest / len(pieces))
        level = level * jnp.repeat(jnp.exp(heights), dims[axis_at] // shards_of).reshape((-1,) + (1,) * (len(dims) - 1 - axis_at))
    return level


def shared_out(own_key, own, number, rows, amount, top, most, lean):
    sequence = jax.random.permutation(own_key, amount)
    packed, common = load_shares(amount, rows * top, most, lean, True), load_shares(amount, rows * top, most, lean, False)
    places = jnp.arange(amount)

    def named(sizes, rotation):
        used = int((sizes > 0).sum())
        fixed = max(1, used // 4)
        moved = fixed + (places - fixed + rotation * (used - fixed)) % max(1, amount - fixed)
        return jnp.zeros((amount,), jnp.int32).at[sequence[jnp.where(places < fixed, places, moved)]].set(jnp.asarray(sizes, jnp.int32))

    sizes = jnp.where(number % 4 == 0, named(packed, number // 4), named(common, number - number // 4 - 1))
    mixed = jax.random.permutation(jax.random.fold_in(own, 3), amount)
    donor, sink = mixed[0:amount // 2 * 2:2], mixed[1:amount // 2 * 2:2]
    slack = jnp.minimum(sizes[donor] - 1, most - sizes[sink]) // 2
    slack = jnp.where((donor == sequence[0]) | (sink == sequence[0]) | (sizes[sink] == 0), 0, jnp.maximum(slack, 0))
    moved = jax.random.randint(jax.random.fold_in(own, 4), (amount // 2,), 0, 1 << 20) % (slack + 1)
    sizes = sizes.at[donor].add(-moved).at[sink].add(moved)
    items = jnp.searchsorted(jnp.cumsum(sizes), jnp.arange(rows * top), side="right").astype(jnp.int32)
    table = items.reshape(top, rows).T
    table = table[jax.random.permutation(jax.random.fold_in(own, 1), rows)]
    rotation = jax.random.randint(jax.random.fold_in(own, 2), (rows, 1), 0, top)
    return jnp.take_along_axis(table, (jnp.arange(top)[None, :] + rotation) % top, axis=1)


def load_shares(count, total, most, slope, full):
    loads = [(1 << 20) // math.isqrt(grade ** slope) + 1 for grade in range(1, count + 1)]
    largest = most if full else min(most, max(-(-total // count), total * loads[0] // sum(loads)))
    least = 1 if total - largest >= count - 1 else 0
    given, spare = [largest] + [least] * (count - 1), total - largest - least * (count - 1)
    while spare > 0:
        movable = [i for i in range(1, count) if given[i] < largest] or [i for i in range(1, count) if given[i] < most]
        pool, budget = sum([loads[i] for i in movable]), spare
        for i in movable:
            addition = min(most - given[i], max(1, budget * loads[i] // pool), spare)
            given[i] = given[i] + addition
            spare = spare - addition
    return np.array(given)


def bell_draw(own_key, dims, width, reach, shards=(), dtype=jnp.bfloat16):
    entries = width * jax.random.normal(own_key, dims, jnp.float32)
    if shards:
        entries = entries * steps_of(own_key, dims, shards, -0.22, 0.18)
    return jnp.clip(entries, -reach, reach).astype(dtype)


def setup_inputs(seed: int = 0, part: int = 0) -> dict:
    seeds = jax.random.split(jax.random.key(seed), 11)
    own_keys = jax.random.split(jax.random.fold_in(seeds[10], part), 11)
    final_adjoint = bell_draw(own_keys[0], (TRACERS, LEVELS, LAT, LON), 1.0, 6.0, ((1, 2), (2, 4), (3, 2)), jnp.float32)
    lon_courant = jnp.clip(jnp.exp(math.log(0.24) - 2.4849066 * jax.random.uniform(own_keys[1], (LEVELS, LAT, LON), jnp.float32) ** steps_of(own_keys[1], (LEVELS, LAT, LON), ((0, 2), (1, 4), (2, 2)), -0.2, 0.2)), 0.02, 0.24)
    lat_courant = jnp.clip(jnp.exp(math.log(0.24) - 2.4849066 * jax.random.uniform(own_keys[2], (LEVELS, LAT, LON), jnp.float32) ** steps_of(own_keys[2], (LEVELS, LAT, LON), ((0, 2), (1, 4), (2, 2)), -0.2, 0.2)), 0.02, 0.24)
    upwind_flags = with_ends((jax.random.randint(own_keys[3], (2, LEVELS, LAT, LON), 0, 2) < 1).astype(jnp.int32), jax.random.fold_in(own_keys[3], 1), 0, 1)
    vertical_mixing = jnp.clip(jnp.exp(math.log(0.45) - 3.8066625 * jax.random.uniform(own_keys[4], (LEVELS, LAT, LON), jnp.float32) ** steps_of(own_keys[4], (LEVELS, LAT, LON), ((0, 2), (1, 4), (2, 2)), -0.2, 0.2)), 0.01, 0.45)
    level_profile = jnp.clip(jnp.exp(math.log(0.1) - 2.3025851 * jax.random.uniform(seeds[5], (LEVELS,), jnp.float32) ** steps_of(seeds[5], (LEVELS,), ((0, 2),), -0.2, 0.2)), 0.01, 0.1)
    sounding_owner_keys = jax.random.split(jax.random.fold_in(own_keys[6], 1), SOUNDINGS // SND_DEV)
    sounding_owner_turns = jax.random.permutation(jax.random.fold_in(own_keys[6], 3), SOUNDINGS // SND_DEV)
    sounding_owner = jax.vmap(lambda own, number: shared_out(jax.random.fold_in(own_keys[6], 2), own, number, SND_DEV, OWNERS, 1, CAP, 2))(sounding_owner_keys, sounding_owner_turns).reshape((SOUNDINGS, 1))
    sounding_target = with_ends(jax.random.randint(own_keys[7], (SOUNDINGS,), 0, STEPS * RLAT * CLON), jax.random.fold_in(own_keys[7], 1), 0, (STEPS * RLAT * CLON) - 1).astype(jnp.int32)
    misfit = bell_draw(own_keys[8], (TRACERS, SOUNDINGS), 1.0, 6.0, ((1, 8),), jnp.float32)
    averaging_kernel = jnp.clip(0.2 + 1.3 * jax.random.uniform(own_keys[9], (LEVELS, SOUNDINGS), jnp.float32) ** steps_of(own_keys[9], (LEVELS, SOUNDINGS), ((0, 2), (1, 8)), -0.2, 0.2), 0.2, 1.5)
    return dict(final_adjoint=final_adjoint, lon_courant=lon_courant, lat_courant=lat_courant, upwind_flags=upwind_flags, vertical_mixing=vertical_mixing, level_profile=level_profile, sounding_owner=sounding_owner, sounding_target=sounding_target, misfit=misfit, averaging_kernel=averaging_kernel)


def shift_from_below(field, axis):
    size = field.shape[axis]
    zero_shape = list(field.shape)
    zero_shape[axis] = 1
    zeros = jnp.zeros(zero_shape, jnp.float32)
    kept = jax.lax.slice_in_dim(field, 0, size - 1, axis=axis)
    return jnp.concatenate([zeros, kept], axis=axis)


def shift_from_above(field, axis):
    size = field.shape[axis]
    zero_shape = list(field.shape)
    zero_shape[axis] = 1
    zeros = jnp.zeros(zero_shape, jnp.float32)
    kept = jax.lax.slice_in_dim(field, 1, size, axis=axis)
    return jnp.concatenate([kept, zeros], axis=axis)


def reference(final_adjoint, lon_courant, lat_courant, upwind_flags, vertical_mixing, level_profile, sounding_owner, sounding_target, misfit, averaging_kernel):
    flags = upwind_flags.astype(jnp.float32)
    row_open = (jnp.arange(LAT) < LAT - 1).astype(jnp.float32)[None, :, None]
    level_open = (jnp.arange(LEVELS) < LEVELS - 1).astype(jnp.float32)[:, None, None]
    east = lon_courant * flags[0]
    west = jnp.roll(lon_courant * (1.0 - flags[0]), 1, axis=2)
    north = lat_courant * flags[1] * row_open
    south = shift_from_below(lat_courant * (1.0 - flags[1]) * row_open, 1)
    upward = vertical_mixing * level_open
    downward = shift_from_below(upward, 0)
    owner = sounding_owner[:, 0]
    columns_dev = RLAT * CLON
    step_of = sounding_target // columns_dev
    cell = sounding_target % columns_dev
    row_ids = (owner // N_SUB) * RLAT + cell // CLON
    col_ids = (owner % N_SUB) * CLON + cell % CLON
    flat_ids = (row_ids * LON + col_ids).astype(jnp.int32)
    values = misfit[:, None, :] * averaging_kernel[None, :, :]
    adjoint = final_adjoint
    flux_gradient = jnp.zeros((TRACERS, LAT, LON), jnp.float32)
    for step_index in range(STEPS):
        below = shift_from_below(adjoint, 1)
        above = shift_from_above(adjoint, 1)
        mixed = adjoint + upward * (above - adjoint) + downward * (below - adjoint)
        east_vals = jnp.roll(mixed, -1, axis=3)
        west_vals = jnp.roll(mixed, 1, axis=3)
        north_vals = shift_from_above(mixed, 2)
        south_vals = shift_from_below(mixed, 2)
        moved = mixed + east * (east_vals - mixed) + west * (west_vals - mixed)
        moved = moved + north * (north_vals - mixed) + south * (south_vals - mixed)
        chosen = values * (step_of == step_index).astype(jnp.float32)[None, None, :]
        forcing = jnp.zeros((TRACERS, LEVELS, LAT * LON), jnp.float32).at[:, :, flat_ids].add(chosen)
        adjoint = moved + forcing.reshape(TRACERS, LEVELS, LAT, LON)
        flux_gradient = flux_gradient + jnp.sum(adjoint * level_profile[None, :, None, None], axis=1)
    return adjoint, flux_gradient
```

```python
import functools

import jax
import jax.numpy as jnp
from jax import lax
from jax.experimental import pallas as pl
from jax.experimental.pallas import tpu as pltpu
from jax.sharding import PartitionSpec as P

STEPS = 6
WIDTH = 2
ROUNDS = STEPS // WIDTH
LANES = 128
CHUNK = 3072
F32 = jnp.float32
BF16 = jnp.bfloat16
VMEM = pl.BlockSpec(memory_space=pltpu.VMEM)
SMEM = pl.BlockSpec(memory_space=pltpu.SMEM)
PARAMS = pltpu.CompilerParams(vmem_limit_bytes=48 * 1024 * 1024)


def window(margin, levels):
    count = lax.axis_size("levels")
    if count == 1:
        return 0, levels
    if count == 2:
        return lax.axis_index("levels") * (STEPS - margin), levels + margin
    return STEPS - margin, levels + 2 * margin


def level_moves(levels):
    count = lax.axis_size("levels")
    band = lax.axis_index("levels")
    if count == 1:
        return []
    if count == 2:
        return [([(0, 1), (1, 0)], (levels - STEPS) * (1 - band), levels * (1 - band))]
    up = [(i, i + 1) for i in range(count - 1)]
    down = [(i + 1, i) for i in range(count - 1)]
    return [(up, levels - STEPS, 0), (down, 0, STEPS + levels)]


def move(value, tile_step, level_pairs=None):
    tiles, bands = lax.axis_size("tiles"), lax.axis_size("levels")
    if level_pairs is None:
        level_pairs = [(i, i) for i in range(bands)]
    pairs = [
        (tile * bands + source, (tile + tile_step) * bands + target)
        for tile in range(tiles)
        for source, target in level_pairs
        if 0 <= tile + tile_step < tiles
    ]
    return lax.ppermute(value, ("tiles", "levels"), pairs)


def own_planes(adj, lon, lat, flags, mix):
    tracers, levels, rows, _ = adj.shape
    last_band = lax.axis_index("levels") == lax.axis_size("levels") - 1
    last_tile = lax.axis_index("tiles") == lax.axis_size("tiles") - 1
    shape = lon.shape
    level_ids = lax.broadcasted_iota(jnp.int32, shape, 0)
    row_ids = lax.broadcasted_iota(jnp.int32, shape, 1)
    top = (level_ids == levels - 1) & last_band
    shut = (row_ids == rows - 1) & last_tile
    first = flags[0].astype(F32)
    second = flags[1].astype(F32)
    lat_open = jnp.where(shut, 0.0, lat[...])
    planes = [adj[t] for t in range(tracers)]
    planes.append(jnp.where(top, 0.0, mix[...]))
    planes.append(lon[...] * first)
    planes.append(lon[...] * (1.0 - first))
    planes.append(lat_open * second)
    planes.append(lat_open * (1.0 - second))
    return planes


def edges_kernel(adj, lon, lat, flags, mix, misfit, kernel, owner, target, edge_out, pay_out, buf):
    tracers, levels, rows, columns = adj.shape
    width = edge_out.shape[-1]
    tail = columns // LANES * LANES
    buf[...] = jnp.zeros_like(buf)
    for p, plane in enumerate(own_planes(adj, lon, lat, flags, mix)):
        buf[0, p, :, 0:rows, :] = plane[:, :, 0:LANES]
        buf[1, p, :, 0:rows, 0 : columns - tail] = plane[:, :, tail:]
    lane = lax.broadcasted_iota(jnp.int32, (8, LANES), 1)
    gap = columns - tail
    for p in range(buf.shape[1]):
        for l in range(levels):
            start = pltpu.roll(buf[0, p, l], gap, 1)
            end = pltpu.roll(buf[1, p, l], width - gap, 1)
            both = jnp.where(
                lane >= width - STEPS,
                end,
                jnp.where((lane >= gap) & (lane < gap + STEPS), start, 0.0),
            )
            edge_out[p, l] = both[0:rows]
    pay_out[...] = jnp.zeros_like(pay_out)
    pay_out[0:tracers] = misfit[...]
    pay_out[tracers : tracers + levels] = kernel[...]
    pay_out[tracers + levels : tracers + levels + 1] = owner[...].astype(F32)
    pay_out[tracers + levels + 1 : tracers + levels + 2] = target[...].astype(F32)


def pack_kernel(moves, adj, lon, lat, flags, mix, edge, own_out, north_out, south_out, *rest):
    tracers, levels, rows, columns = adj.shape
    tail = columns // LANES * LANES
    gap = columns - tail
    buf = rest[-1]
    outs = rest[:-1]
    buf[...] = jnp.zeros_like(buf)
    lane = lax.broadcasted_iota(jnp.int32, (levels, rows, LANES), 2)
    for p, plane in enumerate(own_planes(adj, lon, lat, flags, mix)):
        buf[p, :, 0:rows, 0:columns] = plane
        last = buf[p, :, 0:rows, tail : tail + LANES]
        buf[p, :, 0:rows, tail : tail + LANES] = jnp.where(lane < gap, last, edge[p])
    mixing, east, west, north, south = range(tracers, tracers + 5)
    own_out[...] = buf[:, :, 0:rows, :]

    def rows_of(out, first, row, single, with_south, start, count):
        pick = pl.ds(start, count)
        entry = 0
        planes = list(range(tracers)) + [mixing, north] + ([south] if with_south else [])
        for p in planes:
            out[entry] = buf[p, pick, first : first + WIDTH, :]
            entry += 1
        out[entry, :, 0:1, :] = buf[east, pick, single : single + 1, :]
        out[entry, :, 1:2, :] = buf[west, pick, single : single + 1, :]

    rows_of(north_out, rows - WIDTH, rows, rows - 1, True, 0, levels)
    rows_of(south_out, 0, rows, 0, False, 0, levels)
    for i, (_, start, _) in enumerate(moves()):
        level_out, north_far, south_far = outs[3 * i : 3 * i + 3]
        level_out[...] = buf[:, pl.ds(start, STEPS), 0:rows, :]
        rows_of(north_far, rows - WIDTH, rows, rows - 1, True, start, STEPS)
        rows_of(south_far, 0, rows, 0, False, start, STEPS)


def advance(step, src, dst, coef, forcing, index, profile, flux, levels):
    tracers = src.shape[0]
    first, count = window(STEPS - 1 - step, levels)
    own, _ = window(0, levels)
    lanes = src.shape[-1]
    total = [flux[t] for t in range(tracers)]
    for i in range(count):
        at = first + i
        up, down = coef[0, at + 1], coef[0, at]
        east, west, north, south = (coef[c, at + 1] for c in range(1, 5))
        own_id = at - own
        inside = (own_id >= 0) & (own_id < levels)
        weight = jnp.where(inside, profile[jnp.clip(own_id, 0, levels - 1)], 0.0)
        for t in range(tracers):
            a = src[t, at + 1]
            b = a + up * (src[t, at + 2] - a) + down * (src[t, at] - a)
            moved = b + east * (pltpu.roll(b, lanes - 1, 1) - b) + west * (pltpu.roll(b, 1, 1) - b)
            moved = moved + north * (pltpu.roll(b, 7, 0) - b) + south * (pltpu.roll(b, 1, 0) - b)
            new = moved + forcing[index, t, at]
            dst[t, at + 1] = new
            total[t] = total[t] + weight * new
    for t in range(tracers):
        flux[t] = total[t]


def clear_pads(ref):
    levels = ref.shape[1]
    ref[:, 0:1] = jnp.zeros((ref.shape[0], 1) + ref.shape[2:], F32)
    ref[:, levels - 1 : levels] = jnp.zeros((ref.shape[0], 1) + ref.shape[2:], F32)


def run_steps(number, work, other, coef, forcing, profile, flux, levels):
    refs = [work, other]
    for i in range(WIDTH):
        advance(number * WIDTH + i, refs[i % 2], refs[(i + 1) % 2], coef, forcing, i, profile, flux, levels)
    return refs[WIDTH % 2]


def send_rows(number, state, north_out, south_out, rows, levels):
    start, count = window(STEPS - (number + 1) * WIDTH, levels)
    north_out[...] = state[:, pl.ds(start + 1, count), rows - WIDTH : rows, :]
    south_out[...] = state[:, pl.ds(start + 1, count), 0:WIDTH, :]


def first_kernel(moves, *refs):
    number = len(moves())
    own, from_south, from_north = refs[:3]
    far = refs[3 : 3 + 3 * number]
    forcing, profile, state_out, coef_out, flux, north_out, south_out, work, other, raw = refs[3 + 3 * number :]
    planes, levels, rows, lanes = own.shape
    tracers = planes - 5
    mixing, east, west, north, south = range(tracers, tracers + 5)
    raw[...] = jnp.zeros_like(raw)
    flux[...] = jnp.zeros_like(flux)
    clear_pads(work)
    clear_pads(other)

    def place(start, count, body, below, above):
        pick = pl.ds(start + 1, count)
        lo, hi = slice(6, 6 + WIDTH), slice(rows, rows + WIDTH)
        for p in range(planes):
            ref, plane = (work, p) if p < tracers else (raw, p - tracers)
            ref[plane, pick, 0:rows, :] = body[p]
        for entry, p in enumerate(list(range(tracers)) + [mixing, north, south]):
            ref, plane = (work, p) if p < tracers else (raw, p - tracers)
            ref[plane, pick, lo, :] = below[entry]
            if p != south:
                ref[plane, pick, hi, :] = above[entry]
        for k, p in enumerate((east, west)):
            raw[p - tracers, pick, 7:8, :] = below[tracers + 3, :, k : k + 1, :]
            raw[p - tracers, pick, rows : rows + 1, :] = above[tracers + 2, :, k : k + 1, :]

    own_start, _ = window(0, levels)
    place(own_start, levels, own, from_south, from_north)
    for i, (_, _, slot) in enumerate(moves()):
        place(slot, STEPS, *far[3 * i : 3 * i + 3])
    coef_out[0] = raw[0]
    coef_out[1] = raw[1]
    coef_out[3] = raw[3]
    for l in range(raw.shape[1]):
        coef_out[2, l] = pltpu.roll(raw[2, l], 1, 1)
        coef_out[4, l] = pltpu.roll(raw[4, l], 1, 0)
    last = run_steps(0, work, other, coef_out, forcing, profile, flux, levels)
    state_out[...] = last[...]
    send_rows(0, state_out, north_out, south_out, rows, levels)


def next_kernel(number, levels, rows, state, coef, from_south, from_north, forcing, profile, flux_in, *refs):
    work, other = refs[-2:]
    start, count = window(STEPS - number * WIDTH, levels)
    pick = pl.ds(start + 1, count)
    work[...] = state[...]
    work[:, pick, rows : rows + WIDTH, :] = from_north[...]
    work[:, pick, 6 : 6 + WIDTH, :] = from_south[...]
    clear_pads(other)
    if number < ROUNDS - 1:
        state_out, flux, north_out, south_out = refs[:-2]
        flux[...] = flux_in[...]
        last = run_steps(number, work, other, coef, forcing, profile, flux, levels)
        state_out[...] = last[...]
        send_rows(number, state_out, north_out, south_out, rows, levels)
        return
    adjoint, keep, give, flux = refs[:-2]
    flux[...] = flux_in[...]
    last = run_steps(number, work, other, coef, forcing, profile, flux, levels)
    own, _ = window(0, levels)
    columns = adjoint.shape[-1]
    adjoint[...] = last[:, pl.ds(own + 1, levels), 0:rows, 0:columns]
    if lax.axis_size("levels") == 2:
        half = rows // 2
        upper = lax.axis_index("levels") == 1
        low, high = flux[:, 0:half, 0:columns], flux[:, half:rows, 0:columns]
        keep[...] = jnp.where(upper, high, low)
        give[...] = jnp.where(upper, low, high)
    else:
        keep[...] = flux[:, 0:rows, 0:columns]
        give[...] = jnp.zeros_like(give)


def forcing_kernel(tracers, levels, rows, columns, got, out, left, right, terms, keys, kern):
    bands, sources, _, held = got.shape
    lanes = out.shape[-1]
    wide = out.shape[2]
    subs = lax.axis_size("sub")
    band, tile, sub = (lax.axis_index(name) for name in ("levels", "tiles", "sub"))
    own, _ = window(0, levels)
    for s in range(sources):
        cols = slice(s * held, (s + 1) * held)
        owner = got[band, s, tracers + levels : tracers + levels + 1, :]
        target = got[band, s, tracers + levels + 1 : tracers + levels + 2, :]
        cells = rows * columns
        step = jnp.floor((target + 0.5) * (1.0 / cells))
        cell = target - step * cells
        row = jnp.floor((cell + 0.5) * (1.0 / columns))
        col = cell - row * columns
        owner_tile = jnp.floor((owner + 0.5) * (1.0 / subs))
        owner_sub = owner - owner_tile * subs
        row = row + (owner_tile - tile.astype(F32)) * rows
        shift = owner_sub - sub.astype(F32)
        col = col + jnp.where(shift < 0, shift + subs, shift) * columns
        near = (row >= -2) & (row <= rows + 1)
        east_side = col < columns + STEPS
        west_side = col >= subs * columns - STEPS
        lane = jnp.where(east_side, col, jnp.where(west_side, col - subs * columns + lanes, -1.0))
        key = jnp.where(near, step * 8 + jnp.where(row < 0, row + 8, row), -1.0)
        keys[:, cols] = jnp.broadcast_to(key, (8, held))
        ids = lax.broadcasted_iota(jnp.int32, (lanes, held), 0).astype(F32)
        right[:, cols] = jnp.where(ids == lane, 1.0, 0.0).astype(BF16)
        for l in range(wide):
            level = band * levels + l - own
            source_band = jnp.clip(level // levels, 0, bands - 1)
            source_level = level - (level // levels) * levels
            kern[l, :, cols] = got[source_band, s, pl.ds(tracers + source_level, 1), :]
    for l in range(wide):
        for t in range(tracers):
            weights = [got[band, s, t : t + 1, :] for s in range(sources)]
            value = kern[l] * (jnp.concatenate(weights, axis=1) if sources > 1 else weights[0])
            high = value.astype(BF16).astype(F32)
            low = value - high
            both = [jnp.broadcast_to(x, (8, x.shape[1])) for x in (high, low)]
            terms[l * tracers + t] = jnp.concatenate(both, axis=0).astype(BF16)
    ids = lax.broadcasted_iota(jnp.int32, (8, keys.shape[1]), 0).astype(F32)
    for pair in range(STEPS // 2):
        first, count = window(STEPS - 1 - 2 * pair, levels)

        def one_step(odd, carry, pair=pair, first=first, count=count):
            step = 2 * pair + odd
            hit = jnp.where(keys[...] == ids + (step * 8).astype(F32), 1.0, 0.0)
            mask = jnp.concatenate([hit, hit], axis=0).astype(BF16)

            def fill(i, carry):
                left[pl.ds(pl.multiple_of(i * 16, 16), 16), :] = terms[first * tracers + i] * mask
                return carry

            lax.fori_loop(0, count * tracers, fill, 0)
            size = count * tracers * 16
            product = lax.dot_general(
                left[0:size, :], right[...], (((1,), (1,)), ((), ())), preferred_element_type=F32
            )
            for i in range(count):
                for t in range(tracers):
                    base = (i * tracers + t) * 16
                    value = product[base : base + 8] + product[base + 8 : base + 16]
                    place = (step, t, first + i)
                    if pl.num_programs(0) == 1:
                        out[place] = value
                    else:
                        old = jnp.where(pl.program_id(0) == 0, 0.0, out[place])
                        out[place] = old + value
            return carry

        lax.fori_loop(0, 2, one_step, 0)


def per_device(
    final_adjoint,
    lon_courant,
    lat_courant,
    upwind_flags,
    vertical_mixing,
    level_profile,
    sounding_owner,
    sounding_target,
    misfit,
    averaging_kernel,
):
    tracers, levels, rows, columns = final_adjoint.shape
    held = misfit.shape[1]
    bands, subs, tiles = (lax.axis_size(name) for name in ("levels", "sub", "tiles"))
    planes = tracers + 5
    lanes = -(-(columns + 2 * STEPS) // LANES) * LANES
    wide = window(STEPS, levels)[1]
    moves = functools.partial(level_moves, levels)
    shape = lambda *dims: jax.ShapeDtypeStruct(dims, F32)
    call = functools.partial(pl.pallas_call, compiler_params=PARAMS)
    fields = (final_adjoint, lon_courant, lat_courant, upwind_flags, vertical_mixing)

    pay_rows = -(-(tracers + levels + 2) // 8) * 8
    edge, payload = call(
        edges_kernel,
        out_shape=(shape(planes, levels, rows, LANES), shape(pay_rows, held)),
        in_specs=[VMEM] * 9,
        out_specs=(VMEM, VMEM),
        scratch_shapes=[pltpu.VMEM((2, planes, levels, 8, LANES), F32)],
        name="edges",
    )(*fields, misfit, averaging_kernel, sounding_owner.reshape(1, held), sounding_target.reshape(1, held))
    edge = lax.ppermute(edge, "sub", [(i, (i + 1) % subs) for i in range(subs)])
    gathered = lax.all_gather(payload, ("levels", "tiles", "sub"))
    gathered = gathered.reshape(bands, tiles * subs, pay_rows, held)

    sizes = []
    for count in [levels] + [STEPS] * len(moves()):
        if count != levels or sizes:
            sizes.append(shape(planes, count, rows, lanes))
        sizes.append(shape(tracers + 4, count, WIDTH, lanes))
        sizes.append(shape(tracers + 3, count, WIDTH, lanes))
    packed = call(
        functools.partial(pack_kernel, moves),
        out_shape=(shape(planes, levels, rows, lanes), *sizes),
        in_specs=[VMEM] * 6,
        out_specs=[VMEM] * (1 + len(sizes)),
        scratch_shapes=[pltpu.VMEM((planes, levels, 8, lanes), F32)],
        name="pack",
    )(*fields, edge)
    own = packed[0]
    received = [move(packed[1], 1), move(packed[2], -1)]
    for i, (pairs, _, _) in enumerate(moves()):
        level_part, north_part, south_part = packed[3 + 3 * i : 6 + 3 * i]
        received += [move(level_part, 0, pairs), move(north_part, 1, pairs), move(south_part, -1, pairs)]

    sources = max(1, min(tiles * subs, CHUNK // held))
    batch = sources * held
    chunks = tiles * subs // sources
    forcing = call(
        functools.partial(forcing_kernel, tracers, levels, rows, columns),
        out_shape=shape(STEPS, tracers, wide, 8, lanes),
        grid=(chunks,),
        in_specs=[pl.BlockSpec((bands, sources, pay_rows, held), lambda i: (0, i, 0, 0))],
        out_specs=pl.BlockSpec((STEPS, tracers, wide, 8, lanes), lambda i: (0, 0, 0, 0, 0)),
        scratch_shapes=[
            pltpu.VMEM((wide * tracers * 16, batch), BF16),
            pltpu.VMEM((lanes, batch), BF16),
            pltpu.VMEM((wide * tracers, 16, batch), BF16),
            pltpu.VMEM((8, batch), F32),
            pltpu.VMEM((wide, 1, batch), F32),
        ],
        name="forcing",
    )(gathered)

    def force_spec(number):
        return pl.BlockSpec((WIDTH, tracers, wide, 8, lanes), lambda i: (number, 0, 0, 0, 0))

    state_shape = (tracers, wide + 2, 8, lanes)
    coef_shape = (5, wide + 2, 8, lanes)
    flux_shape = (tracers, 8, lanes)

    def whole(dims):
        return pl.BlockSpec(dims, lambda i: (0,) * len(dims))

    def messages(number):
        count = window(STEPS - number * WIDTH, levels)[1]
        return shape(tracers, count, WIDTH, lanes)

    scratch = [pltpu.VMEM(state_shape, F32)] * 2
    inputs = [own, *received]
    outs = (shape(*state_shape), shape(*coef_shape), shape(*flux_shape), messages(1), messages(1))
    state, coef, flux, north, south = call(
        functools.partial(first_kernel, moves),
        out_shape=outs,
        grid=(1,),
        in_specs=[whole(x.shape) for x in inputs] + [force_spec(0), SMEM],
        out_specs=[whole(x.shape) for x in outs],
        scratch_shapes=scratch + [pltpu.VMEM(coef_shape, F32)],
        name="round0",
    )(*inputs, forcing, level_profile)
    half = rows // 2 if bands == 2 else rows
    for number in range(1, ROUNDS):
        inputs = [state, coef, move(north, 1), move(south, -1)]
        if number < ROUNDS - 1:
            outs = (shape(*state_shape), shape(*flux_shape), messages(number + 1), messages(number + 1))
            extra = []
        else:
            part = shape(tracers, half, columns)
            outs = (shape(tracers, levels, rows, columns), part, part)
            extra = [pltpu.VMEM(flux_shape, F32)]
        results = call(
            functools.partial(next_kernel, number, levels, rows),
            out_shape=outs,
            grid=(1,),
            in_specs=[whole(x.shape) for x in inputs] + [force_spec(number), SMEM, whole(flux_shape)],
            out_specs=[whole(x.shape) for x in outs],
            scratch_shapes=extra + scratch,
            name="round" + str(number),
        )(*inputs, forcing, level_profile, flux)
        if number < ROUNDS - 1:
            state, flux, north, south = results
    adjoint, keep, give = results
    if bands == 2:
        flux_gradient = keep + lax.ppermute(give, "levels", [(0, 1), (1, 0)])
    else:
        flux_gradient = lax.psum_scatter(keep, "levels", scatter_dimension=1, tiled=True)
    return adjoint, flux_gradient


def solution(mesh):
    return jax.shard_map(
        per_device,
        mesh=mesh,
        in_specs=(
            P("groups", "levels", "tiles", "sub"),
            P(("groups", "levels"), "tiles", "sub"),
            P(("groups", "levels"), "tiles", "sub"),
            P(None, ("groups", "levels"), "tiles", "sub"),
            P(("groups", "levels"), "tiles", "sub"),
            P("levels"),
            P(("groups", "tiles", "sub"), None),
            P(("groups", "tiles", "sub")),
            P(None, ("groups", "tiles", "sub")),
            P("levels", ("groups", "tiles", "sub")),
        ),
        out_specs=(P("groups", "levels", "tiles", "sub"), P("groups", ("tiles", "levels"), "sub")),
        check_vma=False,
    )
```

```python
import functools

import jax
import jax.numpy as jnp
from jax import lax
from jax.experimental import pallas as pl
from jax.experimental.pallas import tpu as pltpu
from jax.sharding import PartitionSpec as P

STEPS = 6
WIDTH = 2
ROUNDS = STEPS // WIDTH
LANES = 128
CHUNK = 3072
F32 = jnp.float32
BF16 = jnp.bfloat16
VMEM = pl.BlockSpec(memory_space=pltpu.VMEM)
SMEM = pl.BlockSpec(memory_space=pltpu.SMEM)
HBM = pl.BlockSpec(memory_space=pltpu.HBM)
MIB = 1024 * 1024


def window(margin, levels):
    count = lax.axis_size("levels")
    if count == 1:
        return 0, levels
    if count == 2:
        return lax.axis_index("levels") * (STEPS - margin), levels + margin
    return STEPS - margin, levels + 2 * margin


def level_moves(levels):
    count = lax.axis_size("levels")
    band = lax.axis_index("levels")
    if count == 1:
        return []
    if count == 2:
        return [([(0, 1), (1, 0)], (levels - STEPS) * (1 - band), levels * (1 - band))]
    up = [(i, i + 1) for i in range(count - 1)]
    down = [(i + 1, i) for i in range(count - 1)]
    return [(up, levels - STEPS, 0), (down, 0, STEPS + levels)]


def swap_tiles(value, odd):
    tiles = lax.axis_size("tiles")
    pairs = []
    for low in range(odd, tiles - 1, 2):
        pairs += [(low, low + 1), (low + 1, low)]
    return lax.ppermute(value, "tiles", pairs)


def is_even():
    return lax.rem(lax.axis_index("tiles"), 2) == 0


def own_planes(adj, lon, lat, flags, mix):
    tracers, levels, rows, _ = adj.shape
    last_band = lax.axis_index("levels") == lax.axis_size("levels") - 1
    last_tile = lax.axis_index("tiles") == lax.axis_size("tiles") - 1
    shape = lon.shape
    level_ids = lax.broadcasted_iota(jnp.int32, shape, 0)
    row_ids = lax.broadcasted_iota(jnp.int32, shape, 1)
    top = (level_ids == levels - 1) & last_band
    shut = (row_ids == rows - 1) & last_tile
    first = flags[0].astype(F32)
    second = flags[1].astype(F32)
    lat_open = jnp.where(shut, 0.0, lat[...])
    planes = [adj[t] for t in range(tracers)]
    planes.append(jnp.where(top, 0.0, mix[...]))
    planes.append(lon[...] * first)
    planes.append(lon[...] * (1.0 - first))
    planes.append(lat_open * second)
    planes.append(lat_open * (1.0 - second))
    return planes


def fetch(sources, targets, sems):
    copies = [pltpu.make_async_copy(x, y, sems.at[i]) for i, (x, y) in enumerate(zip(sources, targets))]
    for copy in copies:
        copy.start()
    for copy in copies:
        copy.wait()


def edges_kernel(*refs):
    inputs, (own_out, edge_out), held, buf, sems = refs[:5], refs[5:7], refs[7:12], refs[12], refs[13]
    fetch(inputs, held, sems)
    _, levels, rows, columns = held[0].shape
    width = edge_out.shape[-1]
    tail = columns // LANES * LANES
    gap = columns - tail
    buf[...] = jnp.zeros_like(buf)
    for p, plane in enumerate(own_planes(*held)):
        buf[p, :, 0:rows, 0:columns] = plane
    own_out[...] = buf[:, :, 0:rows, :]
    lane = lax.broadcasted_iota(jnp.int32, (8, LANES), 1)
    for p in range(buf.shape[0]):
        for l in range(levels):
            start = pltpu.roll(buf[p, l, :, 0:LANES], gap, 1)
            end = pltpu.roll(buf[p, l, :, tail : tail + LANES], width - gap, 1)
            both = jnp.where(
                lane >= width - STEPS,
                end,
                jnp.where((lane >= gap) & (lane < gap + STEPS), start, 0.0),
            )
            edge_out[p, l] = both[0:rows]


def payload_kernel(number, *refs):
    inputs, out, held, flat, sems = refs[: 4 + number], refs[4 + number], refs[5 + number : -2], refs[-2], refs[-1]
    fetch(inputs, held, sems)
    misfit, kernel, owner, target = held[:4]
    tracers, levels = misfit.shape[0], kernel.shape[0]
    base = tracers + 2
    flat[...] = jnp.zeros_like(flat)
    flat[0:tracers] = misfit[...]
    flat[tracers : tracers + 1] = owner[...].astype(F32)
    flat[tracers + 1 : base] = target[...].astype(F32).reshape(1, target.shape[0])
    if number == 0:
        flat[base : base + levels] = kernel[...]
    elif number == 1:
        far = inputs[4]

        @pl.when(lax.axis_index("levels") == 0)
        def _():
            flat[base : base + levels] = kernel[...]
            flat[base + levels : base + levels + STEPS] = far[0:STEPS]

        @pl.when(lax.axis_index("levels") == 1)
        def _():
            flat[base : base + STEPS] = far[levels - STEPS : levels]
            flat[base + STEPS : base + STEPS + levels] = kernel[...]
    else:
        flat[base : base + STEPS] = inputs[4][levels - STEPS : levels]
        flat[base + STEPS : base + STEPS + levels] = kernel[...]
        flat[base + STEPS + levels : base + 2 * STEPS + levels] = inputs[5][0:STEPS]
    for copy in range(out.shape[0]):
        for group in range(out.shape[1]):
            out[copy, group] = flat[4 * group : 4 * group + 4]


def with_edges(plane, edge, columns):
    tail = columns // LANES * LANES
    lane = lax.broadcasted_iota(jnp.int32, plane.shape[:-1] + (LANES,), 2)
    return jnp.where(lane < columns - tail, plane[..., tail : tail + LANES], edge)


def levels_kernel(moves, columns, own, edge, *outs):
    tail = columns // LANES * LANES
    for out, (_, start, _) in zip(outs, moves()):
        pick = pl.ds(start, STEPS)
        out[..., 0:tail] = own[:, pick, :, 0:tail]
        for p in range(own.shape[0]):
            out[p, :, :, tail : tail + LANES] = with_edges(own[p, pick], edge[p, pick], columns)


def tiles_kernel(moves, columns, own, edge, *refs):
    number = len(moves())
    far, (body, first_out, second_out) = refs[:number], refs[number:]
    planes, levels, rows, _ = own.shape
    tracers = planes - 5
    tail = columns // LANES * LANES
    mixing, east, west, north, south = range(tracers, planes)
    start, _ = window(0, levels)
    pick = pl.ds(start, levels)
    body[:, pick, :, 0:tail] = own[:, :, :, 0:tail]
    for p in range(planes):
        body[p, pick, :, tail : tail + LANES] = with_edges(own[p], edge[p], columns)
    for part, (_, _, slot) in zip(far, moves()):
        body[:, pl.ds(slot, STEPS)] = part[...]

    def rows_of(out, first, single):
        for entry, p in enumerate(list(range(tracers)) + [mixing, north, south]):
            out[entry] = body[p, :, first : first + WIDTH, :]
        out[tracers + 3, :, 0:1, :] = body[east, :, single : single + 1, :]
        out[tracers + 3, :, 1:2, :] = body[west, :, single : single + 1, :]

    @pl.when(is_even())
    def _():
        rows_of(first_out, rows - WIDTH, rows - 1)
        rows_of(second_out, 0, 0)

    @pl.when(jnp.logical_not(is_even()))
    def _():
        rows_of(first_out, 0, 0)
        rows_of(second_out, rows - WIDTH, rows - 1)


def advance(step, src, dst, coef, forcing, index, profile, flux, levels):
    tracers = src.shape[0]
    first, count = window(STEPS - 1 - step, levels)
    own, _ = window(0, levels)
    lanes = src.shape[-1]
    total = [flux[t] for t in range(tracers)]
    for i in range(count):
        at = first + i
        up, down = coef[0, at + 1], coef[0, at]
        east, west, north, south = (coef[c, at + 1] for c in range(1, 5))
        own_id = at - own
        inside = (own_id >= 0) & (own_id < levels)
        weight = jnp.where(inside, profile[jnp.clip(own_id, 0, levels - 1)], 0.0)
        for t in range(tracers):
            a = src[t, at + 1]
            b = a + up * (src[t, at + 2] - a) + down * (src[t, at] - a)
            moved = b + east * (pltpu.roll(b, lanes - 1, 1) - b) + west * (pltpu.roll(b, 1, 1) - b)
            moved = moved + north * (pltpu.roll(b, 7, 0) - b) + south * (pltpu.roll(b, 1, 0) - b)
            new = moved + forcing[index, t, at]
            dst[t, at + 1] = new
            total[t] = total[t] + weight * new
    for t in range(tracers):
        flux[t] = total[t]


def clear_pads(ref):
    levels = ref.shape[1]
    ref[:, 0:1] = jnp.zeros((ref.shape[0], 1) + ref.shape[2:], F32)
    ref[:, levels - 1 : levels] = jnp.zeros((ref.shape[0], 1) + ref.shape[2:], F32)


def run_steps(number, work, other, coef, forcing, profile, flux, levels):
    refs = [work, other]
    for i in range(WIDTH):
        advance(number * WIDTH + i, refs[i % 2], refs[(i + 1) % 2], coef, forcing, i, profile, flux, levels)
    return refs[WIDTH % 2]


def send_rows(number, state, first_out, second_out, rows, levels):
    start, count = window(STEPS - (number + 1) * WIDTH, levels)
    upper = state[:, pl.ds(start + 1, count), rows - WIDTH : rows, :]
    lower = state[:, pl.ds(start + 1, count), 0:WIDTH, :]
    even = is_even()
    first_out[...] = jnp.where(even, upper, lower)
    second_out[...] = jnp.where(even, lower, upper)


def first_kernel(levels, body, first, second, forcing, profile, *refs):
    state_out, coef_out, flux, first_out, second_out, work, other, raw = refs
    planes, wide, rows, lanes = body.shape
    tracers = planes - 5
    mixing, east, west, north, south = range(tracers, planes)
    raw[...] = jnp.zeros_like(raw)
    flux[...] = jnp.zeros_like(flux)
    clear_pads(work)
    clear_pads(other)
    even = is_even()
    pick = slice(1, wide + 1)
    for p in range(planes):
        ref, plane = (work, p) if p < tracers else (raw, p - tracers)
        ref[plane, pick, 0:rows, :] = body[p]
    for entry, p in enumerate(list(range(tracers)) + [mixing, north, south]):
        ref, plane = (work, p) if p < tracers else (raw, p - tracers)
        ref[plane, pick, rows : rows + WIDTH, :] = jnp.where(even, first[entry], second[entry])
        ref[plane, pick, 8 - WIDTH : 8, :] = jnp.where(even, second[entry], first[entry])
    for k, p in enumerate((east, west)):
        one, two = first[tracers + 3, :, k : k + 1, :], second[tracers + 3, :, k : k + 1, :]
        raw[p - tracers, pick, rows : rows + 1, :] = jnp.where(even, one, two)
        raw[p - tracers, pick, 7:8, :] = jnp.where(even, two, one)
    coef_out[0] = raw[0]
    coef_out[1] = raw[1]
    coef_out[3] = raw[3]
    for l in range(raw.shape[1]):
        coef_out[2, l] = pltpu.roll(raw[2, l], 1, 1)
        coef_out[4, l] = pltpu.roll(raw[4, l], 1, 0)
    last = run_steps(0, work, other, coef_out, forcing, profile, flux, levels)
    state_out[...] = last[...]
    send_rows(0, state_out, first_out, second_out, rows, levels)


def next_kernel(number, levels, rows, state, coef, first, second, forcing, profile, flux_in, *refs):
    work, other = refs[-2:]
    start, count = window(STEPS - number * WIDTH, levels)
    pick = pl.ds(start + 1, count)
    even = is_even()
    work[...] = state[...]
    work[:, pick, rows : rows + WIDTH, :] = jnp.where(even, first[...], second[...])
    work[:, pick, 8 - WIDTH : 8, :] = jnp.where(even, second[...], first[...])
    clear_pads(other)
    if number < ROUNDS - 1:
        state_out, flux, first_out, second_out = refs[:-2]
        flux[...] = flux_in[...]
        last = run_steps(number, work, other, coef, forcing, profile, flux, levels)
        state_out[...] = last[...]
        send_rows(number, state_out, first_out, second_out, rows, levels)
        return
    adjoint, keep, give, flux = refs[:-2]
    flux[...] = flux_in[...]
    last = run_steps(number, work, other, coef, forcing, profile, flux, levels)
    own, _ = window(0, levels)
    columns = adjoint.shape[-1]
    adjoint[...] = last[:, pl.ds(own + 1, levels), 0:rows, 0:columns]
    if lax.axis_size("levels") == 2:
        half = rows // 2
        upper = lax.axis_index("levels") == 1
        low, high = flux[:, 0:half, 0:columns], flux[:, half:rows, 0:columns]
        keep[...] = jnp.where(upper, high, low)
        give[...] = jnp.where(upper, low, high)
    else:
        keep[...] = flux[:, 0:rows, 0:columns]
        give[...] = jnp.zeros_like(give)


def forcing_kernel(number, tracers, levels, rows, columns, near, far, out, left, right, terms, flat, parts):
    sources, groups, _, held = near.shape
    lanes = out.shape[-1]
    subs = lax.axis_size("sub")
    tile, sub = lax.axis_index("tiles"), lax.axis_index("sub")
    for s in range(sources * subs):
        ref = near if s < sources else far
        for group in range(groups):
            flat[4 * group : 4 * group + 4, s * held : (s + 1) * held] = ref[s % sources, group]
    owner = flat[tracers : tracers + 1, :]
    target = flat[tracers + 1 : tracers + 2, :]
    cells = rows * columns
    step = jnp.floor((target + 0.5) * (1.0 / cells))
    cell = target - step * cells
    row = jnp.floor((cell + 0.5) * (1.0 / columns))
    col = cell - row * columns
    owner_tile = jnp.floor((owner + 0.5) * (1.0 / subs))
    row = row + (owner_tile - tile.astype(F32)) * rows
    shift = owner - owner_tile * subs - sub.astype(F32)
    col = col + jnp.where(shift < 0, shift + subs, shift) * columns
    east_side = col < columns + STEPS
    west_side = col >= subs * columns - STEPS
    lane = jnp.where(east_side, col, jnp.where(west_side, col - subs * columns + lanes, -1.0))
    close = (row >= 1 - WIDTH) & (row <= rows + WIDTH - 2)
    key = jnp.where(close, step * 8 + jnp.where(row < 0, row + 8, row), -1.0)
    for start in range(0, lanes, LANES):
        ids = lax.broadcasted_iota(jnp.int32, (LANES, lane.shape[1]), 0).astype(F32) + start
        right[start : start + LANES] = jnp.where(ids == lane, 1.0, 0.0).astype(BF16)
    for t in range(tracers):
        value = flat[...] * flat[t : t + 1, :]
        high = value.astype(BF16).astype(F32)
        parts[0, t] = high
        parts[1, t] = value - high
    first, count = window(STEPS - 1 - WIDTH * number, levels)
    batch = flat.shape[1]
    for i in range(count):
        for t in range(tracers):
            row_id = pl.ds(tracers + 2 + first + i, 1)
            both = [jnp.broadcast_to(parts[k, t, row_id, :], (8, batch)) for k in range(2)]
            terms[i * tracers + t] = jnp.concatenate(both, axis=0).astype(BF16)
    ids = lax.broadcasted_iota(jnp.int32, (8, batch), 0).astype(F32)
    for i in range(WIDTH):
        now = number * WIDTH + i
        begin, size = window(STEPS - 1 - now, levels)
        hit = jnp.where(key == ids + now * 8.0, 1.0, 0.0)
        mask = jnp.concatenate([hit, hit], axis=0).astype(BF16)
        offset = (begin - first) * tracers

        def fill(q, carry, mask=mask, offset=offset):
            left[pl.ds(pl.multiple_of(q * 16, 16), 16), :] = terms[offset + q] * mask
            return carry

        lax.fori_loop(0, size * tracers, fill, 0)
        product = lax.dot_general(
            left[0 : size * tracers * 16, :],
            right[...],
            (((1,), (1,)), ((), ())),
            preferred_element_type=F32,
        )
        for l in range(size):
            for t in range(tracers):
                base = (l * tracers + t) * 16
                value = product[base : base + 8] + product[base + 8 : base + 16]
                if pl.num_programs(0) == 1:
                    out[i, t, begin + l] = value
                else:
                    old = jnp.where(pl.program_id(0) == 0, 0.0, out[i, t, begin + l])
                    out[i, t, begin + l] = old + value


def per_device(
    final_adjoint,
    lon_courant,
    lat_courant,
    upwind_flags,
    vertical_mixing,
    level_profile,
    sounding_owner,
    sounding_target,
    misfit,
    averaging_kernel,
):
    tracers, levels, rows, columns = final_adjoint.shape
    held = misfit.shape[1]
    bands, subs, tiles = (lax.axis_size(name) for name in ("levels", "sub", "tiles"))
    planes = tracers + 5
    lanes = -(-(columns + 2 * STEPS) // LANES) * LANES
    wide = window(STEPS, levels)[1]
    moves = functools.partial(level_moves, levels)
    number = len(moves())
    shape = lambda *dims: jax.ShapeDtypeStruct(dims, F32)
    sub_pairs = [(i, (i + 1) % subs) for i in range(subs)]

    def call(body, limit, flops=0, **kwargs):
        return pl.pallas_call(
            body,
            compiler_params=pltpu.CompilerParams(vmem_limit_bytes=limit * MIB),
            cost_estimate=pl.CostEstimate(flops=flops, bytes_accessed=MIB, transcendentals=0),
            **kwargs,
        )

    def room(*arrays):
        return [pltpu.VMEM(x.shape, x.dtype) for x in arrays]

    beside = [lax.ppermute(averaging_kernel, "levels", pairs) for pairs, _, _ in moves()]
    fields = (final_adjoint, lon_courant, lat_courant, upwind_flags, vertical_mixing)
    own, edge = call(
        edges_kernel,
        60,
        out_shape=(shape(planes, levels, rows, lanes), shape(planes, levels, rows, LANES)),
        in_specs=[HBM] * 5,
        out_specs=(VMEM, VMEM),
        scratch_shapes=room(*fields)
        + [pltpu.VMEM((planes, levels, 8, lanes), F32), pltpu.SemaphoreType.DMA((5,))],
        name="edges",
    )(*fields)
    edge = lax.ppermute(edge, "sub", sub_pairs)
    inputs = (misfit, averaging_kernel, sounding_owner.reshape(1, held), sounding_target, *beside)
    groups = -(-(tracers + 2 + wide) // 4)
    payload = call(
        functools.partial(payload_kernel, number),
        16 if held <= 1024 else 32,
        out_shape=shape(tiles, groups, 4, held),
        in_specs=[HBM] * 4 + [VMEM] * number,
        out_specs=VMEM,
        scratch_shapes=room(*inputs[:4])
        + [pltpu.VMEM((-(-groups // 2) * 8, held), F32), pltpu.SemaphoreType.DMA((4,))],
        name="payload",
    )(*inputs)
    near = lax.all_to_all(payload, "tiles", split_axis=0, concat_axis=0, tiled=True)
    far = lax.ppermute(near, "sub", sub_pairs)

    sent = call(
        functools.partial(levels_kernel, moves, columns),
        8,
        out_shape=[shape(planes, STEPS, rows, lanes)] * number,
        in_specs=[VMEM] * 2,
        out_specs=[VMEM] * number,
        name="levels",
    )(own, edge)
    parts = [lax.ppermute(part, "levels", pairs) for part, (pairs, _, _) in zip(sent, moves())]
    message = shape(tracers + 4, wide, WIDTH, lanes)
    body, first, second = call(
        functools.partial(tiles_kernel, moves, columns),
        8,
        out_shape=(shape(planes, wide, rows, lanes), message, message),
        in_specs=[VMEM] * (2 + number),
        out_specs=[VMEM] * 3,
        name="tiles",
    )(own, edge, *parts)
    first, second = swap_tiles(first, 0), swap_tiles(second, 1)

    sources = max(1, min(tiles, CHUNK // (subs * held)))
    batch = sources * subs * held
    force_shape = (WIDTH, tracers, wide, 8, lanes)

    def forcing_of(round_id):
        count = window(STEPS - 1 - WIDTH * round_id, levels)[1]
        depth = -(-groups // 2) * 8
        block = pl.BlockSpec((sources, groups, 4, held), lambda i: (i, 0, 0, 0))
        return call(
            functools.partial(forcing_kernel, round_id, tracers, levels, rows, columns),
            20 if batch <= CHUNK else 60,
            flops=4 * count * tracers * 16 * batch * lanes,
            out_shape=shape(*force_shape),
            grid=(tiles // sources,),
            in_specs=[block, block],
            out_specs=pl.BlockSpec(force_shape, lambda i: (0, 0, 0, 0, 0)),
            scratch_shapes=[
                pltpu.VMEM((count * tracers * 16, batch), BF16),
                pltpu.VMEM((lanes, batch), BF16),
                pltpu.VMEM((count * tracers, 16, batch), BF16),
                pltpu.VMEM((depth, batch), F32),
                pltpu.VMEM((2, tracers, depth, batch), F32),
            ],
            name="forcing" + str(round_id),
        )(near, far)

    forcings = [forcing_of(i) for i in range(ROUNDS)]
    state_shape = (tracers, wide + 2, 8, lanes)
    coef_shape = (5, wide + 2, 8, lanes)
    flux_shape = (tracers, 8, lanes)

    def messages(round_id):
        count = window(STEPS - round_id * WIDTH, levels)[1]
        return [shape(tracers, count, WIDTH, lanes)] * 2

    scratch = [pltpu.VMEM(state_shape, F32)] * 2
    state, coef, flux, first, second = call(
        functools.partial(first_kernel, levels),
        12,
        out_shape=[shape(*state_shape), shape(*coef_shape), shape(*flux_shape), *messages(1)],
        in_specs=[VMEM] * 4 + [SMEM],
        out_specs=[VMEM] * 5,
        scratch_shapes=scratch + [pltpu.VMEM(coef_shape, F32)],
        name="round0",
    )(body, first, second, forcings[0], level_profile)
    half = rows // 2 if bands == 2 else rows
    for round_id in range(1, ROUNDS):
        first, second = swap_tiles(first, 0), swap_tiles(second, 1)
        if round_id < ROUNDS - 1:
            outs = [shape(*state_shape), shape(*flux_shape), *messages(round_id + 1)]
            extra = []
        else:
            part = shape(tracers, half, columns)
            outs = [shape(tracers, levels, rows, columns), part, part]
            extra = [pltpu.VMEM(flux_shape, F32)]
        results = call(
            functools.partial(next_kernel, round_id, levels, rows),
            12,
            out_shape=outs,
            in_specs=[VMEM] * 5 + [SMEM, VMEM],
            out_specs=[VMEM] * len(outs),
            scratch_shapes=extra + scratch,
            name="round" + str(round_id),
        )(state, coef, first, second, forcings[round_id], level_profile, flux)
        if round_id < ROUNDS - 1:
            state, flux, first, second = results
    adjoint, keep, give = results
    if bands == 2:
        flux_gradient = keep + lax.ppermute(give, "levels", [(0, 1), (1, 0)])
    else:
        flux_gradient = lax.psum_scatter(keep, "levels", scatter_dimension=1, tiled=True)
    return adjoint, flux_gradient


def solution(mesh):
    return jax.shard_map(
        per_device,
        mesh=mesh,
        in_specs=(
            P("groups", "levels", "tiles", "sub"),
            P(("groups", "levels"), "tiles", "sub"),
            P(("groups", "levels"), "tiles", "sub"),
            P(None, ("groups", "levels"), "tiles", "sub"),
            P(("groups", "levels"), "tiles", "sub"),
            P("levels"),
            P(("groups", "tiles", "sub"), None),
            P(("groups", "tiles", "sub")),
            P(None, ("groups", "tiles", "sub")),
            P("levels", ("groups", "tiles", "sub")),
        ),
        out_specs=(P("groups", "levels", "tiles", "sub"), P("groups", ("tiles", "levels"), "sub")),
        check_vma=False,
    )
```

```python
import functools

import jax
import jax.numpy as jnp
from jax import lax
from jax.experimental import pallas as pl
from jax.experimental.pallas import tpu as pltpu
from jax.sharding import PartitionSpec as P

STEPS = 6
WIDTH = 2
ROUNDS = STEPS // WIDTH
LANES = 128
CHUNK = 3072
F32 = jnp.float32
BF16 = jnp.bfloat16
VMEM = pl.BlockSpec(memory_space=pltpu.VMEM)
SMEM = pl.BlockSpec(memory_space=pltpu.SMEM)
HBM = pl.BlockSpec(memory_space=pltpu.HBM)
MIB = 1024 * 1024


def window(margin, levels):
    count = lax.axis_size("levels")
    if count == 1:
        return 0, levels
    if count == 2:
        return lax.axis_index("levels") * (STEPS - margin), levels + margin
    return STEPS - margin, levels + 2 * margin


def level_moves(levels):
    count = lax.axis_size("levels")
    band = lax.axis_index("levels")
    if count == 1:
        return []
    if count == 2:
        return [([(0, 1), (1, 0)], (levels - STEPS) * (1 - band), levels * (1 - band))]
    up = [(i, i + 1) for i in range(count - 1)]
    down = [(i + 1, i) for i in range(count - 1)]
    return [(up, levels - STEPS, 0), (down, 0, STEPS + levels)]


def swap_tiles(value, odd):
    tiles = lax.axis_size("tiles")
    pairs = []
    for low in range(odd, tiles - 1, 2):
        pairs += [(low, low + 1), (low + 1, low)]
    return lax.ppermute(value, "tiles", pairs)


def is_even():
    return lax.rem(lax.axis_index("tiles"), 2) == 0


def own_planes(adj, lon, lat, flags, mix):
    tracers, levels, rows, _ = adj.shape
    last_band = lax.axis_index("levels") == lax.axis_size("levels") - 1
    last_tile = lax.axis_index("tiles") == lax.axis_size("tiles") - 1
    shape = lon.shape
    level_ids = lax.broadcasted_iota(jnp.int32, shape, 0)
    row_ids = lax.broadcasted_iota(jnp.int32, shape, 1)
    top = (level_ids == levels - 1) & last_band
    shut = (row_ids == rows - 1) & last_tile
    first = flags[0].astype(F32)
    second = flags[1].astype(F32)
    lat_open = jnp.where(shut, 0.0, lat[...])
    planes = [adj[t] for t in range(tracers)]
    planes.append(jnp.where(top, 0.0, mix[...]))
    planes.append(lon[...] * first)
    planes.append(lon[...] * (1.0 - first))
    planes.append(lat_open * second)
    planes.append(lat_open * (1.0 - second))
    return planes


def fetch(sources, targets, sems):
    copies = [pltpu.make_async_copy(x, y, sems.at[i]) for i, (x, y) in enumerate(zip(sources, targets))]
    for copy in copies:
        copy.start()
    for copy in copies:
        copy.wait()


def soundings_of(number, flat, misfit, kernel, owner, target):
    tracers, levels = misfit.shape[0], kernel.shape[0]
    base = tracers + 2
    flat[...] = jnp.zeros_like(flat)
    flat[0:tracers] = misfit[...]
    flat[tracers : tracers + 1] = owner[...].astype(F32)
    flat[tracers + 1 : base] = target[...].astype(F32).reshape(1, target.shape[0])
    if number == 1:

        @pl.when(lax.axis_index("levels") == 0)
        def _():
            flat[base : base + levels] = kernel[...]

        @pl.when(lax.axis_index("levels") == 1)
        def _():
            flat[base + STEPS : base + STEPS + levels] = kernel[...]
    else:
        start = base + (STEPS if number else 0)
        flat[start : start + levels] = kernel[...]


def edges_kernel(moves, *refs):
    inputs, own_out, edge_out, base = refs[:9], refs[9], refs[10], refs[11]
    outs, held, buf, sems = refs[12:-11], refs[-11:-2], refs[-2], refs[-1]
    fetch(inputs, held, sems)
    soundings_of(len(moves()), base, *held[5:])
    held = held[:5]
    _, levels, rows, columns = held[0].shape
    width = edge_out.shape[-1]
    tail = columns // LANES * LANES
    gap = columns - tail
    buf[...] = jnp.zeros_like(buf)
    for p, plane in enumerate(own_planes(*held)):
        buf[p, :, 0:rows, 0:columns] = plane
    own_out[...] = buf[:, :, 0:rows, :]
    lane = lax.broadcasted_iota(jnp.int32, (8, LANES), 1)
    for p in range(buf.shape[0]):
        for l in range(levels):
            start = pltpu.roll(buf[p, l, :, 0:LANES], gap, 1)
            end = pltpu.roll(buf[p, l, :, tail : tail + LANES], width - gap, 1)
            both = jnp.where(
                lane >= width - STEPS,
                end,
                jnp.where((lane >= gap) & (lane < gap + STEPS), start, 0.0),
            )
            edge_out[p, l] = both[0:rows]
    for i, (_, start, _) in enumerate(moves()):
        outs[2 * i][...] = own_out[:, pl.ds(start, STEPS)]
        outs[2 * i + 1][...] = edge_out[:, pl.ds(start, STEPS)]


def payload_kernel(number, levels, tracers, *refs):
    out, flat = refs[-2:]
    base = tracers + 2
    for half in range(2):
        part = refs[half * (1 + number) : (half + 1) * (1 + number)]
        flat[...] = part[0][...]
        if number == 1:

            @pl.when(lax.axis_index("levels") == 0)
            def _(part=part):
                flat[base + levels : base + levels + STEPS] = part[1][0:STEPS]

            @pl.when(lax.axis_index("levels") == 1)
            def _(part=part):
                flat[base : base + STEPS] = part[1][levels - STEPS : levels]

        if number == 2:
            flat[base : base + STEPS] = part[1][levels - STEPS : levels]
            flat[base + STEPS + levels : base + 2 * STEPS + levels] = part[2][0:STEPS]
        for group in range(out.shape[1]):
            out[half, group] = flat[4 * group : 4 * group + 4]


def with_edges(plane, edge, columns):
    tail = columns // LANES * LANES
    lane = lax.broadcasted_iota(jnp.int32, plane.shape[:-1] + (LANES,), 2)
    return jnp.where(lane < columns - tail, plane[..., tail : tail + LANES], edge)


def tiles_kernel(moves, columns, own, edge, *refs):
    number = len(moves())
    far, (body, first_out, second_out) = refs[: 2 * number], refs[2 * number :]
    planes, levels, rows, _ = own.shape
    tracers = planes - 5
    tail = columns // LANES * LANES
    mixing, east, west, north, south = range(tracers, planes)
    start, _ = window(0, levels)
    pick = pl.ds(start, levels)
    body[:, pick, :, 0:tail] = own[:, :, :, 0:tail]
    for p in range(planes):
        body[p, pick, :, tail : tail + LANES] = with_edges(own[p], edge[p], columns)
    for i, (_, _, slot) in enumerate(moves()):
        part, beside = far[2 * i], far[2 * i + 1]
        there = pl.ds(slot, STEPS)
        body[:, there, :, 0:tail] = part[:, :, :, 0:tail]
        for p in range(planes):
            body[p, there, :, tail : tail + LANES] = with_edges(part[p], beside[p], columns)

    def rows_of(out, first, single):
        for entry, p in enumerate(list(range(tracers)) + [mixing, north, south]):
            out[entry] = body[p, :, first : first + WIDTH, :]
        out[tracers + 3, :, 0:1, :] = body[east, :, single : single + 1, :]
        out[tracers + 3, :, 1:2, :] = body[west, :, single : single + 1, :]

    @pl.when(is_even())
    def _():
        rows_of(first_out, rows - WIDTH, rows - 1)
        rows_of(second_out, 0, 0)

    @pl.when(jnp.logical_not(is_even()))
    def _():
        rows_of(first_out, 0, 0)
        rows_of(second_out, rows - WIDTH, rows - 1)


def advance(step, src, dst, coef, forcing, index, profile, flux, levels):
    tracers = src.shape[0]
    first, count = window(STEPS - 1 - step, levels)
    own, _ = window(0, levels)
    lanes = src.shape[-1]
    total = [flux[t] for t in range(tracers)]
    for i in range(count):
        at = first + i
        up, down = coef[0, at + 1], coef[0, at]
        east, west, north, south = (coef[c, at + 1] for c in range(1, 5))
        own_id = at - own
        inside = (own_id >= 0) & (own_id < levels)
        weight = jnp.where(inside, profile[jnp.clip(own_id, 0, levels - 1)], 0.0)
        for t in range(tracers):
            a = src[t, at + 1]
            b = a + up * (src[t, at + 2] - a) + down * (src[t, at] - a)
            moved = b + east * (pltpu.roll(b, lanes - 1, 1) - b) + west * (pltpu.roll(b, 1, 1) - b)
            moved = moved + north * (pltpu.roll(b, 7, 0) - b) + south * (pltpu.roll(b, 1, 0) - b)
            new = moved + forcing[index, t, at]
            dst[t, at + 1] = new
            total[t] = total[t] + weight * new
    for t in range(tracers):
        flux[t] = total[t]


def clear_pads(ref):
    levels = ref.shape[1]
    ref[:, 0:1] = jnp.zeros((ref.shape[0], 1) + ref.shape[2:], F32)
    ref[:, levels - 1 : levels] = jnp.zeros((ref.shape[0], 1) + ref.shape[2:], F32)


def run_steps(number, work, other, coef, forcing, profile, flux, levels):
    refs = [work, other]
    for i in range(WIDTH):
        advance(number * WIDTH + i, refs[i % 2], refs[(i + 1) % 2], coef, forcing, i, profile, flux, levels)
    return refs[WIDTH % 2]


def send_rows(number, state, first_out, second_out, rows, levels):
    start, count = window(STEPS - (number + 1) * WIDTH, levels)
    upper = state[:, pl.ds(start + 1, count), rows - WIDTH : rows, :]
    lower = state[:, pl.ds(start + 1, count), 0:WIDTH, :]
    even = is_even()
    first_out[...] = jnp.where(even, upper, lower)
    second_out[...] = jnp.where(even, lower, upper)


def first_kernel(levels, body, first, second, forcing, profile, *refs):
    state_out, coef_out, flux, first_out, second_out, work, other, raw = refs
    planes, wide, rows, lanes = body.shape
    tracers = planes - 5
    mixing, east, west, north, south = range(tracers, planes)
    raw[...] = jnp.zeros_like(raw)
    flux[...] = jnp.zeros_like(flux)
    clear_pads(work)
    clear_pads(other)
    even = is_even()
    pick = slice(1, wide + 1)
    for p in range(planes):
        ref, plane = (work, p) if p < tracers else (raw, p - tracers)
        ref[plane, pick, 0:rows, :] = body[p]
    for entry, p in enumerate(list(range(tracers)) + [mixing, north, south]):
        ref, plane = (work, p) if p < tracers else (raw, p - tracers)
        ref[plane, pick, rows : rows + WIDTH, :] = jnp.where(even, first[entry], second[entry])
        ref[plane, pick, 8 - WIDTH : 8, :] = jnp.where(even, second[entry], first[entry])
    for k, p in enumerate((east, west)):
        one, two = first[tracers + 3, :, k : k + 1, :], second[tracers + 3, :, k : k + 1, :]
        raw[p - tracers, pick, rows : rows + 1, :] = jnp.where(even, one, two)
        raw[p - tracers, pick, 7:8, :] = jnp.where(even, two, one)
    coef_out[0] = raw[0]
    coef_out[1] = raw[1]
    coef_out[3] = raw[3]
    for l in range(raw.shape[1]):
        coef_out[2, l] = pltpu.roll(raw[2, l], 1, 1)
        coef_out[4, l] = pltpu.roll(raw[4, l], 1, 0)
    last = run_steps(0, work, other, coef_out, forcing, profile, flux, levels)
    state_out[...] = last[...]
    send_rows(0, state_out, first_out, second_out, rows, levels)


def next_kernel(number, levels, rows, state, coef, first, second, forcing, profile, flux_in, *refs):
    work, other = refs[-2:]
    start, count = window(STEPS - number * WIDTH, levels)
    pick = pl.ds(start + 1, count)
    even = is_even()
    work[...] = state[...]
    work[:, pick, rows : rows + WIDTH, :] = jnp.where(even, first[...], second[...])
    work[:, pick, 8 - WIDTH : 8, :] = jnp.where(even, second[...], first[...])
    clear_pads(other)
    if number < ROUNDS - 1:
        state_out, flux, first_out, second_out = refs[:-2]
        flux[...] = flux_in[...]
        last = run_steps(number, work, other, coef, forcing, profile, flux, levels)
        state_out[...] = last[...]
        send_rows(number, state_out, first_out, second_out, rows, levels)
        return
    adjoint, keep, give, flux = refs[:-2]
    flux[...] = flux_in[...]
    last = run_steps(number, work, other, coef, forcing, profile, flux, levels)
    own, _ = window(0, levels)
    columns = adjoint.shape[-1]
    adjoint[...] = last[:, pl.ds(own + 1, levels), 0:rows, 0:columns]
    if lax.axis_size("levels") == 2:
        half = rows // 2
        upper = lax.axis_index("levels") == 1
        low, high = flux[:, 0:half, 0:columns], flux[:, half:rows, 0:columns]
        keep[...] = jnp.where(upper, high, low)
        give[...] = jnp.where(upper, low, high)
    else:
        keep[...] = flux[:, 0:rows, 0:columns]
        give[...] = jnp.zeros_like(give)


def forcing_kernel(number, tracers, levels, rows, columns, *refs):
    got, (out, left, right, terms, flat, parts) = refs[:-6], refs[-6:]
    sources, groups, _, held = got[0].shape
    lanes = out.shape[-1]
    subs = lax.axis_size("sub")
    tile, sub = lax.axis_index("tiles"), lax.axis_index("sub")
    for s in range(sources * len(got)):
        ref = got[s // sources]
        for group in range(groups):
            flat[4 * group : 4 * group + 4, s * held : (s + 1) * held] = ref[s % sources, group]
    owner = flat[tracers : tracers + 1, :]
    target = flat[tracers + 1 : tracers + 2, :]
    cells = rows * columns
    step = jnp.floor((target + 0.5) * (1.0 / cells))
    cell = target - step * cells
    row = jnp.floor((cell + 0.5) * (1.0 / columns))
    col = cell - row * columns
    owner_tile = jnp.floor((owner + 0.5) * (1.0 / subs))
    row = row + (owner_tile - tile.astype(F32)) * rows
    shift = owner - owner_tile * subs - sub.astype(F32)
    col = col + jnp.where(shift < 0, shift + subs, shift) * columns
    east_side = col < columns + STEPS
    west_side = col >= subs * columns - STEPS
    lane = jnp.where(east_side, col, jnp.where(west_side, col - subs * columns + lanes, -1.0))
    close = (row >= 1 - WIDTH) & (row <= rows + WIDTH - 2)
    key = jnp.where(close, step * 8 + jnp.where(row < 0, row + 8, row), -1.0)
    for start in range(0, lanes, LANES):
        ids = lax.broadcasted_iota(jnp.int32, (LANES, lane.shape[1]), 0).astype(F32) + start
        right[start : start + LANES] = jnp.where(ids == lane, 1.0, 0.0).astype(BF16)
    for t in range(tracers):
        value = flat[...] * flat[t : t + 1, :]
        high = value.astype(BF16).astype(F32)
        parts[0, t] = high
        parts[1, t] = value - high
    first, count = window(STEPS - 1 - WIDTH * number, levels)
    batch = flat.shape[1]
    for i in range(count):
        for t in range(tracers):
            row_id = pl.ds(tracers + 2 + first + i, 1)
            both = [jnp.broadcast_to(parts[k, t, row_id, :], (8, batch)) for k in range(2)]
            terms[i * tracers + t] = jnp.concatenate(both, axis=0).astype(BF16)
    ids = lax.broadcasted_iota(jnp.int32, (8, batch), 0).astype(F32)
    for i in range(WIDTH):
        now = number * WIDTH + i
        begin, size = window(STEPS - 1 - now, levels)
        hit = jnp.where(key == ids + now * 8.0, 1.0, 0.0)
        mask = jnp.concatenate([hit, hit], axis=0).astype(BF16)
        offset = (begin - first) * tracers

        def fill(q, carry, mask=mask, offset=offset):
            left[pl.ds(pl.multiple_of(q * 16, 16), 16), :] = terms[offset + q] * mask
            return carry

        lax.fori_loop(0, size * tracers, fill, 0)
        product = lax.dot_general(
            left[0 : size * tracers * 16, :],
            right[...],
            (((1,), (1,)), ((), ())),
            preferred_element_type=F32,
        )
        for l in range(size):
            for t in range(tracers):
                base = (l * tracers + t) * 16
                value = product[base : base + 8] + product[base + 8 : base + 16]
                if pl.num_programs(0) == 1:
                    out[i, t, begin + l] = value
                else:
                    old = jnp.where(pl.program_id(0) == 0, 0.0, out[i, t, begin + l])
                    out[i, t, begin + l] = old + value


def per_device(
    final_adjoint,
    lon_courant,
    lat_courant,
    upwind_flags,
    vertical_mixing,
    level_profile,
    sounding_owner,
    sounding_target,
    misfit,
    averaging_kernel,
):
    tracers, levels, rows, columns = final_adjoint.shape
    held = misfit.shape[1]
    bands, subs, tiles = (lax.axis_size(name) for name in ("levels", "sub", "tiles"))
    planes = tracers + 5
    lanes = -(-(columns + 2 * STEPS) // LANES) * LANES
    wide = window(STEPS, levels)[1]
    moves = functools.partial(level_moves, levels)
    number = len(moves())
    shape = lambda *dims: jax.ShapeDtypeStruct(dims, F32)
    sub_pairs = [(i, (i + 1) % subs) for i in range(subs)]

    def call(body, limit, flops=0, **kwargs):
        return pl.pallas_call(
            body,
            compiler_params=pltpu.CompilerParams(vmem_limit_bytes=limit * MIB),
            cost_estimate=pl.CostEstimate(flops=flops, bytes_accessed=MIB, transcendentals=0),
            **kwargs,
        )

    def room(*arrays):
        return [pltpu.VMEM(x.shape, x.dtype) for x in arrays]

    across = [(pairs, [(a * subs + c, b * subs + d) for a, b in pairs for c, d in sub_pairs]) for pairs, _, _ in moves()]
    beside = [lax.ppermute(averaging_kernel, "levels", pairs) for pairs, _ in across]
    crossed = [lax.ppermute(averaging_kernel, ("levels", "sub"), pairs) for _, pairs in across]
    fields = (final_adjoint, lon_courant, lat_courant, upwind_flags, vertical_mixing)
    fields += (misfit, averaging_kernel, sounding_owner.reshape(1, held), sounding_target)
    level_part, edge_part = shape(planes, STEPS, rows, lanes), shape(planes, STEPS, rows, LANES)
    groups = -(-(tracers + 2 + wide) // 4)
    flat_rows = -(-groups // 2) * 8
    own, edge, payload, *parts = call(
        functools.partial(edges_kernel, moves),
        60,
        out_shape=[shape(planes, levels, rows, lanes), shape(planes, levels, rows, LANES)]
        + [shape(flat_rows, held)]
        + [level_part, edge_part] * number,
        in_specs=[HBM] * 9,
        out_specs=[VMEM] * (3 + 2 * number),
        scratch_shapes=room(*fields)
        + [pltpu.VMEM((planes, levels, 8, lanes), F32), pltpu.SemaphoreType.DMA((9,))],
        name="edges",
    )(*fields)
    edge = lax.ppermute(edge, "sub", sub_pairs)
    for i, (pairs, cross) in enumerate(across):
        parts[2 * i] = lax.ppermute(parts[2 * i], "levels", pairs)
        parts[2 * i + 1] = lax.ppermute(parts[2 * i + 1], ("levels", "sub"), cross)
    both = call(
        functools.partial(payload_kernel, number, levels, tracers),
        8,
        out_shape=shape(2, groups, 4, held),
        in_specs=[VMEM] * (2 + 2 * number),
        out_specs=VMEM,
        scratch_shapes=[pltpu.VMEM((flat_rows, held), F32)],
        name="payload",
    )(payload, *beside, lax.ppermute(payload, "sub", sub_pairs), *crossed)
    if tiles == 4:
        got = [both] + [lax.ppermute(both, "tiles", [(i, i ^ k) for i in range(tiles)]) for k in (1, 2, 3)]
    else:
        got = [lax.all_gather(both, "tiles", tiled=True)]

    message = shape(tracers + 4, wide, WIDTH, lanes)
    body, first, second = call(
        functools.partial(tiles_kernel, moves, columns),
        8,
        out_shape=(shape(planes, wide, rows, lanes), message, message),
        in_specs=[VMEM] * (2 + 2 * number),
        out_specs=[VMEM] * 3,
        name="tiles",
    )(own, edge, *parts)
    first, second = swap_tiles(first, 0), swap_tiles(second, 1)

    held_here = got[0].shape[0]
    sources = held_here if len(got) > 1 else max(1, min(held_here, CHUNK // held))
    batch = sources * len(got) * held
    force_shape = (WIDTH, tracers, wide, 8, lanes)

    def forcing_of(round_id):
        count = window(STEPS - 1 - WIDTH * round_id, levels)[1]
        depth = -(-groups // 2) * 8
        block = pl.BlockSpec((sources, groups, 4, held), lambda i: (i, 0, 0, 0))
        return call(
            functools.partial(forcing_kernel, round_id, tracers, levels, rows, columns),
            20 if batch <= CHUNK else 60,
            flops=4 * count * tracers * 16 * batch * lanes,
            out_shape=shape(*force_shape),
            grid=(held_here // sources,),
            in_specs=[block] * len(got),
            out_specs=pl.BlockSpec(force_shape, lambda i: (0, 0, 0, 0, 0)),
            scratch_shapes=[
                pltpu.VMEM((count * tracers * 16, batch), BF16),
                pltpu.VMEM((lanes, batch), BF16),
                pltpu.VMEM((count * tracers, 16, batch), BF16),
                pltpu.VMEM((depth, batch), F32),
                pltpu.VMEM((2, tracers, depth, batch), F32),
            ],
            name="forcing" + str(round_id),
        )(*got)

    forcings = [forcing_of(i) for i in range(ROUNDS)]
    state_shape = (tracers, wide + 2, 8, lanes)
    coef_shape = (5, wide + 2, 8, lanes)
    flux_shape = (tracers, 8, lanes)

    def messages(round_id):
        count = window(STEPS - round_id * WIDTH, levels)[1]
        return [shape(tracers, count, WIDTH, lanes)] * 2

    scratch = [pltpu.VMEM(state_shape, F32)] * 2
    state, coef, flux, first, second = call(
        functools.partial(first_kernel, levels),
        12,
        out_shape=[shape(*state_shape), shape(*coef_shape), shape(*flux_shape), *messages(1)],
        in_specs=[VMEM] * 4 + [SMEM],
        out_specs=[VMEM] * 5,
        scratch_shapes=scratch + [pltpu.VMEM(coef_shape, F32)],
        name="round0",
    )(body, first, second, forcings[0], level_profile)
    half = rows // 2 if bands == 2 else rows
    for round_id in range(1, ROUNDS):
        first, second = swap_tiles(first, 0), swap_tiles(second, 1)
        if round_id < ROUNDS - 1:
            outs = [shape(*state_shape), shape(*flux_shape), *messages(round_id + 1)]
            extra = []
        else:
            part = shape(tracers, half, columns)
            outs = [shape(tracers, levels, rows, columns), part, part]
            extra = [pltpu.VMEM(flux_shape, F32)]
        results = call(
            functools.partial(next_kernel, round_id, levels, rows),
            12,
            out_shape=outs,
            in_specs=[VMEM] * 5 + [SMEM, VMEM],
            out_specs=[VMEM] * len(outs),
            scratch_shapes=extra + scratch,
            name="round" + str(round_id),
        )(state, coef, first, second, forcings[round_id], level_profile, flux)
        if round_id < ROUNDS - 1:
            state, flux, first, second = results
    adjoint, keep, give = results
    if bands == 2:
        flux_gradient = keep + lax.ppermute(give, "levels", [(0, 1), (1, 0)])
    else:
        flux_gradient = lax.psum_scatter(keep, "levels", scatter_dimension=1, tiled=True)
    return adjoint, flux_gradient


def solution(mesh):
    return jax.shard_map(
        per_device,
        mesh=mesh,
        in_specs=(
            P("groups", "levels", "tiles", "sub"),
            P(("groups", "levels"), "tiles", "sub"),
            P(("groups", "levels"), "tiles", "sub"),
            P(None, ("groups", "levels"), "tiles", "sub"),
            P(("groups", "levels"), "tiles", "sub"),
            P("levels"),
            P(("groups", "tiles", "sub"), None),
            P(("groups", "tiles", "sub")),
            P(None, ("groups", "tiles", "sub")),
            P("levels", ("groups", "tiles", "sub")),
        ),
        out_specs=(P("groups", "levels", "tiles", "sub"), P("groups", ("tiles", "levels"), "sub")),
        check_vma=False,
    )
```

```python
import functools

import jax
import jax.numpy as jnp
from jax import lax
from jax.experimental import pallas as pl
from jax.experimental.pallas import tpu as pltpu
from jax.sharding import PartitionSpec as P

STEPS = 6
WIDTH = 3
FORCED = ((0, 1, 2, 3), (4, 5))
ROUNDS = STEPS // WIDTH
LANES = 128
CHUNK = 3072
F32 = jnp.float32
BF16 = jnp.bfloat16
VMEM = pl.BlockSpec(memory_space=pltpu.VMEM)
SMEM = pl.BlockSpec(memory_space=pltpu.SMEM)
HBM = pl.BlockSpec(memory_space=pltpu.HBM)
MIB = 1024 * 1024


def window(margin, levels):
    count = lax.axis_size("levels")
    if count == 1:
        return 0, levels
    if count == 2:
        return lax.axis_index("levels") * (STEPS - margin), levels + margin
    return STEPS - margin, levels + 2 * margin


def level_moves(levels):
    count = lax.axis_size("levels")
    band = lax.axis_index("levels")
    if count == 1:
        return []
    if count == 2:
        return [([(0, 1), (1, 0)], (levels - STEPS) * (1 - band), levels * (1 - band))]
    up = [(i, i + 1) for i in range(count - 1)]
    down = [(i + 1, i) for i in range(count - 1)]
    return [(up, levels - STEPS, 0), (down, 0, STEPS + levels)]


def swap_tiles(value, odd):
    tiles = lax.axis_size("tiles")
    pairs = []
    for low in range(odd, tiles - 1, 2):
        pairs += [(low, low + 1), (low + 1, low)]
    return lax.ppermute(value, "tiles", pairs)


def is_even():
    return lax.rem(lax.axis_index("tiles"), 2) == 0


def own_planes(adj, lon, lat, flags, mix):
    tracers, levels, rows, _ = adj.shape
    last_band = lax.axis_index("levels") == lax.axis_size("levels") - 1
    last_tile = lax.axis_index("tiles") == lax.axis_size("tiles") - 1
    shape = lon.shape
    level_ids = lax.broadcasted_iota(jnp.int32, shape, 0)
    row_ids = lax.broadcasted_iota(jnp.int32, shape, 1)
    top = (level_ids == levels - 1) & last_band
    shut = (row_ids == rows - 1) & last_tile
    first = flags[0].astype(F32)
    second = flags[1].astype(F32)
    lat_open = jnp.where(shut, 0.0, lat[...])
    planes = [adj[t] for t in range(tracers)]
    planes.append(jnp.where(top, 0.0, mix[...]))
    planes.append(lon[...] * first)
    planes.append(lon[...] * (1.0 - first))
    planes.append(lat_open * second)
    planes.append(lat_open * (1.0 - second))
    return planes


def fetch(sources, targets, sems):
    copies = [pltpu.make_async_copy(x, y, sems.at[i]) for i, (x, y) in enumerate(zip(sources, targets))]
    for copy in copies:
        copy.start()
    for copy in copies:
        copy.wait()


def soundings_of(number, flat, misfit, kernel, owner, target):
    tracers, levels = misfit.shape[0], kernel.shape[0]
    base = tracers + 2
    flat[...] = jnp.zeros_like(flat)
    flat[0:tracers] = misfit[...]
    flat[tracers : tracers + 1] = owner[...].astype(F32)
    flat[tracers + 1 : base] = target[...].astype(F32).reshape(1, target.shape[0])
    if number == 1:

        @pl.when(lax.axis_index("levels") == 0)
        def _():
            flat[base : base + levels] = kernel[...]

        @pl.when(lax.axis_index("levels") == 1)
        def _():
            flat[base + STEPS : base + STEPS + levels] = kernel[...]
    else:
        start = base + (STEPS if number else 0)
        flat[start : start + levels] = kernel[...]


def edges_kernel(moves, *refs):
    inputs, own_out, edge_out, base = refs[:9], refs[9], refs[10], refs[11]
    outs, held, buf, sems = refs[12:-11], refs[-11:-2], refs[-2], refs[-1]
    fetch(inputs, held, sems)
    soundings_of(len(moves()), base, *held[5:])
    held = held[:5]
    _, levels, rows, columns = held[0].shape
    width = edge_out.shape[-1]
    tail = columns // LANES * LANES
    gap = columns - tail
    buf[...] = jnp.zeros_like(buf)
    for p, plane in enumerate(own_planes(*held)):
        buf[p, :, 0:rows, 0:columns] = plane
    own_out[...] = buf[:, :, 0:rows, :]
    lane = lax.broadcasted_iota(jnp.int32, (8, LANES), 1)
    for p in range(buf.shape[0]):
        for l in range(levels):
            start = pltpu.roll(buf[p, l, :, 0:LANES], gap, 1)
            end = pltpu.roll(buf[p, l, :, tail : tail + LANES], width - gap, 1)
            both = jnp.where(
                lane >= width - STEPS,
                end,
                jnp.where((lane >= gap) & (lane < gap + STEPS), start, 0.0),
            )
            edge_out[p, l] = both[0:rows]
    for i, (_, start, _) in enumerate(moves()):
        outs[2 * i][...] = own_out[:, pl.ds(start, STEPS)]
        outs[2 * i + 1][...] = edge_out[:, pl.ds(start, STEPS)]


def payload_kernel(number, levels, tracers, *refs):
    out, flat = refs[-2:]
    base = tracers + 2
    for half in range(2):
        part = refs[half * (1 + number) : (half + 1) * (1 + number)]
        flat[...] = part[0][...]
        if number == 1:

            @pl.when(lax.axis_index("levels") == 0)
            def _(part=part):
                flat[base + levels : base + levels + STEPS] = part[1][0:STEPS]

            @pl.when(lax.axis_index("levels") == 1)
            def _(part=part):
                flat[base : base + STEPS] = part[1][levels - STEPS : levels]

        if number == 2:
            flat[base : base + STEPS] = part[1][levels - STEPS : levels]
            flat[base + STEPS + levels : base + 2 * STEPS + levels] = part[2][0:STEPS]
        for group in range(out.shape[1]):
            out[half, group] = flat[4 * group : 4 * group + 4]


def with_edges(plane, edge, columns):
    tail = columns // LANES * LANES
    lane = lax.broadcasted_iota(jnp.int32, plane.shape[:-1] + (LANES,), 2)
    return jnp.where(lane < columns - tail, plane[..., tail : tail + LANES], edge)


def tiles_kernel(moves, columns, own, edge, *refs):
    number = len(moves())
    far, (body, first_out, second_out) = refs[: 2 * number], refs[2 * number :]
    planes, levels, rows, _ = own.shape
    tracers = planes - 5
    tail = columns // LANES * LANES
    mixing, east, west, north, south = range(tracers, planes)
    start, _ = window(0, levels)
    pick = pl.ds(start, levels)
    body[:, pick, :, 0:tail] = own[:, :, :, 0:tail]
    for p in range(planes):
        body[p, pick, :, tail : tail + LANES] = with_edges(own[p], edge[p], columns)
    for i, (_, _, slot) in enumerate(moves()):
        part, beside = far[2 * i], far[2 * i + 1]
        there = pl.ds(slot, STEPS)
        body[:, there, :, 0:tail] = part[:, :, :, 0:tail]
        for p in range(planes):
            body[p, there, :, tail : tail + LANES] = with_edges(part[p], beside[p], columns)

    def rows_of(out, first, third):
        near = list(range(tracers)) + [mixing, north, south, east, west]
        for entry, p in enumerate(near):
            out[entry] = body[p, :, first : first + 2, :]
        for k, p in enumerate(list(range(tracers)) + [mixing, south, south]):
            half = slice(k % 2, k % 2 + 1)
            out[len(near) + k // 2, :, half, :] = body[p, :, third : third + 1, :]

    @pl.when(is_even())
    def _():
        rows_of(first_out, rows - 2, rows - 3)
        rows_of(second_out, 0, 2)

    @pl.when(jnp.logical_not(is_even()))
    def _():
        rows_of(first_out, 0, 2)
        rows_of(second_out, rows - 2, rows - 3)


def advance(step, src, dst, outer, coef, forcing, profile, flux, levels):
    tracers = src.shape[0]
    first, count = window(STEPS - 1 - step, levels)
    own, _ = window(0, levels)
    lanes = src.shape[-1]
    ids = lax.broadcasted_iota(jnp.int32, src.shape[-2:], 0)
    force, index = forcing(step)
    total = [flux[t] for t in range(tracers)]
    for i in range(count):
        at = first + i
        up, down = coef[0, at + 1], coef[0, at]
        east, west, north, south = (coef[c, at + 1] for c in range(1, 5))
        if outer is not None:
            up_outer, down_outer = coef[5, at + 1], coef[5, at]
        own_id = at - own
        inside = (own_id >= 0) & (own_id < levels)
        weight = jnp.where(inside, profile[jnp.clip(own_id, 0, levels - 1)], 0.0)
        for t in range(tracers):
            a = src[t, at + 1]
            b = a + up * (src[t, at + 2] - a) + down * (src[t, at] - a)
            moved = b + east * (pltpu.roll(b, lanes - 1, 1) - b) + west * (pltpu.roll(b, 1, 1) - b)
            above, below = pltpu.roll(b, 7, 0), pltpu.roll(b, 1, 0)
            if outer is not None:
                a = outer[t, at + 1]
                b_outer = a + up_outer * (outer[t, at + 2] - a) + down_outer * (outer[t, at] - a)
                above = jnp.where(ids == 5, b_outer, above)
                below = jnp.where(ids == 6, b_outer, below)
            moved = moved + north * (above - b) + south * (below - b)
            new = moved + force[index, t, at]
            dst[t, at + 1] = new
            total[t] = total[t] + weight * new
    for t in range(tracers):
        flux[t] = total[t]


def clear_pads(ref):
    levels = ref.shape[1]
    ref[:, 0:1] = jnp.zeros((ref.shape[0], 1) + ref.shape[2:], F32)
    ref[:, levels - 1 : levels] = jnp.zeros((ref.shape[0], 1) + ref.shape[2:], F32)


def forced_in(number):
    return [i for i, steps in enumerate(FORCED) if any(step // WIDTH == number for step in steps)]


def run_steps(number, work, other, outer, coef, forcings, profile, flux, levels):
    def forcing(step):
        for i, ref in zip(forced_in(number), forcings):
            if step in FORCED[i]:
                return ref, FORCED[i].index(step)

    refs = [work, other]
    for i in range(WIDTH):
        extra = outer if i == 0 else None
        advance(number * WIDTH + i, refs[i % 2], refs[(i + 1) % 2], extra, coef, forcing, profile, flux, levels)
    return refs[WIDTH % 2]


def send_rows(number, state, first_out, second_out, rows, levels):
    start, count = window(STEPS - (number + 1) * WIDTH, levels)
    pick = pl.ds(start + 1, count)
    tracers = state.shape[0]
    even = is_even()
    for t in range(tracers):
        upper, lower = state[t, pick, rows - 2 : rows, :], state[t, pick, 0:2, :]
        first_out[t] = jnp.where(even, upper, lower)
        second_out[t] = jnp.where(even, lower, upper)
        upper, lower = state[t, pick, rows - 3 : rows - 2, :], state[t, pick, 2:3, :]
        entry, half = tracers + t // 2, slice(t % 2, t % 2 + 1)
        first_out[entry, :, half, :] = jnp.where(even, upper, lower)
        second_out[entry, :, half, :] = jnp.where(even, lower, upper)


def place_outer(ref, plane, pick, first, second, entry, half):
    even = is_even()
    one, two = first[entry, :, half : half + 1, :], second[entry, :, half : half + 1, :]
    ref[plane, pick, 5:6, :] = jnp.where(even, one, two)
    ref[plane, pick, 6:7, :] = jnp.where(even, two, one)


def first_kernel(levels, body, first, second, *refs):
    count = len(forced_in(0))
    forcings, profile = refs[:count], refs[count]
    state_out, coef_out, flux, first_out, second_out, work, other, outer, raw = refs[count + 1 :]
    planes, wide, rows, lanes = body.shape
    tracers = planes - 5
    mixing, east, west, north, south = range(tracers, planes)
    raw[...] = jnp.zeros_like(raw)
    flux[...] = jnp.zeros_like(flux)
    clear_pads(work)
    clear_pads(other)
    clear_pads(outer)
    even = is_even()
    pick = slice(1, wide + 1)
    for p in range(planes):
        ref, plane = (work, p) if p < tracers else (raw, p - tracers)
        ref[plane, pick, 0:rows, :] = body[p]
    near = list(range(tracers)) + [mixing, north, south, east, west]
    for entry, p in enumerate(near):
        ref, plane = (work, p) if p < tracers else (raw, p - tracers)
        ref[plane, pick, rows : rows + 2, :] = jnp.where(even, first[entry], second[entry])
        ref[plane, pick, 6:8, :] = jnp.where(even, second[entry], first[entry])
    for k in range(tracers):
        place_outer(outer, k, pick, first, second, len(near) + k // 2, k % 2)
    for plane, k in ((5, tracers), (6, tracers + 1)):
        place_outer(raw, plane, pick, first, second, len(near) + k // 2, k % 2)
    coef_out[0] = raw[0]
    coef_out[1] = raw[1]
    coef_out[3] = raw[3]
    coef_out[5] = raw[5]
    ids = lax.broadcasted_iota(jnp.int32, (8, lanes), 0)
    for l in range(raw.shape[1]):
        coef_out[2, l] = pltpu.roll(raw[2, l], 1, 1)
        coef_out[4, l] = jnp.where(ids == 6, raw[6, l], pltpu.roll(raw[4, l], 1, 0))
    last = run_steps(0, work, other, outer, coef_out, forcings, profile, flux, levels)
    state_out[...] = last[...]
    send_rows(0, state_out, first_out, second_out, rows, levels)


def next_kernel(number, levels, rows, state, coef, first, second, *refs):
    count = len(forced_in(number))
    forcings, profile, flux_in = refs[:count], refs[count], refs[count + 1]
    refs = refs[count + 2 :]
    work, other, outer = refs[-3:]
    start, size = window(STEPS - number * WIDTH, levels)
    pick = pl.ds(start + 1, size)
    even = is_even()
    tracers = state.shape[0]
    work[...] = state[...]
    for t in range(tracers):
        work[t, pick, rows : rows + 2, :] = jnp.where(even, first[t], second[t])
        work[t, pick, 6:8, :] = jnp.where(even, second[t], first[t])
    clear_pads(other)
    clear_pads(outer)
    for t in range(tracers):
        place_outer(outer, t, pick, first, second, tracers + t // 2, t % 2)
    if number < ROUNDS - 1:
        state_out, flux, first_out, second_out = refs[:-3]
        flux[...] = flux_in[...]
        last = run_steps(number, work, other, outer, coef, forcings, profile, flux, levels)
        state_out[...] = last[...]
        send_rows(number, state_out, first_out, second_out, rows, levels)
        return
    adjoint, keep, give, flux = refs[:-3]
    flux[...] = flux_in[...]
    last = run_steps(number, work, other, outer, coef, forcings, profile, flux, levels)
    own, _ = window(0, levels)
    columns = adjoint.shape[-1]
    adjoint[...] = last[:, pl.ds(own + 1, levels), 0:rows, 0:columns]
    if lax.axis_size("levels") == 2:
        half = rows // 2
        upper = lax.axis_index("levels") == 1
        low, high = flux[:, 0:half, 0:columns], flux[:, half:rows, 0:columns]
        keep[...] = jnp.where(upper, high, low)
        give[...] = jnp.where(upper, low, high)
    else:
        keep[...] = flux[:, 0:rows, 0:columns]
        give[...] = jnp.zeros_like(give)


def forcing_kernel(steps, tracers, levels, rows, columns, *refs):
    got, (out, left, right, terms, flat, parts) = refs[:-6], refs[-6:]
    sources, groups, _, held = got[0].shape
    lanes = out.shape[-1]
    subs = lax.axis_size("sub")
    tile, sub = lax.axis_index("tiles"), lax.axis_index("sub")
    for s in range(sources * len(got)):
        ref = got[s // sources]
        for group in range(groups):
            flat[4 * group : 4 * group + 4, s * held : (s + 1) * held] = ref[s % sources, group]
    owner = flat[tracers : tracers + 1, :]
    target = flat[tracers + 1 : tracers + 2, :]
    cells = rows * columns
    step = jnp.floor((target + 0.5) * (1.0 / cells))
    cell = target - step * cells
    row = jnp.floor((cell + 0.5) * (1.0 / columns))
    col = cell - row * columns
    owner_tile = jnp.floor((owner + 0.5) * (1.0 / subs))
    row = row + (owner_tile - tile.astype(F32)) * rows
    shift = owner - owner_tile * subs - sub.astype(F32)
    col = col + jnp.where(shift < 0, shift + subs, shift) * columns
    east_side = col < columns + STEPS
    west_side = col >= subs * columns - STEPS
    lane = jnp.where(east_side, col, jnp.where(west_side, col - subs * columns + lanes, -1.0))
    close = (row >= 1 - WIDTH) & (row <= rows + WIDTH - 2)
    key = jnp.where(close, step * 8 + jnp.where(row < 0, row + 8, row), -1.0)
    for start in range(0, lanes, LANES):
        ids = lax.broadcasted_iota(jnp.int32, (LANES, lane.shape[1]), 0).astype(F32) + start
        right[start : start + LANES] = jnp.where(ids == lane, 1.0, 0.0).astype(BF16)
    for t in range(tracers):
        value = flat[...] * flat[t : t + 1, :]
        high = value.astype(BF16).astype(F32)
        parts[0, t] = high
        parts[1, t] = value - high
    first, count = window(STEPS - 1 - steps[0], levels)
    batch = flat.shape[1]
    for i in range(count):
        for t in range(tracers):
            row_id = pl.ds(tracers + 2 + first + i, 1)
            both = [jnp.broadcast_to(parts[k, t, row_id, :], (8, batch)) for k in range(2)]
            terms[i * tracers + t] = jnp.concatenate(both, axis=0).astype(BF16)
    ids = lax.broadcasted_iota(jnp.int32, (8, batch), 0).astype(F32)
    for i, now in enumerate(steps):
        begin, size = window(STEPS - 1 - now, levels)
        hit = jnp.where(key == ids + now * 8.0, 1.0, 0.0)
        mask = jnp.concatenate([hit, hit], axis=0).astype(BF16)
        offset = (begin - first) * tracers

        def fill(q, carry, mask=mask, offset=offset):
            left[pl.ds(pl.multiple_of(q * 16, 16), 16), :] = terms[offset + q] * mask
            return carry

        lax.fori_loop(0, size * tracers, fill, 0)
        product = lax.dot_general(
            left[0 : size * tracers * 16, :],
            right[...],
            (((1,), (1,)), ((), ())),
            preferred_element_type=F32,
        )
        for l in range(size):
            for t in range(tracers):
                base = (l * tracers + t) * 16
                value = product[base : base + 8] + product[base + 8 : base + 16]
                if pl.num_programs(0) == 1:
                    out[i, t, begin + l] = value
                else:
                    old = jnp.where(pl.program_id(0) == 0, 0.0, out[i, t, begin + l])
                    out[i, t, begin + l] = old + value


def per_device(
    final_adjoint,
    lon_courant,
    lat_courant,
    upwind_flags,
    vertical_mixing,
    level_profile,
    sounding_owner,
    sounding_target,
    misfit,
    averaging_kernel,
):
    tracers, levels, rows, columns = final_adjoint.shape
    held = misfit.shape[1]
    bands, subs, tiles = (lax.axis_size(name) for name in ("levels", "sub", "tiles"))
    planes = tracers + 5
    lanes = -(-(columns + 2 * STEPS) // LANES) * LANES
    wide = window(STEPS, levels)[1]
    moves = functools.partial(level_moves, levels)
    number = len(moves())
    shape = lambda *dims: jax.ShapeDtypeStruct(dims, F32)
    sub_pairs = [(i, (i + 1) % subs) for i in range(subs)]

    def call(body, limit, flops=0, **kwargs):
        return pl.pallas_call(
            body,
            compiler_params=pltpu.CompilerParams(vmem_limit_bytes=limit * MIB),
            cost_estimate=pl.CostEstimate(flops=flops, bytes_accessed=MIB, transcendentals=0),
            **kwargs,
        )

    def room(*arrays):
        return [pltpu.VMEM(x.shape, x.dtype) for x in arrays]

    across = [(pairs, [(a * subs + c, b * subs + d) for a, b in pairs for c, d in sub_pairs]) for pairs, _, _ in moves()]
    beside = [lax.ppermute(averaging_kernel, "levels", pairs) for pairs, _ in across]
    crossed = [lax.ppermute(averaging_kernel, ("levels", "sub"), pairs) for _, pairs in across]
    fields = (final_adjoint, lon_courant, lat_courant, upwind_flags, vertical_mixing)
    fields += (misfit, averaging_kernel, sounding_owner.reshape(1, held), sounding_target)
    level_part, edge_part = shape(planes, STEPS, rows, lanes), shape(planes, STEPS, rows, LANES)
    groups = -(-(tracers + 2 + wide) // 4)
    flat_rows = -(-groups // 2) * 8
    own, edge, payload, *parts = call(
        functools.partial(edges_kernel, moves),
        60,
        out_shape=[shape(planes, levels, rows, lanes), shape(planes, levels, rows, LANES)]
        + [shape(flat_rows, held)]
        + [level_part, edge_part] * number,
        in_specs=[HBM] * 9,
        out_specs=[VMEM] * (3 + 2 * number),
        scratch_shapes=room(*fields)
        + [pltpu.VMEM((planes, levels, 8, lanes), F32), pltpu.SemaphoreType.DMA((9,))],
        name="edges",
    )(*fields)
    edge = lax.ppermute(edge, "sub", sub_pairs)
    swapped = lax.ppermute(payload, "sub", sub_pairs)
    parts, beside, crossed, swapped = lax.optimization_barrier((parts, beside, crossed, swapped))
    for i, (pairs, cross) in enumerate(across):
        parts[2 * i] = lax.ppermute(parts[2 * i], "levels", pairs)
        parts[2 * i + 1] = lax.ppermute(parts[2 * i + 1], ("levels", "sub"), cross)
    both = call(
        functools.partial(payload_kernel, number, levels, tracers),
        8,
        out_shape=shape(2, groups, 4, held),
        in_specs=[VMEM] * (2 + 2 * number),
        out_specs=VMEM,
        scratch_shapes=[pltpu.VMEM((flat_rows, held), F32)],
        name="payload",
    )(payload, *beside, swapped, *crossed)
    if tiles == 4:
        got = [both] + [lax.ppermute(both, "tiles", [(i, i ^ k) for i in range(tiles)]) for k in (1, 2, 3)]
    else:
        got = [lax.all_gather(both, "tiles", tiled=True)]

    message = shape(tracers + 5 + (tracers + 3) // 2, wide, 2, lanes)
    body, first, second = call(
        functools.partial(tiles_kernel, moves, columns),
        8,
        out_shape=(shape(planes, wide, rows, lanes), message, message),
        in_specs=[VMEM] * (2 + 2 * number),
        out_specs=[VMEM] * 3,
        name="tiles",
    )(own, edge, *parts)
    first, second = swap_tiles(first, 0), swap_tiles(second, 1)

    held_here = got[0].shape[0]
    sources = held_here if len(got) > 1 else max(1, min(held_here, CHUNK // held))
    batch = sources * len(got) * held
    def forcing_of(steps):
        count = window(STEPS - 1 - steps[0], levels)[1]
        force_shape = (len(steps), tracers, wide, 8, lanes)
        block = pl.BlockSpec((sources, groups, 4, held), lambda i: (i, 0, 0, 0))
        return call(
            functools.partial(forcing_kernel, steps, tracers, levels, rows, columns),
            20 if batch <= CHUNK else 60,
            flops=2 * len(steps) * count * tracers * 16 * batch * lanes,
            out_shape=shape(*force_shape),
            grid=(held_here // sources,),
            in_specs=[block] * len(got),
            out_specs=pl.BlockSpec(force_shape, lambda i: (0, 0, 0, 0, 0)),
            scratch_shapes=[
                pltpu.VMEM((count * tracers * 16, batch), BF16),
                pltpu.VMEM((lanes, batch), BF16),
                pltpu.VMEM((count * tracers, 16, batch), BF16),
                pltpu.VMEM((flat_rows, batch), F32),
                pltpu.VMEM((2, tracers, flat_rows, batch), F32),
            ],
            name="forcing" + str(steps[0]),
        )(*got)

    forcings = [forcing_of(steps) for steps in FORCED]
    state_shape = (tracers, wide + 2, 8, lanes)
    coef_shape = (6, wide + 2, 8, lanes)
    flux_shape = (tracers, 8, lanes)

    def messages(round_id):
        count = window(STEPS - round_id * WIDTH, levels)[1]
        return [shape(tracers + (tracers + 1) // 2, count, 2, lanes)] * 2

    scratch = [pltpu.VMEM(state_shape, F32)] * 3
    state, coef, flux, first, second = call(
        functools.partial(first_kernel, levels),
        16,
        out_shape=[shape(*state_shape), shape(*coef_shape), shape(*flux_shape), *messages(1)],
        in_specs=[VMEM] * (3 + len(forced_in(0))) + [SMEM],
        out_specs=[VMEM] * 5,
        scratch_shapes=scratch + [pltpu.VMEM((7, wide + 2, 8, lanes), F32)],
        name="round0",
    )(body, first, second, *[forcings[i] for i in forced_in(0)], level_profile)
    half = rows // 2 if bands == 2 else rows
    for round_id in range(1, ROUNDS):
        first, second = swap_tiles(first, 0), swap_tiles(second, 1)
        if round_id < ROUNDS - 1:
            outs = [shape(*state_shape), shape(*flux_shape), *messages(round_id + 1)]
            extra = []
        else:
            part = shape(tracers, half, columns)
            outs = [shape(tracers, levels, rows, columns), part, part]
            extra = [pltpu.VMEM(flux_shape, F32)]
        results = call(
            functools.partial(next_kernel, round_id, levels, rows),
            16,
            out_shape=outs,
            in_specs=[VMEM] * (4 + len(forced_in(round_id))) + [SMEM, VMEM],
            out_specs=[VMEM] * len(outs),
            scratch_shapes=extra + scratch,
            name="round" + str(round_id),
        )(state, coef, first, second, *[forcings[i] for i in forced_in(round_id)], level_profile, flux)
        if round_id < ROUNDS - 1:
            state, flux, first, second = results
    adjoint, keep, give = results
    if bands == 2:
        flux_gradient = keep + lax.ppermute(give, "levels", [(0, 1), (1, 0)])
    else:
        flux_gradient = lax.psum_scatter(keep, "levels", scatter_dimension=1, tiled=True)
    return adjoint, flux_gradient


def solution(mesh):
    return jax.shard_map(
        per_device,
        mesh=mesh,
        in_specs=(
            P("groups", "levels", "tiles", "sub"),
            P(("groups", "levels"), "tiles", "sub"),
            P(("groups", "levels"), "tiles", "sub"),
            P(None, ("groups", "levels"), "tiles", "sub"),
            P(("groups", "levels"), "tiles", "sub"),
            P("levels"),
            P(("groups", "tiles", "sub"), None),
            P(("groups", "tiles", "sub")),
            P(None, ("groups", "tiles", "sub")),
            P("levels", ("groups", "tiles", "sub")),
        ),
        out_specs=(P("groups", "levels", "tiles", "sub"), P("groups", ("tiles", "levels"), "sub")),
        check_vma=False,
    )
```

```python
import functools

import jax
import jax.numpy as jnp
from jax import lax
from jax.experimental import pallas as pl
from jax.experimental.pallas import tpu as pltpu
from jax.sharding import PartitionSpec as P

STEPS = 6
WIDTH = 3
FORCED = ((0, 1, 2), (3, 4, 5))
ROUNDS = STEPS // WIDTH
LANES = 128
CHUNK = 3072
F32 = jnp.float32
BF16 = jnp.bfloat16
VMEM = pl.BlockSpec(memory_space=pltpu.VMEM)
SMEM = pl.BlockSpec(memory_space=pltpu.SMEM)
HBM = pl.BlockSpec(memory_space=pltpu.HBM)
MIB = 1024 * 1024


def window(margin, levels):
    count = lax.axis_size("levels")
    if count == 1:
        return 0, levels
    if count == 2:
        return lax.axis_index("levels") * (STEPS - margin), levels + margin
    return STEPS - margin, levels + 2 * margin


def level_moves(levels):
    count = lax.axis_size("levels")
    band = lax.axis_index("levels")
    if count == 1:
        return []
    if count == 2:
        return [([(0, 1), (1, 0)], (levels - STEPS) * (1 - band), levels * (1 - band))]
    up = [(i, i + 1) for i in range(count - 1)]
    down = [(i + 1, i) for i in range(count - 1)]
    return [(up, levels - STEPS, 0), (down, 0, STEPS + levels)]


def swap_tiles(value, odd):
    tiles = lax.axis_size("tiles")
    pairs = []
    for low in range(odd, tiles - 1, 2):
        pairs += [(low, low + 1), (low + 1, low)]
    return lax.ppermute(value, "tiles", pairs)


def is_even():
    return lax.rem(lax.axis_index("tiles"), 2) == 0


def own_planes(adj, lon, lat, flags, mix):
    tracers, levels, rows, _ = adj.shape
    last_band = lax.axis_index("levels") == lax.axis_size("levels") - 1
    last_tile = lax.axis_index("tiles") == lax.axis_size("tiles") - 1
    shape = lon.shape
    level_ids = lax.broadcasted_iota(jnp.int32, shape, 0)
    row_ids = lax.broadcasted_iota(jnp.int32, shape, 1)
    top = (level_ids == levels - 1) & last_band
    shut = (row_ids == rows - 1) & last_tile
    first = flags[0].astype(F32)
    second = flags[1].astype(F32)
    lat_open = jnp.where(shut, 0.0, lat[...])
    planes = [adj[t] for t in range(tracers)]
    planes.append(jnp.where(top, 0.0, mix[...]))
    planes.append(lon[...] * first)
    planes.append(lon[...] * (1.0 - first))
    planes.append(lat_open * second)
    planes.append(lat_open * (1.0 - second))
    return planes


def fetch(sources, targets, sems):
    copies = [pltpu.make_async_copy(x, y, sems.at[i]) for i, (x, y) in enumerate(zip(sources, targets))]
    for copy in copies:
        copy.start()
    for copy in copies:
        copy.wait()


def soundings_of(number, flat, misfit, kernel, owner, target):
    tracers, levels = misfit.shape[0], kernel.shape[0]
    base = tracers + 2
    flat[...] = jnp.zeros_like(flat)
    flat[0:tracers] = misfit[...]
    flat[tracers : tracers + 1] = owner[...].astype(F32)
    flat[tracers + 1 : base] = target[...].astype(F32).reshape(1, target.shape[0])
    if number == 1:

        @pl.when(lax.axis_index("levels") == 0)
        def _():
            flat[base : base + levels] = kernel[...]

        @pl.when(lax.axis_index("levels") == 1)
        def _():
            flat[base + STEPS : base + STEPS + levels] = kernel[...]
    else:
        start = base + (STEPS if number else 0)
        flat[start : start + levels] = kernel[...]


def edges_kernel(moves, *refs):
    inputs, own_out, edge_out, base = refs[:9], refs[9], refs[10], refs[11]
    held, buf, sems = refs[-11:-2], refs[-2], refs[-1]
    fetch(inputs, held, sems)
    soundings_of(len(moves()), base, *held[5:])
    held = held[:5]
    _, levels, rows, columns = held[0].shape
    width = edge_out.shape[-1]
    tail = columns // LANES * LANES
    gap = columns - tail
    buf[...] = jnp.zeros_like(buf)
    for p, plane in enumerate(own_planes(*held)):
        buf[p, :, 0:rows, 0:columns] = plane
    own_out[...] = buf[:, :, 0:rows, :]
    lane = lax.broadcasted_iota(jnp.int32, (8, LANES), 1)
    for p in range(buf.shape[0]):
        for l in range(levels):
            start = pltpu.roll(buf[p, l, :, 0:LANES], gap, 1)
            end = pltpu.roll(buf[p, l, :, tail : tail + LANES], width - gap, 1)
            both = jnp.where(
                lane >= width - STEPS,
                end,
                jnp.where((lane >= gap) & (lane < gap + STEPS), start, 0.0),
            )
            edge_out[p, l] = both[0:rows]

def payload_kernel(number, levels, tracers, *refs):
    out, flat = refs[-2:]
    base = tracers + 2
    for half in range(2):
        part = refs[half * (1 + number) : (half + 1) * (1 + number)]
        flat[...] = part[0][...]
        if number == 1:

            @pl.when(lax.axis_index("levels") == 0)
            def _(part=part):
                flat[base + levels : base + levels + STEPS] = part[1][0:STEPS]

            @pl.when(lax.axis_index("levels") == 1)
            def _(part=part):
                flat[base : base + STEPS] = part[1][levels - STEPS : levels]

        if number == 2:
            flat[base : base + STEPS] = part[1][levels - STEPS : levels]
            flat[base + STEPS + levels : base + 2 * STEPS + levels] = part[2][0:STEPS]
        for group in range(out.shape[1]):
            out[half, group] = flat[4 * group : 4 * group + 4]


def with_edges(plane, edge, columns):
    tail = columns // LANES * LANES
    lane = lax.broadcasted_iota(jnp.int32, plane.shape[:-1] + (LANES,), 2)
    return jnp.where(lane < columns - tail, plane[..., tail : tail + LANES], edge)


def tile_messages(body, first_out, second_out):
    planes, _, rows, _ = body.shape
    tracers = planes - 5
    mixing, east, west, north, south = range(tracers, planes)

    def rows_of(out, first, third):
        near = list(range(tracers)) + [mixing, north, south, east, west]
        for entry, p in enumerate(near):
            out[entry] = body[p, :, first : first + 2, :]
        for k, p in enumerate(list(range(tracers)) + [mixing, south, south]):
            half = slice(k % 2, k % 2 + 1)
            out[len(near) + k // 2, :, half, :] = body[p, :, third : third + 1, :]

    @pl.when(is_even())
    def _():
        rows_of(first_out, rows - 2, rows - 3)
        rows_of(second_out, 0, 2)

    @pl.when(jnp.logical_not(is_even()))
    def _():
        rows_of(first_out, 0, 2)
        rows_of(second_out, rows - 2, rows - 3)


def spread_kernel(moves, columns, own, edge, body, first_out, second_out, *outs):
    tail = columns // LANES * LANES
    body[:, :, :, 0:tail] = own[:, :, :, 0:tail]
    for p in range(own.shape[0]):
        body[p, :, :, tail : tail + LANES] = with_edges(own[p], edge[p], columns)
    for out, (_, start, _) in zip(outs, moves()):
        out[...] = body[:, pl.ds(start, STEPS)]
    tile_messages(body, first_out, second_out)


def far_kernel(number, *refs):
    for i in range(number):
        tile_messages(refs[i], refs[number + 2 * i], refs[number + 2 * i + 1])


def advance(step, src, dst, outer, coef, forcing, profile, flux, levels):
    tracers = src.shape[0]
    first, count = window(STEPS - 1 - step, levels)
    own, _ = window(0, levels)
    lanes = src.shape[-1]
    ids = lax.broadcasted_iota(jnp.int32, src.shape[-2:], 0)
    force, index = forcing(step)
    total = [flux[t] for t in range(tracers)]
    for i in range(count):
        at = first + i
        up, down = coef[0, at + 1], coef[0, at]
        east, west, north, south = (coef[c, at + 1] for c in range(1, 5))
        if outer is not None:
            up_outer, down_outer = coef[5, at + 1], coef[5, at]
        own_id = at - own
        inside = (own_id >= 0) & (own_id < levels)
        weight = jnp.where(inside, profile[jnp.clip(own_id, 0, levels - 1)], 0.0)
        for t in range(tracers):
            a = src[t, at + 1]
            b = a + up * (src[t, at + 2] - a) + down * (src[t, at] - a)
            moved = b + east * (pltpu.roll(b, lanes - 1, 1) - b) + west * (pltpu.roll(b, 1, 1) - b)
            above, below = pltpu.roll(b, 7, 0), pltpu.roll(b, 1, 0)
            if outer is not None:
                a = outer[t, at + 1]
                b_outer = a + up_outer * (outer[t, at + 2] - a) + down_outer * (outer[t, at] - a)
                above = jnp.where(ids == 5, b_outer, above)
                below = jnp.where(ids == 6, b_outer, below)
            moved = moved + north * (above - b) + south * (below - b)
            new = moved + force[index, t, at]
            dst[t, at + 1] = new
            total[t] = total[t] + weight * new
    for t in range(tracers):
        flux[t] = total[t]


def clear_pads(ref):
    levels = ref.shape[1]
    ref[:, 0:1] = jnp.zeros((ref.shape[0], 1) + ref.shape[2:], F32)
    ref[:, levels - 1 : levels] = jnp.zeros((ref.shape[0], 1) + ref.shape[2:], F32)


def forced_in(number):
    return [i for i, steps in enumerate(FORCED) if any(step // WIDTH == number for step in steps)]


def run_steps(number, work, other, outer, coef, forcings, profile, flux, levels):
    def forcing(step):
        for i, ref in zip(forced_in(number), forcings):
            if step in FORCED[i]:
                return ref, FORCED[i].index(step)

    refs = [work, other]
    for i in range(WIDTH):
        extra = outer if i == 0 else None
        advance(number * WIDTH + i, refs[i % 2], refs[(i + 1) % 2], extra, coef, forcing, profile, flux, levels)
    return refs[WIDTH % 2]


def send_rows(number, state, first_out, second_out, rows, levels):
    start, count = window(STEPS - (number + 1) * WIDTH, levels)
    pick = pl.ds(start + 1, count)
    tracers = state.shape[0]
    even = is_even()
    for t in range(tracers):
        upper, lower = state[t, pick, rows - 2 : rows, :], state[t, pick, 0:2, :]
        first_out[t] = jnp.where(even, upper, lower)
        second_out[t] = jnp.where(even, lower, upper)
        upper, lower = state[t, pick, rows - 3 : rows - 2, :], state[t, pick, 2:3, :]
        entry, half = tracers + t // 2, slice(t % 2, t % 2 + 1)
        first_out[entry, :, half, :] = jnp.where(even, upper, lower)
        second_out[entry, :, half, :] = jnp.where(even, lower, upper)


def place_outer(ref, plane, pick, first, second, entry, half):
    even = is_even()
    one, two = first[entry, :, half : half + 1, :], second[entry, :, half : half + 1, :]
    ref[plane, pick, 5:6, :] = jnp.where(even, one, two)
    ref[plane, pick, 6:7, :] = jnp.where(even, two, one)


def first_kernel(moves, levels, *refs):
    number = len(moves())
    groups = [refs[3 * i : 3 * i + 3] for i in range(1 + number)]
    refs = refs[3 * (1 + number) :]
    count = len(forced_in(0))
    forcings, profile = refs[:count], refs[count]
    state_out, coef_out, flux, first_out, second_out, work, other, outer, raw = refs[count + 1 :]
    planes, _, rows, lanes = groups[0][0].shape
    tracers = planes - 5
    mixing, east, west, north, south = range(tracers, planes)
    raw[...] = jnp.zeros_like(raw)
    flux[...] = jnp.zeros_like(flux)
    clear_pads(work)
    clear_pads(other)
    clear_pads(outer)
    even = is_even()
    starts = [window(0, levels)[0]] + [slot for _, _, slot in moves()]
    for (body, first, second), start in zip(groups, starts):
        pick = pl.ds(start + 1, body.shape[1])
        for p in range(planes):
            ref, plane = (work, p) if p < tracers else (raw, p - tracers)
            ref[plane, pick, 0:rows, :] = body[p]
        near = list(range(tracers)) + [mixing, north, south, east, west]
        for entry, p in enumerate(near):
            ref, plane = (work, p) if p < tracers else (raw, p - tracers)
            ref[plane, pick, rows : rows + 2, :] = jnp.where(even, first[entry], second[entry])
            ref[plane, pick, 6:8, :] = jnp.where(even, second[entry], first[entry])
        for k in range(tracers):
            place_outer(outer, k, pick, first, second, len(near) + k // 2, k % 2)
        for plane, k in ((5, tracers), (6, tracers + 1)):
            place_outer(raw, plane, pick, first, second, len(near) + k // 2, k % 2)
    coef_out[0] = raw[0]
    coef_out[1] = raw[1]
    coef_out[3] = raw[3]
    coef_out[5] = raw[5]
    ids = lax.broadcasted_iota(jnp.int32, (8, lanes), 0)
    for l in range(raw.shape[1]):
        coef_out[2, l] = pltpu.roll(raw[2, l], 1, 1)
        coef_out[4, l] = jnp.where(ids == 6, raw[6, l], pltpu.roll(raw[4, l], 1, 0))
    last = run_steps(0, work, other, outer, coef_out, forcings, profile, flux, levels)
    state_out[...] = last[...]
    send_rows(0, state_out, first_out, second_out, rows, levels)


def next_kernel(number, levels, rows, state, coef, first, second, *refs):
    count = len(forced_in(number))
    forcings, profile, flux_in = refs[:count], refs[count], refs[count + 1]
    refs = refs[count + 2 :]
    work, other, outer = refs[-3:]
    start, size = window(STEPS - number * WIDTH, levels)
    pick = pl.ds(start + 1, size)
    even = is_even()
    tracers = state.shape[0]
    work[...] = state[...]
    for t in range(tracers):
        work[t, pick, rows : rows + 2, :] = jnp.where(even, first[t], second[t])
        work[t, pick, 6:8, :] = jnp.where(even, second[t], first[t])
    clear_pads(other)
    clear_pads(outer)
    for t in range(tracers):
        place_outer(outer, t, pick, first, second, tracers + t // 2, t % 2)
    if number < ROUNDS - 1:
        state_out, flux, first_out, second_out = refs[:-3]
        flux[...] = flux_in[...]
        last = run_steps(number, work, other, outer, coef, forcings, profile, flux, levels)
        state_out[...] = last[...]
        send_rows(number, state_out, first_out, second_out, rows, levels)
        return
    adjoint, keep, give, flux = refs[:-3]
    flux[...] = flux_in[...]
    last = run_steps(number, work, other, outer, coef, forcings, profile, flux, levels)
    own, _ = window(0, levels)
    columns = adjoint.shape[-1]
    adjoint[...] = last[:, pl.ds(own + 1, levels), 0:rows, 0:columns]
    if lax.axis_size("levels") == 2:
        half = rows // 2
        upper = lax.axis_index("levels") == 1
        low, high = flux[:, 0:half, 0:columns], flux[:, half:rows, 0:columns]
        keep[...] = jnp.where(upper, high, low)
        give[...] = jnp.where(upper, low, high)
    else:
        keep[...] = flux[:, 0:rows, 0:columns]
        give[...] = jnp.zeros_like(give)


def prepare(tracers, levels, rows, columns, got, terms, right, keys, flat, parts):
    sources, groups, _, held = got[0].shape
    lanes = right.shape[0]
    subs = lax.axis_size("sub")
    tile, sub = lax.axis_index("tiles"), lax.axis_index("sub")
    for s in range(sources * len(got)):
        ref = got[s // sources]
        for group in range(groups):
            flat[4 * group : 4 * group + 4, s * held : (s + 1) * held] = ref[s % sources, group]
    owner = flat[tracers : tracers + 1, :]
    target = flat[tracers + 1 : tracers + 2, :]
    cells = rows * columns
    step = jnp.floor((target + 0.5) * (1.0 / cells))
    cell = target - step * cells
    row = jnp.floor((cell + 0.5) * (1.0 / columns))
    col = cell - row * columns
    owner_tile = jnp.floor((owner + 0.5) * (1.0 / subs))
    row = row + (owner_tile - tile.astype(F32)) * rows
    shift = owner - owner_tile * subs - sub.astype(F32)
    col = col + jnp.where(shift < 0, shift + subs, shift) * columns
    east_side = col < columns + STEPS
    west_side = col >= subs * columns - STEPS
    lane = jnp.where(east_side, col, jnp.where(west_side, col - subs * columns + lanes, -1.0))
    close = (row >= 1 - WIDTH) & (row <= rows + WIDTH - 2)
    key = jnp.where(close, step * 8 + jnp.where(row < 0, row + 8, row), -1.0)
    for start in range(0, lanes, LANES):
        ids = lax.broadcasted_iota(jnp.int32, (LANES, lane.shape[1]), 0).astype(F32) + start
        right[start : start + LANES] = jnp.where(ids == lane, 1.0, 0.0).astype(BF16)
    for t in range(tracers):
        value = flat[...] * flat[t : t + 1, :]
        high = value.astype(BF16).astype(F32)
        parts[0, t] = high
        parts[1, t] = value - high
    first, count = window(STEPS - 1, levels)
    batch = flat.shape[1]
    for i in range(count):
        for t in range(tracers):
            row_id = pl.ds(tracers + 2 + first + i, 1)
            both = [jnp.broadcast_to(parts[k, t, row_id, :], (8, batch)) for k in range(2)]
            terms[i * tracers + t] = jnp.concatenate(both, axis=0).astype(BF16)
    keys[...] = jnp.broadcast_to(key, keys.shape)


def prepare_kernel(tracers, levels, rows, columns, *refs):
    prepare(tracers, levels, rows, columns, refs[:-5], *refs[-5:])


def forcing_kernel(steps, tracers, levels, rows, columns, *refs):
    if len(refs) > 5:
        out, left, terms, right, keys = refs[-7:-2]
        prepare(tracers, levels, rows, columns, refs[:-7], terms, right, keys, *refs[-2:])
    else:
        terms, right, keys, out, left = refs
    first, _ = window(STEPS - 1, levels)
    batch = keys.shape[1]
    ids = lax.broadcasted_iota(jnp.int32, (8, batch), 0).astype(F32)
    for i, now in enumerate(steps):
        begin, size = window(STEPS - 1 - now, levels)
        hit = jnp.where(keys[...] == ids + now * 8.0, 1.0, 0.0)
        mask = jnp.concatenate([hit, hit], axis=0).astype(BF16)
        offset = (begin - first) * tracers

        def fill(q, carry, mask=mask, offset=offset):
            left[pl.ds(pl.multiple_of(q * 16, 16), 16), :] = terms[offset + q] * mask
            return carry

        lax.fori_loop(0, size * tracers, fill, 0)
        product = lax.dot_general(
            left[0 : size * tracers * 16, :],
            right[...],
            (((1,), (1,)), ((), ())),
            preferred_element_type=F32,
        )
        for l in range(size):
            for t in range(tracers):
                base = (l * tracers + t) * 16
                value = product[base : base + 8] + product[base + 8 : base + 16]
                if pl.num_programs(0) == 1:
                    out[i, t, begin + l] = value
                else:
                    old = jnp.where(pl.program_id(0) == 0, 0.0, out[i, t, begin + l])
                    out[i, t, begin + l] = old + value


def per_device(
    final_adjoint,
    lon_courant,
    lat_courant,
    upwind_flags,
    vertical_mixing,
    level_profile,
    sounding_owner,
    sounding_target,
    misfit,
    averaging_kernel,
):
    tracers, levels, rows, columns = final_adjoint.shape
    held = misfit.shape[1]
    bands, subs, tiles = (lax.axis_size(name) for name in ("levels", "sub", "tiles"))
    planes = tracers + 5
    lanes = -(-(columns + 2 * STEPS) // LANES) * LANES
    wide = window(STEPS, levels)[1]
    moves = functools.partial(level_moves, levels)
    number = len(moves())
    shape = lambda *dims: jax.ShapeDtypeStruct(dims, F32)
    sub_pairs = [(i, (i + 1) % subs) for i in range(subs)]

    def call(body, limit, flops=0, **kwargs):
        return pl.pallas_call(
            body,
            compiler_params=pltpu.CompilerParams(vmem_limit_bytes=limit * MIB),
            cost_estimate=pl.CostEstimate(flops=flops, bytes_accessed=MIB, transcendentals=0),
            **kwargs,
        )

    def room(*arrays):
        return [pltpu.VMEM(x.shape, x.dtype) for x in arrays]

    across = [(pairs, [(a * subs + c, b * subs + d) for a, b in pairs for c, d in sub_pairs]) for pairs, _, _ in moves()]
    beside = [lax.ppermute(averaging_kernel, "levels", pairs) for pairs, _ in across]
    crossed = [lax.ppermute(averaging_kernel, ("levels", "sub"), pairs) for _, pairs in across]
    fields = (final_adjoint, lon_courant, lat_courant, upwind_flags, vertical_mixing)
    fields += (misfit, averaging_kernel, sounding_owner.reshape(1, held), sounding_target)
    groups = -(-(tracers + 2 + wide) // 4)
    flat_rows = -(-groups // 2) * 8
    own, edge, payload = call(
        functools.partial(edges_kernel, moves),
        60,
        out_shape=[shape(planes, levels, rows, lanes), shape(planes, levels, rows, LANES)]
        + [shape(flat_rows, held)],
        in_specs=[HBM] * 9,
        out_specs=[VMEM] * 3,
        scratch_shapes=room(*fields)
        + [pltpu.VMEM((planes, levels, 8, lanes), F32), pltpu.SemaphoreType.DMA((9,))],
        name="edges",
    )(*fields)
    edge = lax.ppermute(edge, "sub", sub_pairs)
    swapped = lax.ppermute(payload, "sub", sub_pairs)
    edge, beside, crossed, swapped = lax.optimization_barrier((edge, beside, crossed, swapped))
    depth = tracers + 5 + (tracers + 3) // 2
    body, first, second, *parts = call(
        functools.partial(spread_kernel, moves, columns),
        8,
        out_shape=[shape(planes, levels, rows, lanes)]
        + [shape(depth, levels, 2, lanes)] * 2
        + [shape(planes, STEPS, rows, lanes)] * number,
        in_specs=[VMEM] * 2,
        out_specs=[VMEM] * (3 + number),
        name="spread",
    )(own, edge)
    parts = [lax.ppermute(part, "levels", pairs) for part, (pairs, _) in zip(parts, across)]
    both = call(
        functools.partial(payload_kernel, number, levels, tracers),
        8,
        out_shape=shape(2, groups, 4, held),
        in_specs=[VMEM] * (2 + 2 * number),
        out_specs=VMEM,
        scratch_shapes=[pltpu.VMEM((flat_rows, held), F32)],
        name="payload",
    )(payload, *beside, swapped, *crossed)
    if tiles == 4:
        got = [both] + [lax.ppermute(both, "tiles", [(i, i ^ k) for i in range(tiles)]) for k in (1, 2, 3)]
    else:
        got = [lax.all_gather(both, "tiles", tiled=True)]

    blocks = [body, swap_tiles(first, 0), swap_tiles(second, 1)]

    held_here = got[0].shape[0]
    sources = held_here if len(got) > 1 else max(1, min(held_here, CHUNK // held))
    batch = sources * len(got) * held
    count = window(STEPS - 1, levels)[1] * tracers
    sizes = (tracers, levels, rows, columns)
    prepared = [((count, 16, batch), BF16), ((lanes, batch), BF16), ((8, batch), F32)]
    working = [pltpu.VMEM((flat_rows, batch), F32), pltpu.VMEM((2, tracers, flat_rows, batch), F32)]
    if held_here == sources:
        got = call(
            functools.partial(prepare_kernel, *sizes),
            16,
            out_shape=[jax.ShapeDtypeStruct(*x) for x in prepared],
            in_specs=[VMEM] * len(got),
            out_specs=[VMEM] * 3,
            scratch_shapes=working,
            name="prepare",
        )(*got)
        parts, got = lax.optimization_barrier((parts, got))
    if number:
        far = call(
            functools.partial(far_kernel, number),
            8,
            out_shape=[shape(depth, STEPS, 2, lanes)] * (2 * number),
            in_specs=[VMEM] * number,
            out_specs=[VMEM] * (2 * number),
            name="far",
        )(*parts)
    for i in range(number):
        blocks += [parts[i], swap_tiles(far[2 * i], 0), swap_tiles(far[2 * i + 1], 1)]

    def forcing_of(steps):
        force_shape = (len(steps), tracers, wide, 8, lanes)
        scratch = [pltpu.VMEM((count * 16, batch), BF16)]
        block = pl.BlockSpec((sources, groups, 4, held), lambda i: (i, 0, 0, 0))
        specs, limit = [block], 60
        if len(got) == 3:
            specs = [pl.BlockSpec(x.shape, lambda i, rank=x.ndim: (0,) * rank) for x in got]
            limit = 24
        else:
            scratch += [pltpu.VMEM(*x) for x in prepared] + working
        return call(
            functools.partial(forcing_kernel, steps, *sizes),
            limit,
            flops=2 * len(steps) * count * 16 * batch * lanes,
            out_shape=shape(*force_shape),
            grid=(held_here // sources,),
            in_specs=specs,
            out_specs=pl.BlockSpec(force_shape, lambda i: (0, 0, 0, 0, 0)),
            scratch_shapes=scratch,
            name="forcing" + str(steps[0]),
        )(*got)

    forcings = [forcing_of(steps) for steps in FORCED]
    state_shape = (tracers, wide + 2, 8, lanes)
    coef_shape = (6, wide + 2, 8, lanes)
    flux_shape = (tracers, 8, lanes)

    def messages(round_id):
        count = window(STEPS - round_id * WIDTH, levels)[1]
        return [shape(tracers + (tracers + 1) // 2, count, 2, lanes)] * 2

    scratch = [pltpu.VMEM(state_shape, F32)] * 3
    state, coef, flux, first, second = call(
        functools.partial(first_kernel, moves, levels),
        16,
        out_shape=[shape(*state_shape), shape(*coef_shape), shape(*flux_shape), *messages(1)],
        in_specs=[VMEM] * (len(blocks) + len(forced_in(0))) + [SMEM],
        out_specs=[VMEM] * 5,
        scratch_shapes=scratch + [pltpu.VMEM((7, wide + 2, 8, lanes), F32)],
        name="round0",
    )(*blocks, *[forcings[i] for i in forced_in(0)], level_profile)
    half = rows // 2 if bands == 2 else rows
    for round_id in range(1, ROUNDS):
        first, second = swap_tiles(first, 0), swap_tiles(second, 1)
        if round_id < ROUNDS - 1:
            outs = [shape(*state_shape), shape(*flux_shape), *messages(round_id + 1)]
            extra = []
        else:
            part = shape(tracers, half, columns)
            outs = [shape(tracers, levels, rows, columns), part, part]
            extra = [pltpu.VMEM(flux_shape, F32)]
        results = call(
            functools.partial(next_kernel, round_id, levels, rows),
            16,
            out_shape=outs,
            in_specs=[VMEM] * (4 + len(forced_in(round_id))) + [SMEM, VMEM],
            out_specs=[VMEM] * len(outs),
            scratch_shapes=extra + scratch,
            name="round" + str(round_id),
        )(state, coef, first, second, *[forcings[i] for i in forced_in(round_id)], level_profile, flux)
        if round_id < ROUNDS - 1:
            state, flux, first, second = results
    adjoint, keep, give = results
    if bands == 2:
        flux_gradient = keep + lax.ppermute(give, "levels", [(0, 1), (1, 0)])
    else:
        flux_gradient = lax.psum_scatter(keep, "levels", scatter_dimension=1, tiled=True)
    return adjoint, flux_gradient


def solution(mesh):
    return jax.shard_map(
        per_device,
        mesh=mesh,
        in_specs=(
            P("groups", "levels", "tiles", "sub"),
            P(("groups", "levels"), "tiles", "sub"),
            P(("groups", "levels"), "tiles", "sub"),
            P(None, ("groups", "levels"), "tiles", "sub"),
            P(("groups", "levels"), "tiles", "sub"),
            P("levels"),
            P(("groups", "tiles", "sub"), None),
            P(("groups", "tiles", "sub")),
            P(None, ("groups", "tiles", "sub")),
            P("levels", ("groups", "tiles", "sub")),
        ),
        out_specs=(P("groups", "levels", "tiles", "sub"), P("groups", ("tiles", "levels"), "sub")),
        check_vma=False,
    )
```

```python
import functools

import jax
import jax.numpy as jnp
from jax import lax
from jax.experimental import pallas as pl
from jax.experimental.pallas import tpu as pltpu
from jax.sharding import PartitionSpec as P

STEPS = 6
WIDTH = 3
FORCED = ((0, 1, 2, 5), (3, 4))
ROUNDS = STEPS // WIDTH
LANES = 128
CHUNK = 3072
F32 = jnp.float32
BF16 = jnp.bfloat16
VMEM = pl.BlockSpec(memory_space=pltpu.VMEM)
SMEM = pl.BlockSpec(memory_space=pltpu.SMEM)
HBM = pl.BlockSpec(memory_space=pltpu.HBM)
MIB = 1024 * 1024


def window(margin, levels):
    count = lax.axis_size("levels")
    if count == 1:
        return 0, levels
    if count == 2:
        return lax.axis_index("levels") * (STEPS - margin), levels + margin
    return STEPS - margin, levels + 2 * margin


def level_moves(levels):
    count = lax.axis_size("levels")
    band = lax.axis_index("levels")
    if count == 1:
        return []
    if count == 2:
        return [([(0, 1), (1, 0)], (levels - STEPS) * (1 - band), levels * (1 - band))]
    up = [(i, i + 1) for i in range(count - 1)]
    down = [(i + 1, i) for i in range(count - 1)]
    return [(up, levels - STEPS, 0), (down, 0, STEPS + levels)]


def swap_tiles(value, odd):
    tiles = lax.axis_size("tiles")
    pairs = []
    for low in range(odd, tiles - 1, 2):
        pairs += [(low, low + 1), (low + 1, low)]
    return lax.ppermute(value, "tiles", pairs)


def is_even():
    return lax.rem(lax.axis_index("tiles"), 2) == 0


def own_planes(adj, lon, lat, flags, mix):
    tracers, levels, rows, _ = adj.shape
    last_band = lax.axis_index("levels") == lax.axis_size("levels") - 1
    last_tile = lax.axis_index("tiles") == lax.axis_size("tiles") - 1
    shape = lon.shape
    level_ids = lax.broadcasted_iota(jnp.int32, shape, 0)
    row_ids = lax.broadcasted_iota(jnp.int32, shape, 1)
    top = (level_ids == levels - 1) & last_band
    shut = (row_ids == rows - 1) & last_tile
    first = flags[0].astype(F32)
    second = flags[1].astype(F32)
    lat_open = jnp.where(shut, 0.0, lat[...])
    planes = [adj[t] for t in range(tracers)]
    planes.append(jnp.where(top, 0.0, mix[...]))
    planes.append(lon[...] * first)
    planes.append(lon[...] * (1.0 - first))
    planes.append(lat_open * second)
    planes.append(lat_open * (1.0 - second))
    return planes


def fetch(sources, targets, sems):
    copies = [pltpu.make_async_copy(x, y, sems.at[i]) for i, (x, y) in enumerate(zip(sources, targets))]
    for copy in copies:
        copy.start()
    for copy in copies:
        copy.wait()


def soundings_of(number, flat, misfit, kernel, owner, target):
    tracers, levels = misfit.shape[0], kernel.shape[0]
    base = tracers + 2
    flat[...] = jnp.zeros_like(flat)
    flat[0:tracers] = misfit[...]
    flat[tracers : tracers + 1] = owner[...].astype(F32)
    flat[tracers + 1 : base] = target[...].astype(F32).reshape(1, target.shape[0])
    if number == 1:

        @pl.when(lax.axis_index("levels") == 0)
        def _():
            flat[base : base + levels] = kernel[...]

        @pl.when(lax.axis_index("levels") == 1)
        def _():
            flat[base + STEPS : base + STEPS + levels] = kernel[...]
    else:
        start = base + (STEPS if number else 0)
        flat[start : start + levels] = kernel[...]


def edges_kernel(moves, *refs):
    inputs, own_out, edge_out, base = refs[:9], refs[9], refs[10], refs[11]
    held, buf, sems = refs[-11:-2], refs[-2], refs[-1]
    fetch(inputs, held, sems)
    soundings_of(len(moves()), base, *held[5:])
    held = held[:5]
    _, levels, rows, columns = held[0].shape
    width = edge_out.shape[-1]
    tail = columns // LANES * LANES
    gap = columns - tail
    buf[...] = jnp.zeros_like(buf)
    for p, plane in enumerate(own_planes(*held)):
        buf[p, :, 0:rows, 0:columns] = plane
    own_out[...] = buf[:, :, 0:rows, :]
    lane = lax.broadcasted_iota(jnp.int32, (8, LANES), 1)
    for p in range(buf.shape[0]):
        for l in range(levels):
            start = pltpu.roll(buf[p, l, :, 0:LANES], gap, 1)
            end = pltpu.roll(buf[p, l, :, tail : tail + LANES], width - gap, 1)
            both = jnp.where(
                lane >= width - STEPS,
                end,
                jnp.where((lane >= gap) & (lane < gap + STEPS), start, 0.0),
            )
            edge_out[p, l] = both[0:rows]

def payload_kernel(number, levels, tracers, *refs):
    out, flat = refs[-2:]
    base = tracers + 2
    for half in range(2):
        part = refs[half * (1 + number) : (half + 1) * (1 + number)]
        flat[...] = part[0][...]
        if number == 1:

            @pl.when(lax.axis_index("levels") == 0)
            def _(part=part):
                flat[base + levels : base + levels + STEPS] = part[1][0:STEPS]

            @pl.when(lax.axis_index("levels") == 1)
            def _(part=part):
                flat[base : base + STEPS] = part[1][levels - STEPS : levels]

        if number == 2:
            flat[base : base + STEPS] = part[1][levels - STEPS : levels]
            flat[base + STEPS + levels : base + 2 * STEPS + levels] = part[2][0:STEPS]
        for group in range(out.shape[1]):
            out[half, group] = flat[4 * group : 4 * group + 4]


def with_edges(plane, edge, columns):
    tail = columns // LANES * LANES
    lane = lax.broadcasted_iota(jnp.int32, plane.shape[:-1] + (LANES,), 2)
    return jnp.where(lane < columns - tail, plane[..., tail : tail + LANES], edge)


def tile_messages(body, first_out, second_out):
    planes, _, rows, _ = body.shape
    tracers = planes - 5
    mixing, east, west, north, south = range(tracers, planes)

    def rows_of(out, first, third):
        near = list(range(tracers)) + [mixing, north, south, east, west]
        for entry, p in enumerate(near):
            out[entry] = body[p, :, first : first + 2, :]
        for k, p in enumerate(list(range(tracers)) + [mixing, south, south]):
            half = slice(k % 2, k % 2 + 1)
            out[len(near) + k // 2, :, half, :] = body[p, :, third : third + 1, :]

    @pl.when(is_even())
    def _():
        rows_of(first_out, rows - 2, rows - 3)
        rows_of(second_out, 0, 2)

    @pl.when(jnp.logical_not(is_even()))
    def _():
        rows_of(first_out, 0, 2)
        rows_of(second_out, rows - 2, rows - 3)


def spread_kernel(moves, columns, own, edge, body, first_out, second_out, *outs):
    tail = columns // LANES * LANES
    body[:, :, :, 0:tail] = own[:, :, :, 0:tail]
    for p in range(own.shape[0]):
        body[p, :, :, tail : tail + LANES] = with_edges(own[p], edge[p], columns)
    for out, (_, start, _) in zip(outs, moves()):
        out[...] = body[:, pl.ds(start, STEPS)]
    tile_messages(body, first_out, second_out)


def far_kernel(number, *refs):
    for i in range(number):
        tile_messages(refs[i], refs[number + 2 * i], refs[number + 2 * i + 1])


def advance(step, src, dst, outer, coef, forcing, profile, flux, levels):
    tracers = src.shape[0]
    first, count = window(STEPS - 1 - step, levels)
    own, _ = window(0, levels)
    lanes = src.shape[-1]
    ids = lax.broadcasted_iota(jnp.int32, src.shape[-2:], 0)
    force, index = forcing(step)
    total = [flux[t] for t in range(tracers)]
    for i in range(count):
        at = first + i
        up, down = coef[0, at + 1], coef[0, at]
        east, west, north, south = (coef[c, at + 1] for c in range(1, 5))
        if outer is not None:
            up_outer, down_outer = coef[5, at + 1], coef[5, at]
        own_id = at - own
        inside = (own_id >= 0) & (own_id < levels)
        weight = jnp.where(inside, profile[jnp.clip(own_id, 0, levels - 1)], 0.0)
        for t in range(tracers):
            a = src[t, at + 1]
            b = a + up * (src[t, at + 2] - a) + down * (src[t, at] - a)
            moved = b + east * (pltpu.roll(b, lanes - 1, 1) - b) + west * (pltpu.roll(b, 1, 1) - b)
            above, below = pltpu.roll(b, 7, 0), pltpu.roll(b, 1, 0)
            if outer is not None:
                a = outer[t, at + 1]
                b_outer = a + up_outer * (outer[t, at + 2] - a) + down_outer * (outer[t, at] - a)
                above = jnp.where(ids == 5, b_outer, above)
                below = jnp.where(ids == 6, b_outer, below)
            moved = moved + north * (above - b) + south * (below - b)
            new = moved + force[index, t, at]
            dst[t, at + 1] = new
            total[t] = total[t] + weight * new
    for t in range(tracers):
        flux[t] = total[t]


def clear_pads(ref):
    levels = ref.shape[1]
    ref[:, 0:1] = jnp.zeros((ref.shape[0], 1) + ref.shape[2:], F32)
    ref[:, levels - 1 : levels] = jnp.zeros((ref.shape[0], 1) + ref.shape[2:], F32)


def forced_in(number):
    return [i for i, steps in enumerate(FORCED) if any(step // WIDTH == number for step in steps)]


def run_steps(number, work, other, outer, coef, forcings, profile, flux, levels):
    def forcing(step):
        for i, ref in zip(forced_in(number), forcings):
            if step in FORCED[i]:
                return ref, FORCED[i].index(step)

    refs = [work, other]
    for i in range(WIDTH):
        extra = outer if i == 0 else None
        advance(number * WIDTH + i, refs[i % 2], refs[(i + 1) % 2], extra, coef, forcing, profile, flux, levels)
    return refs[WIDTH % 2]


def send_rows(number, state, first_out, second_out, rows, levels):
    start, count = window(STEPS - (number + 1) * WIDTH, levels)
    pick = pl.ds(start + 1, count)
    tracers = state.shape[0]
    even = is_even()
    for t in range(tracers):
        upper, lower = state[t, pick, rows - 2 : rows, :], state[t, pick, 0:2, :]
        first_out[t] = jnp.where(even, upper, lower)
        second_out[t] = jnp.where(even, lower, upper)
        upper, lower = state[t, pick, rows - 3 : rows - 2, :], state[t, pick, 2:3, :]
        entry, half = tracers + t // 2, slice(t % 2, t % 2 + 1)
        first_out[entry, :, half, :] = jnp.where(even, upper, lower)
        second_out[entry, :, half, :] = jnp.where(even, lower, upper)


def place_outer(ref, plane, pick, first, second, entry, half):
    even = is_even()
    one, two = first[entry, :, half : half + 1, :], second[entry, :, half : half + 1, :]
    ref[plane, pick, 5:6, :] = jnp.where(even, one, two)
    ref[plane, pick, 6:7, :] = jnp.where(even, two, one)


def first_kernel(moves, levels, *refs):
    number = len(moves())
    groups = [refs[3 * i : 3 * i + 3] for i in range(1 + number)]
    refs = refs[3 * (1 + number) :]
    count = len(forced_in(0))
    forcings, profile = refs[:count], refs[count]
    state_out, coef_out, flux, first_out, second_out, work, other, outer, raw = refs[count + 1 :]
    planes, _, rows, lanes = groups[0][0].shape
    tracers = planes - 5
    mixing, east, west, north, south = range(tracers, planes)
    raw[...] = jnp.zeros_like(raw)
    flux[...] = jnp.zeros_like(flux)
    clear_pads(work)
    clear_pads(other)
    clear_pads(outer)
    even = is_even()
    starts = [window(0, levels)[0]] + [slot for _, _, slot in moves()]
    for (body, first, second), start in zip(groups, starts):
        pick = pl.ds(start + 1, body.shape[1])
        for p in range(planes):
            ref, plane = (work, p) if p < tracers else (raw, p - tracers)
            ref[plane, pick, 0:rows, :] = body[p]
        near = list(range(tracers)) + [mixing, north, south, east, west]
        for entry, p in enumerate(near):
            ref, plane = (work, p) if p < tracers else (raw, p - tracers)
            ref[plane, pick, rows : rows + 2, :] = jnp.where(even, first[entry], second[entry])
            ref[plane, pick, 6:8, :] = jnp.where(even, second[entry], first[entry])
        for k in range(tracers):
            place_outer(outer, k, pick, first, second, len(near) + k // 2, k % 2)
        for plane, k in ((5, tracers), (6, tracers + 1)):
            place_outer(raw, plane, pick, first, second, len(near) + k // 2, k % 2)
    coef_out[0] = raw[0]
    coef_out[1] = raw[1]
    coef_out[3] = raw[3]
    coef_out[5] = raw[5]
    ids = lax.broadcasted_iota(jnp.int32, (8, lanes), 0)
    for l in range(raw.shape[1]):
        coef_out[2, l] = pltpu.roll(raw[2, l], 1, 1)
        coef_out[4, l] = jnp.where(ids == 6, raw[6, l], pltpu.roll(raw[4, l], 1, 0))
    last = run_steps(0, work, other, outer, coef_out, forcings, profile, flux, levels)
    state_out[...] = last[...]
    send_rows(0, state_out, first_out, second_out, rows, levels)


def next_kernel(number, levels, rows, state, coef, first, second, *refs):
    count = len(forced_in(number))
    forcings, profile, flux_in = refs[:count], refs[count], refs[count + 1]
    refs = refs[count + 2 :]
    work, other, outer = refs[-3:]
    start, size = window(STEPS - number * WIDTH, levels)
    pick = pl.ds(start + 1, size)
    even = is_even()
    tracers = state.shape[0]
    work[...] = state[...]
    for t in range(tracers):
        work[t, pick, rows : rows + 2, :] = jnp.where(even, first[t], second[t])
        work[t, pick, 6:8, :] = jnp.where(even, second[t], first[t])
    clear_pads(other)
    clear_pads(outer)
    for t in range(tracers):
        place_outer(outer, t, pick, first, second, tracers + t // 2, t % 2)
    if number < ROUNDS - 1:
        state_out, flux, first_out, second_out = refs[:-3]
        flux[...] = flux_in[...]
        last = run_steps(number, work, other, outer, coef, forcings, profile, flux, levels)
        state_out[...] = last[...]
        send_rows(number, state_out, first_out, second_out, rows, levels)
        return
    adjoint, keep, give, flux = refs[:-3]
    flux[...] = flux_in[...]
    last = run_steps(number, work, other, outer, coef, forcings, profile, flux, levels)
    own, _ = window(0, levels)
    columns = adjoint.shape[-1]
    adjoint[...] = last[:, pl.ds(own + 1, levels), 0:rows, 0:columns]
    if lax.axis_size("levels") == 2:
        half = rows // 2
        upper = lax.axis_index("levels") == 1
        low, high = flux[:, 0:half, 0:columns], flux[:, half:rows, 0:columns]
        keep[...] = jnp.where(upper, high, low)
        give[...] = jnp.where(upper, low, high)
    else:
        keep[...] = flux[:, 0:rows, 0:columns]
        give[...] = jnp.zeros_like(give)


def prepare(tracers, levels, rows, columns, got, terms, right, keys, flat, parts):
    sources, groups, _, held = got[0].shape
    lanes = right.shape[0]
    subs = lax.axis_size("sub")
    tile, sub = lax.axis_index("tiles"), lax.axis_index("sub")
    for s in range(sources * len(got)):
        ref = got[s // sources]
        for group in range(groups):
            flat[4 * group : 4 * group + 4, s * held : (s + 1) * held] = ref[s % sources, group]
    owner = flat[tracers : tracers + 1, :]
    target = flat[tracers + 1 : tracers + 2, :]
    cells = rows * columns
    step = jnp.floor((target + 0.5) * (1.0 / cells))
    cell = target - step * cells
    row = jnp.floor((cell + 0.5) * (1.0 / columns))
    col = cell - row * columns
    owner_tile = jnp.floor((owner + 0.5) * (1.0 / subs))
    row = row + (owner_tile - tile.astype(F32)) * rows
    shift = owner - owner_tile * subs - sub.astype(F32)
    col = col + jnp.where(shift < 0, shift + subs, shift) * columns
    east_side = col < columns + STEPS
    west_side = col >= subs * columns - STEPS
    lane = jnp.where(east_side, col, jnp.where(west_side, col - subs * columns + lanes, -1.0))
    close = (row >= 1 - WIDTH) & (row <= rows + WIDTH - 2)
    key = jnp.where(close, step * 8 + jnp.where(row < 0, row + 8, row), -1.0)
    for start in range(0, lanes, LANES):
        ids = lax.broadcasted_iota(jnp.int32, (LANES, lane.shape[1]), 0).astype(F32) + start
        right[start : start + LANES] = jnp.where(ids == lane, 1.0, 0.0).astype(BF16)
    for t in range(tracers):
        value = flat[...] * flat[t : t + 1, :]
        high = value.astype(BF16).astype(F32)
        parts[0, t] = high
        parts[1, t] = value - high
    first, count = window(STEPS - 1, levels)
    batch = flat.shape[1]
    for i in range(count):
        for t in range(tracers):
            row_id = pl.ds(tracers + 2 + first + i, 1)
            both = [jnp.broadcast_to(parts[k, t, row_id, :], (8, batch)) for k in range(2)]
            terms[i * tracers + t] = jnp.concatenate(both, axis=0).astype(BF16)
    keys[...] = jnp.broadcast_to(key, keys.shape)


def prepare_kernel(tracers, levels, rows, columns, *refs):
    prepare(tracers, levels, rows, columns, refs[:-5], *refs[-5:])


def forcing_kernel(steps, tracers, levels, rows, columns, *refs):
    if len(refs) > 4:
        out, terms, right, keys = refs[-6:-2]
        prepare(tracers, levels, rows, columns, refs[:-6], terms, right, keys, *refs[-2:])
    else:
        terms, right, keys, out = refs
    first, _ = window(STEPS - 1, levels)
    batch = keys.shape[1]
    ids = lax.broadcasted_iota(jnp.int32, (8, batch), 0).astype(F32)
    for i, now in enumerate(steps):
        begin, size = window(STEPS - 1 - now, levels)
        last = now % WIDTH == WIDTH - 1 and 2 * rows == 8
        if last and now - WIDTH in steps:
            continue
        mate = now + WIDTH if last and now + WIDTH in steps else None
        wanted = ids + now * 8.0
        if mate is not None:
            wanted = jnp.where(ids < rows, wanted, ids - rows + mate * 8.0)
        hit = jnp.where(keys[...] == wanted, 1.0, 0.0)
        mask = jnp.concatenate([hit, hit], axis=0).astype(BF16)
        pick = pl.ds((begin - first) * tracers, size * tracers)
        left = (terms[pick] * mask[None]).reshape(size * tracers * 16, batch)
        product = lax.dot_general(
            left, right[...], (((1,), (1,)), ((), ())), preferred_element_type=F32
        )
        for l in range(size):
            for t in range(tracers):
                base = (l * tracers + t) * 16
                value = product[base : base + 8] + product[base + 8 : base + 16]
                places = [((i, t, begin + l), value)]
                if mate is not None:
                    places.append(((steps.index(mate), t, begin + l), pltpu.roll(value, rows, 0)))
                for place, part in places:
                    if pl.num_programs(0) == 1:
                        out[place] = part
                    else:
                        out[place] = jnp.where(pl.program_id(0) == 0, 0.0, out[place]) + part


def per_device(
    final_adjoint,
    lon_courant,
    lat_courant,
    upwind_flags,
    vertical_mixing,
    level_profile,
    sounding_owner,
    sounding_target,
    misfit,
    averaging_kernel,
):
    tracers, levels, rows, columns = final_adjoint.shape
    held = misfit.shape[1]
    bands, subs, tiles = (lax.axis_size(name) for name in ("levels", "sub", "tiles"))
    planes = tracers + 5
    lanes = -(-(columns + 2 * STEPS) // LANES) * LANES
    wide = window(STEPS, levels)[1]
    moves = functools.partial(level_moves, levels)
    number = len(moves())
    shape = lambda *dims: jax.ShapeDtypeStruct(dims, F32)
    sub_pairs = [(i, (i + 1) % subs) for i in range(subs)]

    def call(body, limit, flops=0, **kwargs):
        return pl.pallas_call(
            body,
            compiler_params=pltpu.CompilerParams(vmem_limit_bytes=limit * MIB),
            cost_estimate=pl.CostEstimate(flops=flops, bytes_accessed=MIB, transcendentals=0),
            **kwargs,
        )

    def room(*arrays):
        return [pltpu.VMEM(x.shape, x.dtype) for x in arrays]

    beside = [lax.ppermute(averaging_kernel, "levels", pairs) for pairs, _, _ in moves()]
    fields = (final_adjoint, lon_courant, lat_courant, upwind_flags, vertical_mixing)
    fields += (misfit, averaging_kernel, sounding_owner.reshape(1, held), sounding_target)
    groups = -(-(tracers + 2 + wide) // 4)
    flat_rows = -(-groups // 2) * 8
    own, edge, payload = call(
        functools.partial(edges_kernel, moves),
        60,
        out_shape=[shape(planes, levels, rows, lanes), shape(planes, levels, rows, LANES)]
        + [shape(flat_rows, held)],
        in_specs=[HBM] * 9,
        out_specs=[VMEM] * 3,
        scratch_shapes=room(*fields)
        + [pltpu.VMEM((planes, levels, 8, lanes), F32), pltpu.SemaphoreType.DMA((9,))],
        name="edges",
    )(*fields)
    edge = lax.ppermute(edge, "sub", sub_pairs)
    swapped = lax.ppermute(payload, "sub", sub_pairs)
    edge, beside, swapped = lax.optimization_barrier((edge, beside, swapped))
    crossed = [lax.ppermute(part, "sub", sub_pairs) for part in beside]
    depth = tracers + 5 + (tracers + 3) // 2
    body, first, second, *parts = call(
        functools.partial(spread_kernel, moves, columns),
        8,
        out_shape=[shape(planes, levels, rows, lanes)]
        + [shape(depth, levels, 2, lanes)] * 2
        + [shape(planes, STEPS, rows, lanes)] * number,
        in_specs=[VMEM] * 2,
        out_specs=[VMEM] * (3 + number),
        name="spread",
    )(own, edge)
    parts = [lax.ppermute(part, "levels", pairs) for part, (pairs, _, _) in zip(parts, moves())]
    both = call(
        functools.partial(payload_kernel, number, levels, tracers),
        8,
        out_shape=shape(2, groups, 4, held),
        in_specs=[VMEM] * (2 + 2 * number),
        out_specs=VMEM,
        scratch_shapes=[pltpu.VMEM((flat_rows, held), F32)],
        name="payload",
    )(payload, *beside, swapped, *crossed)
    if tiles == 4:
        got = [both] + [lax.ppermute(both, "tiles", [(i, i ^ k) for i in range(tiles)]) for k in (1, 2, 3)]
    else:
        got = [lax.all_gather(both, "tiles", tiled=True)]

    blocks = [body, swap_tiles(first, 0), swap_tiles(second, 1)]

    held_here = got[0].shape[0]
    sources = held_here if len(got) > 1 else max(1, min(held_here, CHUNK // held))
    batch = sources * len(got) * held
    count = window(STEPS - 1, levels)[1] * tracers
    sizes = (tracers, levels, rows, columns)
    prepared = [((count, 16, batch), BF16), ((lanes, batch), BF16), ((8, batch), F32)]
    working = [pltpu.VMEM((flat_rows, batch), F32), pltpu.VMEM((2, tracers, flat_rows, batch), F32)]
    if held_here == sources:
        got = call(
            functools.partial(prepare_kernel, *sizes),
            16,
            out_shape=[jax.ShapeDtypeStruct(*x) for x in prepared],
            in_specs=[VMEM] * len(got),
            out_specs=[VMEM] * 3,
            scratch_shapes=working,
            name="prepare",
        )(*got)
        parts, got = lax.optimization_barrier((parts, got))
    if number:
        far = call(
            functools.partial(far_kernel, number),
            8,
            out_shape=[shape(depth, STEPS, 2, lanes)] * (2 * number),
            in_specs=[VMEM] * number,
            out_specs=[VMEM] * (2 * number),
            name="far",
        )(*parts)
    for i in range(number):
        blocks += [parts[i], swap_tiles(far[2 * i], 0), swap_tiles(far[2 * i + 1], 1)]

    def forcing_of(steps):
        force_shape = (len(steps), tracers, wide, 8, lanes)
        scratch = []
        block = pl.BlockSpec((sources, groups, 4, held), lambda i: (i, 0, 0, 0))
        specs, limit = [block], 60
        if len(got) == 3:
            specs = [pl.BlockSpec(x.shape, lambda i, rank=x.ndim: (0,) * rank) for x in got]
            limit = 24
        else:
            scratch += [pltpu.VMEM(*x) for x in prepared] + working
        return call(
            functools.partial(forcing_kernel, steps, *sizes),
            limit,
            flops=2 * len(steps) * count * 16 * batch * lanes,
            out_shape=shape(*force_shape),
            grid=(held_here // sources,),
            in_specs=specs,
            out_specs=pl.BlockSpec(force_shape, lambda i: (0, 0, 0, 0, 0)),
            scratch_shapes=scratch,
            name="forcing" + str(steps[0]),
        )(*got)

    forcings = [forcing_of(steps) for steps in FORCED]
    state_shape = (tracers, wide + 2, 8, lanes)
    coef_shape = (6, wide + 2, 8, lanes)
    flux_shape = (tracers, 8, lanes)

    def messages(round_id):
        count = window(STEPS - round_id * WIDTH, levels)[1]
        return [shape(tracers + (tracers + 1) // 2, count, 2, lanes)] * 2

    scratch = [pltpu.VMEM(state_shape, F32)] * 3
    state, coef, flux, first, second = call(
        functools.partial(first_kernel, moves, levels),
        16,
        out_shape=[shape(*state_shape), shape(*coef_shape), shape(*flux_shape), *messages(1)],
        in_specs=[VMEM] * (len(blocks) + len(forced_in(0))) + [SMEM],
        out_specs=[VMEM] * 5,
        scratch_shapes=scratch + [pltpu.VMEM((7, wide + 2, 8, lanes), F32)],
        name="round0",
    )(*blocks, *[forcings[i] for i in forced_in(0)], level_profile)
    half = rows // 2 if bands == 2 else rows
    for round_id in range(1, ROUNDS):
        first, second = swap_tiles(first, 0), swap_tiles(second, 1)
        if round_id < ROUNDS - 1:
            outs = [shape(*state_shape), shape(*flux_shape), *messages(round_id + 1)]
            extra = []
        else:
            part = shape(tracers, half, columns)
            outs = [shape(tracers, levels, rows, columns), part, part]
            extra = [pltpu.VMEM(flux_shape, F32)]
        results = call(
            functools.partial(next_kernel, round_id, levels, rows),
            16,
            out_shape=outs,
            in_specs=[VMEM] * (4 + len(forced_in(round_id))) + [SMEM, VMEM],
            out_specs=[VMEM] * len(outs),
            scratch_shapes=extra + scratch,
            name="round" + str(round_id),
        )(state, coef, first, second, *[forcings[i] for i in forced_in(round_id)], level_profile, flux)
        if round_id < ROUNDS - 1:
            state, flux, first, second = results
    adjoint, keep, give = results
    if bands == 2:
        flux_gradient = keep + lax.ppermute(give, "levels", [(0, 1), (1, 0)])
    else:
        flux_gradient = lax.psum_scatter(keep, "levels", scatter_dimension=1, tiled=True)
    return adjoint, flux_gradient


def solution(mesh):
    return jax.shard_map(
        per_device,
        mesh=mesh,
        in_specs=(
            P("groups", "levels", "tiles", "sub"),
            P(("groups", "levels"), "tiles", "sub"),
            P(("groups", "levels"), "tiles", "sub"),
            P(None, ("groups", "levels"), "tiles", "sub"),
            P(("groups", "levels"), "tiles", "sub"),
            P("levels"),
            P(("groups", "tiles", "sub"), None),
            P(("groups", "tiles", "sub")),
            P(None, ("groups", "tiles", "sub")),
            P("levels", ("groups", "tiles", "sub")),
        ),
        out_specs=(P("groups", "levels", "tiles", "sub"), P("groups", ("tiles", "levels"), "sub")),
        check_vma=False,
    )
```

```python
import functools

import jax
import jax.numpy as jnp
from jax import lax
from jax.experimental import pallas as pl
from jax.experimental.pallas import tpu as pltpu
from jax.sharding import PartitionSpec as P

STEPS = 6
WIDTH = 3
FORCED = ((0, 1, 2, 5), (3, 4))
ROUNDS = STEPS // WIDTH
LANES = 128
CHUNK = 3072
F32 = jnp.float32
BF16 = jnp.bfloat16
VMEM = pl.BlockSpec(memory_space=pltpu.VMEM)
SMEM = pl.BlockSpec(memory_space=pltpu.SMEM)
HBM = pl.BlockSpec(memory_space=pltpu.HBM)
MIB = 1024 * 1024


def window(margin, levels):
    count = lax.axis_size("levels")
    if count == 1:
        return 0, levels
    if count == 2:
        return lax.axis_index("levels") * (STEPS - margin), levels + margin
    return STEPS - margin, levels + 2 * margin


def level_moves(levels):
    count = lax.axis_size("levels")
    band = lax.axis_index("levels")
    if count == 1:
        return []
    if count == 2:
        return [([(0, 1), (1, 0)], (levels - STEPS) * (1 - band), levels * (1 - band))]
    up = [(i, i + 1) for i in range(count - 1)]
    down = [(i + 1, i) for i in range(count - 1)]
    return [(up, levels - STEPS, 0), (down, 0, STEPS + levels)]


def swap_tiles(value, odd):
    tiles = lax.axis_size("tiles")
    pairs = []
    for low in range(odd, tiles - 1, 2):
        pairs += [(low, low + 1), (low + 1, low)]
    return lax.ppermute(value, "tiles", pairs)


def is_even():
    return lax.rem(lax.axis_index("tiles"), 2) == 0


def own_planes(adj, lon, lat, flags, mix):
    tracers, levels, rows, _ = adj.shape
    last_band = lax.axis_index("levels") == lax.axis_size("levels") - 1
    last_tile = lax.axis_index("tiles") == lax.axis_size("tiles") - 1
    shape = lon.shape
    level_ids = lax.broadcasted_iota(jnp.int32, shape, 0)
    row_ids = lax.broadcasted_iota(jnp.int32, shape, 1)
    top = (level_ids == levels - 1) & last_band
    shut = (row_ids == rows - 1) & last_tile
    first = flags[0].astype(F32)
    second = flags[1].astype(F32)
    lat_open = jnp.where(shut, 0.0, lat[...])
    planes = [adj[t] for t in range(tracers)]
    planes.append(jnp.where(top, 0.0, mix[...]))
    planes.append(lon[...] * first)
    planes.append(lon[...] * (1.0 - first))
    planes.append(lat_open * second)
    planes.append(lat_open * (1.0 - second))
    return planes


def fetch(sources, targets, sems):
    copies = [pltpu.make_async_copy(x, y, sems.at[i]) for i, (x, y) in enumerate(zip(sources, targets))]
    for copy in copies:
        copy.start()
    for copy in copies:
        copy.wait()


def soundings_of(number, flat, misfit, kernel, owner, target):
    tracers, levels = misfit.shape[0], kernel.shape[0]
    base = tracers + 2
    flat[...] = jnp.zeros_like(flat)
    flat[0:tracers] = misfit[...]
    flat[tracers : tracers + 1] = owner[...].astype(F32)
    flat[tracers + 1 : base] = target[...].astype(F32).reshape(1, target.shape[0])
    if number == 1:

        @pl.when(lax.axis_index("levels") == 0)
        def _():
            flat[base : base + levels] = kernel[...]

        @pl.when(lax.axis_index("levels") == 1)
        def _():
            flat[base + STEPS : base + STEPS + levels] = kernel[...]
    else:
        start = base + (STEPS if number else 0)
        flat[start : start + levels] = kernel[...]


def edges_kernel(moves, *refs):
    inputs, own_out, edge_out, base = refs[:9], refs[9], refs[10], refs[11]
    held, buf, sems = refs[-11:-2], refs[-2], refs[-1]
    fetch(inputs, held, sems)
    soundings_of(len(moves()), base, *held[5:])
    held = held[:5]
    _, levels, rows, columns = held[0].shape
    width = edge_out.shape[-1]
    tail = columns // LANES * LANES
    gap = columns - tail
    buf[...] = jnp.zeros_like(buf)
    for p, plane in enumerate(own_planes(*held)):
        buf[p, :, 0:rows, 0:columns] = plane
    own_out[...] = buf[:, :, 0:rows, :]
    lane = lax.broadcasted_iota(jnp.int32, (8, LANES), 1)
    for p in range(buf.shape[0]):
        for l in range(levels):
            start = pltpu.roll(buf[p, l, :, 0:LANES], gap, 1)
            end = pltpu.roll(buf[p, l, :, tail : tail + LANES], width - gap, 1)
            both = jnp.where(
                lane >= width - STEPS,
                end,
                jnp.where((lane >= gap) & (lane < gap + STEPS), start, 0.0),
            )
            edge_out[p, l] = both[0:rows]

def payload_kernel(number, levels, tracers, *refs):
    out, flat = refs[-2:]
    base = tracers + 2
    for half in range(2):
        part = refs[half * (1 + number) : (half + 1) * (1 + number)]
        flat[...] = part[0][...]
        if number == 1:

            @pl.when(lax.axis_index("levels") == 0)
            def _(part=part):
                flat[base + levels : base + levels + STEPS] = part[1][0:STEPS]

            @pl.when(lax.axis_index("levels") == 1)
            def _(part=part):
                flat[base : base + STEPS] = part[1][levels - STEPS : levels]

        if number == 2:
            flat[base : base + STEPS] = part[1][levels - STEPS : levels]
            flat[base + STEPS + levels : base + 2 * STEPS + levels] = part[2][0:STEPS]
        for group in range(out.shape[1]):
            out[half, group] = flat[4 * group : 4 * group + 4]


def with_edges(plane, edge, columns):
    tail = columns // LANES * LANES
    lane = lax.broadcasted_iota(jnp.int32, plane.shape[:-1] + (LANES,), 2)
    return jnp.where(lane < columns - tail, plane[..., tail : tail + LANES], edge)


def tile_messages(body, first_out, second_out):
    planes, _, rows, _ = body.shape
    tracers = planes - 5
    mixing, east, west, north, south = range(tracers, planes)

    def rows_of(out, first, third):
        near = list(range(tracers)) + [mixing, north, south, east, west]
        for entry, p in enumerate(near):
            out[entry] = body[p, :, first : first + 2, :]
        for k, p in enumerate(list(range(tracers)) + [mixing, south, south]):
            half = slice(k % 2, k % 2 + 1)
            out[len(near) + k // 2, :, half, :] = body[p, :, third : third + 1, :]

    @pl.when(is_even())
    def _():
        rows_of(first_out, rows - 2, rows - 3)
        rows_of(second_out, 0, 2)

    @pl.when(jnp.logical_not(is_even()))
    def _():
        rows_of(first_out, 0, 2)
        rows_of(second_out, rows - 2, rows - 3)


def spread_kernel(moves, columns, own, edge, body, first_out, second_out, *outs):
    tail = columns // LANES * LANES
    body[:, :, :, 0:tail] = own[:, :, :, 0:tail]
    for p in range(own.shape[0]):
        body[p, :, :, tail : tail + LANES] = with_edges(own[p], edge[p], columns)
    for out, (_, start, _) in zip(outs, moves()):
        out[...] = body[:, pl.ds(start, STEPS)]
    tile_messages(body, first_out, second_out)


def far_kernel(number, *refs):
    for i in range(number):
        tile_messages(refs[i], refs[number + 2 * i], refs[number + 2 * i + 1])


def advance(step, src, dst, outer, coef, forcing, profile, flux, levels):
    tracers = src.shape[0]
    first, count = window(STEPS - 1 - step, levels)
    own, _ = window(0, levels)
    lanes = src.shape[-1]
    ids = lax.broadcasted_iota(jnp.int32, src.shape[-2:], 0)
    force, index = forcing(step)
    total = [flux[t] for t in range(tracers)]
    for i in range(count):
        at = first + i
        up, down = coef[0, at + 1], coef[0, at]
        east, west, north, south = (coef[c, at + 1] for c in range(1, 5))
        if outer is not None:
            up_outer, down_outer = coef[5, at + 1], coef[5, at]
            stay_outer = 1.0 - up_outer - down_outer
        stay = 1.0 - up - down
        keep = 1.0 - east - west - north - south
        own_id = at - own
        inside = (own_id >= 0) & (own_id < levels)
        weight = jnp.where(inside, profile[jnp.clip(own_id, 0, levels - 1)], 0.0)
        for t in range(tracers):
            a = src[t, at + 1]
            b = stay * a + up * src[t, at + 2] + down * src[t, at]
            moved = keep * b + east * pltpu.roll(b, lanes - 1, 1) + west * pltpu.roll(b, 1, 1)
            above, below = pltpu.roll(b, 7, 0), pltpu.roll(b, 1, 0)
            if outer is not None:
                a = outer[t, at + 1]
                b_outer = stay_outer * a + up_outer * outer[t, at + 2] + down_outer * outer[t, at]
                above = jnp.where(ids == 5, b_outer, above)
                below = jnp.where(ids == 6, b_outer, below)
            moved = moved + north * above + south * below
            new = moved + force[index, t, at]
            dst[t, at + 1] = new
            total[t] = total[t] + weight * new
    for t in range(tracers):
        flux[t] = total[t]


def clear_pads(ref):
    levels = ref.shape[1]
    ref[:, 0:1] = jnp.zeros((ref.shape[0], 1) + ref.shape[2:], F32)
    ref[:, levels - 1 : levels] = jnp.zeros((ref.shape[0], 1) + ref.shape[2:], F32)


def forced_in(number):
    return [i for i, steps in enumerate(FORCED) if any(step // WIDTH == number for step in steps)]


def run_steps(number, work, other, outer, coef, forcings, profile, flux, levels):
    def forcing(step):
        for i, ref in zip(forced_in(number), forcings):
            if step in FORCED[i]:
                return ref, FORCED[i].index(step)

    refs = [work, other]
    for i in range(WIDTH):
        extra = outer if i == 0 else None
        advance(number * WIDTH + i, refs[i % 2], refs[(i + 1) % 2], extra, coef, forcing, profile, flux, levels)
    return refs[WIDTH % 2]


def send_rows(number, state, first_out, second_out, rows, levels):
    start, count = window(STEPS - (number + 1) * WIDTH, levels)
    pick = pl.ds(start + 1, count)
    tracers = state.shape[0]
    even = is_even()
    for t in range(tracers):
        upper, lower = state[t, pick, rows - 2 : rows, :], state[t, pick, 0:2, :]
        first_out[t] = jnp.where(even, upper, lower)
        second_out[t] = jnp.where(even, lower, upper)
        upper, lower = state[t, pick, rows - 3 : rows - 2, :], state[t, pick, 2:3, :]
        entry, half = tracers + t // 2, slice(t % 2, t % 2 + 1)
        first_out[entry, :, half, :] = jnp.where(even, upper, lower)
        second_out[entry, :, half, :] = jnp.where(even, lower, upper)


def place_outer(ref, plane, pick, first, second, entry, half):
    even = is_even()
    one, two = first[entry, :, half : half + 1, :], second[entry, :, half : half + 1, :]
    ref[plane, pick, 5:6, :] = jnp.where(even, one, two)
    ref[plane, pick, 6:7, :] = jnp.where(even, two, one)


def first_kernel(moves, levels, *refs):
    number = len(moves())
    groups = [refs[3 * i : 3 * i + 3] for i in range(1 + number)]
    refs = refs[3 * (1 + number) :]
    count = len(forced_in(0))
    forcings, profile = refs[:count], refs[count]
    state_out, coef_out, flux, first_out, second_out, work, other, outer, raw = refs[count + 1 :]
    planes, _, rows, lanes = groups[0][0].shape
    tracers = planes - 5
    mixing, east, west, north, south = range(tracers, planes)
    raw[...] = jnp.zeros_like(raw)
    flux[...] = jnp.zeros_like(flux)
    clear_pads(work)
    clear_pads(other)
    clear_pads(outer)
    even = is_even()
    starts = [window(0, levels)[0]] + [slot for _, _, slot in moves()]
    for (body, first, second), start in zip(groups, starts):
        pick = pl.ds(start + 1, body.shape[1])
        for p in range(planes):
            ref, plane = (work, p) if p < tracers else (raw, p - tracers)
            ref[plane, pick, 0:rows, :] = body[p]
        near = list(range(tracers)) + [mixing, north, south, east, west]
        for entry, p in enumerate(near):
            ref, plane = (work, p) if p < tracers else (raw, p - tracers)
            ref[plane, pick, rows : rows + 2, :] = jnp.where(even, first[entry], second[entry])
            ref[plane, pick, 6:8, :] = jnp.where(even, second[entry], first[entry])
        for k in range(tracers):
            place_outer(outer, k, pick, first, second, len(near) + k // 2, k % 2)
        for plane, k in ((5, tracers), (6, tracers + 1)):
            place_outer(raw, plane, pick, first, second, len(near) + k // 2, k % 2)
    coef_out[0] = raw[0]
    coef_out[1] = raw[1]
    coef_out[3] = raw[3]
    coef_out[5] = raw[5]
    ids = lax.broadcasted_iota(jnp.int32, (8, lanes), 0)
    for l in range(raw.shape[1]):
        coef_out[2, l] = pltpu.roll(raw[2, l], 1, 1)
        coef_out[4, l] = jnp.where(ids == 6, raw[6, l], pltpu.roll(raw[4, l], 1, 0))
    last = run_steps(0, work, other, outer, coef_out, forcings, profile, flux, levels)
    state_out[...] = last[...]
    send_rows(0, state_out, first_out, second_out, rows, levels)


def next_kernel(number, levels, rows, state, coef, first, second, *refs):
    count = len(forced_in(number))
    forcings, profile, flux_in = refs[:count], refs[count], refs[count + 1]
    refs = refs[count + 2 :]
    work, other, outer = refs[-3:]
    start, size = window(STEPS - number * WIDTH, levels)
    pick = pl.ds(start + 1, size)
    even = is_even()
    tracers = state.shape[0]
    work[...] = state[...]
    for t in range(tracers):
        work[t, pick, rows : rows + 2, :] = jnp.where(even, first[t], second[t])
        work[t, pick, 6:8, :] = jnp.where(even, second[t], first[t])
    clear_pads(other)
    clear_pads(outer)
    for t in range(tracers):
        place_outer(outer, t, pick, first, second, tracers + t // 2, t % 2)
    if number < ROUNDS - 1:
        state_out, flux, first_out, second_out = refs[:-3]
        flux[...] = flux_in[...]
        last = run_steps(number, work, other, outer, coef, forcings, profile, flux, levels)
        state_out[...] = last[...]
        send_rows(number, state_out, first_out, second_out, rows, levels)
        return
    adjoint, keep, give, flux = refs[:-3]
    flux[...] = flux_in[...]
    last = run_steps(number, work, other, outer, coef, forcings, profile, flux, levels)
    own, _ = window(0, levels)
    columns = adjoint.shape[-1]
    adjoint[...] = last[:, pl.ds(own + 1, levels), 0:rows, 0:columns]
    if lax.axis_size("levels") == 2:
        half = rows // 2
        upper = lax.axis_index("levels") == 1
        low, high = flux[:, 0:half, 0:columns], flux[:, half:rows, 0:columns]
        keep[...] = jnp.where(upper, high, low)
        give[...] = jnp.where(upper, low, high)
    else:
        keep[...] = flux[:, 0:rows, 0:columns]
        give[...] = jnp.zeros_like(give)


def prepare(tracers, levels, rows, columns, got, terms, right, keys, flat, parts):
    sources, groups, _, held = got[0].shape
    lanes = right.shape[0]
    subs = lax.axis_size("sub")
    tile, sub = lax.axis_index("tiles"), lax.axis_index("sub")
    for s in range(sources * len(got)):
        ref = got[s // sources]
        for group in range(groups):
            flat[4 * group : 4 * group + 4, s * held : (s + 1) * held] = ref[s % sources, group]
    owner = flat[tracers : tracers + 1, :]
    target = flat[tracers + 1 : tracers + 2, :]
    cells = rows * columns
    step = jnp.floor((target + 0.5) * (1.0 / cells))
    cell = target - step * cells
    row = jnp.floor((cell + 0.5) * (1.0 / columns))
    col = cell - row * columns
    owner_tile = jnp.floor((owner + 0.5) * (1.0 / subs))
    row = row + (owner_tile - tile.astype(F32)) * rows
    shift = owner - owner_tile * subs - sub.astype(F32)
    col = col + jnp.where(shift < 0, shift + subs, shift) * columns
    east_side = col < columns + STEPS
    west_side = col >= subs * columns - STEPS
    lane = jnp.where(east_side, col, jnp.where(west_side, col - subs * columns + lanes, -1.0))
    close = (row >= 1 - WIDTH) & (row <= rows + WIDTH - 2)
    key = jnp.where(close, step * 8 + jnp.where(row < 0, row + 8, row), -1.0)
    for start in range(0, lanes, LANES):
        ids = lax.broadcasted_iota(jnp.int32, (LANES, lane.shape[1]), 0).astype(F32) + start
        right[start : start + LANES] = jnp.where(ids == lane, 1.0, 0.0).astype(BF16)
    for t in range(tracers):
        value = flat[...] * flat[t : t + 1, :]
        high = value.astype(BF16).astype(F32)
        parts[0, t] = high
        parts[1, t] = value - high
    first, count = window(STEPS - 1, levels)
    batch = flat.shape[1]
    for i in range(count):
        for t in range(tracers):
            row_id = pl.ds(tracers + 2 + first + i, 1)
            both = [jnp.broadcast_to(parts[k, t, row_id, :], (8, batch)) for k in range(2)]
            terms[i * tracers + t] = jnp.concatenate(both, axis=0).astype(BF16)
    keys[...] = jnp.broadcast_to(key, keys.shape)


def prepare_kernel(tracers, levels, rows, columns, *refs):
    prepare(tracers, levels, rows, columns, refs[:-5], *refs[-5:])


def forcing_kernel(steps, tracers, levels, rows, columns, *refs):
    if len(refs) > 4:
        out, terms, right, keys = refs[-6:-2]
        prepare(tracers, levels, rows, columns, refs[:-6], terms, right, keys, *refs[-2:])
    else:
        terms, right, keys, out = refs
    first, _ = window(STEPS - 1, levels)
    batch = keys.shape[1]
    ids = lax.broadcasted_iota(jnp.int32, (8, batch), 0).astype(F32)
    for i, now in enumerate(steps):
        begin, size = window(STEPS - 1 - now, levels)
        last = now % WIDTH == WIDTH - 1 and 2 * rows == 8
        if last and now - WIDTH in steps:
            continue
        mate = now + WIDTH if last and now + WIDTH in steps else None
        wanted = ids + now * 8.0
        if mate is not None:
            wanted = jnp.where(ids < rows, wanted, ids - rows + mate * 8.0)
        hit = jnp.where(keys[...] == wanted, 1.0, 0.0)
        mask = jnp.concatenate([hit, hit], axis=0).astype(BF16)
        pick = pl.ds((begin - first) * tracers, size * tracers)
        left = (terms[pick] * mask[None]).reshape(size * tracers * 16, batch)
        product = lax.dot_general(
            left, right[...], (((1,), (1,)), ((), ())), preferred_element_type=F32
        )
        for l in range(size):
            for t in range(tracers):
                base = (l * tracers + t) * 16
                value = product[base : base + 8] + product[base + 8 : base + 16]
                places = [((i, t, begin + l), value)]
                if mate is not None:
                    places.append(((steps.index(mate), t, begin + l), pltpu.roll(value, rows, 0)))
                for place, part in places:
                    if pl.num_programs(0) == 1:
                        out[place] = part
                    else:
                        out[place] = jnp.where(pl.program_id(0) == 0, 0.0, out[place]) + part


def per_device(
    final_adjoint,
    lon_courant,
    lat_courant,
    upwind_flags,
    vertical_mixing,
    level_profile,
    sounding_owner,
    sounding_target,
    misfit,
    averaging_kernel,
):
    tracers, levels, rows, columns = final_adjoint.shape
    held = misfit.shape[1]
    bands, subs, tiles = (lax.axis_size(name) for name in ("levels", "sub", "tiles"))
    planes = tracers + 5
    lanes = -(-(columns + 2 * STEPS) // LANES) * LANES
    wide = window(STEPS, levels)[1]
    moves = functools.partial(level_moves, levels)
    number = len(moves())
    shape = lambda *dims: jax.ShapeDtypeStruct(dims, F32)
    sub_pairs = [(i, (i + 1) % subs) for i in range(subs)]

    def call(body, limit, flops=0, **kwargs):
        return pl.pallas_call(
            body,
            compiler_params=pltpu.CompilerParams(vmem_limit_bytes=int(limit * MIB)),
            cost_estimate=pl.CostEstimate(flops=flops, bytes_accessed=MIB, transcendentals=0),
            **kwargs,
        )

    def room(*arrays):
        return [pltpu.VMEM(x.shape, x.dtype) for x in arrays]

    beside = [lax.ppermute(averaging_kernel, "levels", pairs) for pairs, _, _ in moves()]
    fields = (final_adjoint, lon_courant, lat_courant, upwind_flags, vertical_mixing)
    fields += (misfit, averaging_kernel, sounding_owner.reshape(1, held), sounding_target)
    groups = -(-(tracers + 2 + wide) // 4)
    flat_rows = -(-groups // 2) * 8
    own, edge, payload = call(
        functools.partial(edges_kernel, moves),
        60,
        out_shape=[shape(planes, levels, rows, lanes), shape(planes, levels, rows, LANES)]
        + [shape(flat_rows, held)],
        in_specs=[HBM] * 9,
        out_specs=[VMEM] * 3,
        scratch_shapes=room(*fields)
        + [pltpu.VMEM((planes, levels, 8, lanes), F32), pltpu.SemaphoreType.DMA((9,))],
        name="edges",
    )(*fields)
    edge = lax.ppermute(edge, "sub", sub_pairs)
    swapped = lax.ppermute(payload, "sub", sub_pairs)
    edge, beside, swapped = lax.optimization_barrier((edge, beside, swapped))
    crossed = [lax.ppermute(part, "sub", sub_pairs) for part in beside]
    depth = tracers + 5 + (tracers + 3) // 2
    body, first, second, *parts = call(
        functools.partial(spread_kernel, moves, columns),
        8,
        out_shape=[shape(planes, levels, rows, lanes)]
        + [shape(depth, levels, 2, lanes)] * 2
        + [shape(planes, STEPS, rows, lanes)] * number,
        in_specs=[VMEM] * 2,
        out_specs=[VMEM] * (3 + number),
        name="spread",
    )(own, edge)
    parts = [lax.ppermute(part, "levels", pairs) for part, (pairs, _, _) in zip(parts, moves())]
    both = call(
        functools.partial(payload_kernel, number, levels, tracers),
        8,
        out_shape=shape(2, groups, 4, held),
        in_specs=[VMEM] * (2 + 2 * number),
        out_specs=VMEM,
        scratch_shapes=[pltpu.VMEM((flat_rows, held), F32)],
        name="payload",
    )(payload, *beside, swapped, *crossed)
    if tiles == 4:
        got = [both] + [lax.ppermute(both, "tiles", [(i, i ^ k) for i in range(tiles)]) for k in (1, 2, 3)]
    else:
        got = [lax.all_gather(both, "tiles", tiled=True)]

    blocks = [body, swap_tiles(first, 0), swap_tiles(second, 1)]

    held_here = got[0].shape[0]
    sources = held_here if len(got) > 1 else max(1, min(held_here, CHUNK // held))
    batch = sources * len(got) * held
    count = window(STEPS - 1, levels)[1] * tracers
    sizes = (tracers, levels, rows, columns)
    prepared = [((count, 16, batch), BF16), ((lanes, batch), BF16), ((8, batch), F32)]
    working = [pltpu.VMEM((flat_rows, batch), F32), pltpu.VMEM((2, tracers, flat_rows, batch), F32)]
    if held_here == sources:
        got = call(
            functools.partial(prepare_kernel, *sizes),
            16,
            out_shape=[jax.ShapeDtypeStruct(*x) for x in prepared],
            in_specs=[VMEM] * len(got),
            out_specs=[VMEM] * 3,
            scratch_shapes=working,
            name="prepare",
        )(*got)
        parts, got = lax.optimization_barrier((parts, got))
    if number:
        far = call(
            functools.partial(far_kernel, number),
            8,
            out_shape=[shape(depth, STEPS, 2, lanes)] * (2 * number),
            in_specs=[VMEM] * number,
            out_specs=[VMEM] * (2 * number),
            name="far",
        )(*parts)
    for i in range(number):
        blocks += [parts[i], swap_tiles(far[2 * i], 0), swap_tiles(far[2 * i + 1], 1)]

    def forcing_of(steps):
        force_shape = (len(steps), tracers, wide, 8, lanes)
        scratch = []
        block = pl.BlockSpec((sources, groups, 4, held), lambda i: (i, 0, 0, 0))
        specs, limit = [block], 60
        if len(got) == 3:
            specs = [pl.BlockSpec(x.shape, lambda i, rank=x.ndim: (0,) * rank) for x in got]
            limit = 24
        else:
            scratch += [pltpu.VMEM(*x) for x in prepared] + working
        return call(
            functools.partial(forcing_kernel, steps, *sizes),
            limit,
            flops=2 * len(steps) * count * 16 * batch * lanes,
            out_shape=shape(*force_shape),
            grid=(held_here // sources,),
            in_specs=specs,
            out_specs=pl.BlockSpec(force_shape, lambda i: (0, 0, 0, 0, 0)),
            scratch_shapes=scratch,
            name="forcing" + str(steps[0]),
        )(*got)

    forcings = [forcing_of(steps) for steps in FORCED]
    state_shape = (tracers, wide + 2, 8, lanes)
    coef_shape = (6, wide + 2, 8, lanes)
    flux_shape = (tracers, 8, lanes)

    def messages(round_id):
        count = window(STEPS - round_id * WIDTH, levels)[1]
        return [shape(tracers + (tracers + 1) // 2, count, 2, lanes)] * 2

    scratch = [pltpu.VMEM(state_shape, F32)] * 3
    state, coef, flux, first, second = call(
        functools.partial(first_kernel, moves, levels),
        16,
        out_shape=[shape(*state_shape), shape(*coef_shape), shape(*flux_shape), *messages(1)],
        in_specs=[VMEM] * (len(blocks) + len(forced_in(0))) + [SMEM],
        out_specs=[VMEM] * 5,
        scratch_shapes=scratch + [pltpu.VMEM((7, wide + 2, 8, lanes), F32)],
        name="round0",
    )(*blocks, *[forcings[i] for i in forced_in(0)], level_profile)
    half = rows // 2 if bands == 2 else rows
    for round_id in range(1, ROUNDS):
        first, second = swap_tiles(first, 0), swap_tiles(second, 1)
        if round_id < ROUNDS - 1:
            outs = [shape(*state_shape), shape(*flux_shape), *messages(round_id + 1)]
            extra = []
        else:
            part = shape(tracers, half, columns)
            outs = [shape(tracers, levels, rows, columns), part, part]
            extra = [pltpu.VMEM(flux_shape, F32)]
        results = call(
            functools.partial(next_kernel, round_id, levels, rows),
            16,
            out_shape=outs,
            in_specs=[VMEM] * (4 + len(forced_in(round_id))) + [SMEM, VMEM],
            out_specs=[VMEM] * len(outs),
            scratch_shapes=extra + scratch,
            name="round" + str(round_id),
        )(state, coef, first, second, *[forcings[i] for i in forced_in(round_id)], level_profile, flux)
        if round_id < ROUNDS - 1:
            state, flux, first, second = results
    adjoint, keep, give = results
    if bands == 2:
        flux_gradient = keep + lax.ppermute(give, "levels", [(0, 1), (1, 0)])
    else:
        flux_gradient = lax.psum_scatter(keep, "levels", scatter_dimension=1, tiled=True)
    return adjoint, flux_gradient


def solution(mesh):
    return jax.shard_map(
        per_device,
        mesh=mesh,
        in_specs=(
            P("groups", "levels", "tiles", "sub"),
            P(("groups", "levels"), "tiles", "sub"),
            P(("groups", "levels"), "tiles", "sub"),
            P(None, ("groups", "levels"), "tiles", "sub"),
            P(("groups", "levels"), "tiles", "sub"),
            P("levels"),
            P(("groups", "tiles", "sub"), None),
            P(("groups", "tiles", "sub")),
            P(None, ("groups", "tiles", "sub")),
            P("levels", ("groups", "tiles", "sub")),
        ),
        out_specs=(P("groups", "levels", "tiles", "sub"), P("groups", ("tiles", "levels"), "sub")),
        check_vma=False,
    )
```

```python
import functools

import jax
import jax.numpy as jnp
from jax import lax
from jax.experimental import pallas as pl
from jax.experimental.pallas import tpu as pltpu
from jax.sharding import PartitionSpec as P

STEPS = 6
WIDTH = 3
FORCED = ((0, 1, 2, 5), (3, 4))
ROUNDS = STEPS // WIDTH
LANES = 128
CHUNK = 3072
F32 = jnp.float32
BF16 = jnp.bfloat16
VMEM = pl.BlockSpec(memory_space=pltpu.VMEM)
SMEM = pl.BlockSpec(memory_space=pltpu.SMEM)
HBM = pl.BlockSpec(memory_space=pltpu.HBM)
MIB = 1024 * 1024


def window(margin, levels):
    count = lax.axis_size("levels")
    if count == 1:
        return 0, levels
    if count == 2:
        return lax.axis_index("levels") * (STEPS - margin), levels + margin
    return STEPS - margin, levels + 2 * margin


def level_moves(levels):
    count = lax.axis_size("levels")
    band = lax.axis_index("levels")
    if count == 1:
        return []
    if count == 2:
        return [([(0, 1), (1, 0)], (levels - STEPS) * (1 - band), levels * (1 - band))]
    up = [(i, i + 1) for i in range(count - 1)]
    down = [(i + 1, i) for i in range(count - 1)]
    return [(up, levels - STEPS, 0), (down, 0, STEPS + levels)]


def swap_tiles(value, odd):
    tiles = lax.axis_size("tiles")
    pairs = []
    for low in range(odd, tiles - 1, 2):
        pairs += [(low, low + 1), (low + 1, low)]
    return lax.ppermute(value, "tiles", pairs)


def is_even():
    return lax.rem(lax.axis_index("tiles"), 2) == 0


def own_planes(adj, lon, lat, flags, mix):
    tracers, levels, rows, _ = adj.shape
    last_band = lax.axis_index("levels") == lax.axis_size("levels") - 1
    last_tile = lax.axis_index("tiles") == lax.axis_size("tiles") - 1
    shape = lon.shape
    level_ids = lax.broadcasted_iota(jnp.int32, shape, 0)
    row_ids = lax.broadcasted_iota(jnp.int32, shape, 1)
    top = (level_ids == levels - 1) & last_band
    shut = (row_ids == rows - 1) & last_tile
    first = flags[0].astype(F32)
    second = flags[1].astype(F32)
    lat_open = jnp.where(shut, 0.0, lat[...])
    planes = [adj[t] for t in range(tracers)]
    planes.append(jnp.where(top, 0.0, mix[...]))
    planes.append(lon[...] * first)
    planes.append(lon[...] * (1.0 - first))
    planes.append(lat_open * second)
    planes.append(lat_open * (1.0 - second))
    return planes


def fetch(sources, targets, sems):
    copies = [pltpu.make_async_copy(x, y, sems.at[i]) for i, (x, y) in enumerate(zip(sources, targets))]
    for copy in copies:
        copy.start()
    for copy in copies:
        copy.wait()


def soundings_of(number, flat, misfit, kernel, owner, target):
    tracers, levels = misfit.shape[0], kernel.shape[0]
    base = tracers + 2
    flat[...] = jnp.zeros_like(flat)
    flat[0:tracers] = misfit[...]
    flat[tracers : tracers + 1] = owner[...].astype(F32)
    flat[tracers + 1 : base] = target[...].astype(F32).reshape(1, target.shape[0])
    if number == 1:

        @pl.when(lax.axis_index("levels") == 0)
        def _():
            flat[base : base + levels] = kernel[...]

        @pl.when(lax.axis_index("levels") == 1)
        def _():
            flat[base + STEPS : base + STEPS + levels] = kernel[...]
    else:
        start = base + (STEPS if number else 0)
        flat[start : start + levels] = kernel[...]


def edges_kernel(moves, *refs):
    inputs, own_out, edge_out, base = refs[:9], refs[9], refs[10], refs[11]
    held, buf, sems = refs[-11:-2], refs[-2], refs[-1]
    fetch(inputs, held, sems)
    soundings_of(len(moves()), base, *held[5:])
    held = held[:5]
    _, levels, rows, columns = held[0].shape
    width = edge_out.shape[-1]
    tail = columns // LANES * LANES
    gap = columns - tail
    buf[...] = jnp.zeros_like(buf)
    for p, plane in enumerate(own_planes(*held)):
        buf[p, :, 0:rows, 0:columns] = plane
    own_out[...] = buf[:, :, 0:rows, :]
    lane = lax.broadcasted_iota(jnp.int32, (8, LANES), 1)
    for p in range(buf.shape[0]):
        for l in range(levels):
            start = pltpu.roll(buf[p, l, :, 0:LANES], gap, 1)
            end = pltpu.roll(buf[p, l, :, tail : tail + LANES], width - gap, 1)
            both = jnp.where(
                lane >= width - STEPS,
                end,
                jnp.where((lane >= gap) & (lane < gap + STEPS), start, 0.0),
            )
            edge_out[p, l] = both[0:rows]

def payload_kernel(number, levels, tracers, *refs):
    out, flat = refs[-2:]
    base = tracers + 2
    for half in range(2):
        part = refs[half * (1 + number) : (half + 1) * (1 + number)]
        flat[...] = part[0][...]
        if number == 1:

            @pl.when(lax.axis_index("levels") == 0)
            def _(part=part):
                flat[base + levels : base + levels + STEPS] = part[1][0:STEPS]

            @pl.when(lax.axis_index("levels") == 1)
            def _(part=part):
                flat[base : base + STEPS] = part[1][levels - STEPS : levels]

        if number == 2:
            flat[base : base + STEPS] = part[1][levels - STEPS : levels]
            flat[base + STEPS + levels : base + 2 * STEPS + levels] = part[2][0:STEPS]
        for group in range(out.shape[1]):
            out[half, group] = flat[4 * group : 4 * group + 4]


def with_edges(plane, edge, columns):
    tail = columns // LANES * LANES
    lane = lax.broadcasted_iota(jnp.int32, plane.shape[:-1] + (LANES,), 2)
    return jnp.where(lane < columns - tail, plane[..., tail : tail + LANES], edge)


def tile_messages(body, first_out, second_out):
    planes, _, rows, _ = body.shape
    tracers = planes - 5
    mixing, east, west, north, south = range(tracers, planes)

    def rows_of(out, first, third):
        near = list(range(tracers)) + [mixing, north, south, east, west]
        for entry, p in enumerate(near):
            out[entry] = body[p, :, first : first + 2, :]
        for k, p in enumerate(list(range(tracers)) + [mixing, south, south]):
            half = slice(k % 2, k % 2 + 1)
            out[len(near) + k // 2, :, half, :] = body[p, :, third : third + 1, :]

    @pl.when(is_even())
    def _():
        rows_of(first_out, rows - 2, rows - 3)
        rows_of(second_out, 0, 2)

    @pl.when(jnp.logical_not(is_even()))
    def _():
        rows_of(first_out, 0, 2)
        rows_of(second_out, rows - 2, rows - 3)


def spread_kernel(moves, columns, own, edge, body, first_out, second_out, *outs):
    tail = columns // LANES * LANES
    body[:, :, :, 0:tail] = own[:, :, :, 0:tail]
    for p in range(own.shape[0]):
        body[p, :, :, tail : tail + LANES] = with_edges(own[p], edge[p], columns)
    for out, (_, start, _) in zip(outs, moves()):
        out[...] = body[:, pl.ds(start, STEPS)]
    tile_messages(body, first_out, second_out)


def stage_kernel(own, payload, own_out, payload_out):
    own_out[...] = own[...]
    payload_out[...] = payload[...]


def far_kernel(number, *refs):
    for i in range(number):
        tile_messages(refs[i], refs[number + 2 * i], refs[number + 2 * i + 1])


def advance(step, src, dst, outer, coef, forcing, profile, flux, levels):
    tracers = src.shape[0]
    first, count = window(STEPS - 1 - step, levels)
    own, _ = window(0, levels)
    lanes = src.shape[-1]
    ids = lax.broadcasted_iota(jnp.int32, src.shape[-2:], 0)
    force, index = forcing(step)
    total = [flux[t] for t in range(tracers)]
    for i in range(count):
        at = first + i
        up, down = coef[0, at + 1], coef[0, at]
        east, west, north, south = (coef[c, at + 1] for c in range(1, 5))
        if outer is not None:
            up_outer, down_outer = coef[5, at + 1], coef[5, at]
            stay_outer = 1.0 - up_outer - down_outer
        stay = 1.0 - up - down
        keep = 1.0 - east - west - north - south
        own_id = at - own
        inside = (own_id >= 0) & (own_id < levels)
        weight = jnp.where(inside, profile[jnp.clip(own_id, 0, levels - 1)], 0.0)
        for t in range(tracers):
            a = src[t, at + 1]
            b = stay * a + up * src[t, at + 2] + down * src[t, at]
            moved = keep * b + east * pltpu.roll(b, lanes - 1, 1) + west * pltpu.roll(b, 1, 1)
            above, below = pltpu.roll(b, 7, 0), pltpu.roll(b, 1, 0)
            if outer is not None:
                a = outer[t, at + 1]
                b_outer = stay_outer * a + up_outer * outer[t, at + 2] + down_outer * outer[t, at]
                above = jnp.where(ids == 5, b_outer, above)
                below = jnp.where(ids == 6, b_outer, below)
            moved = moved + north * above + south * below
            new = moved + force[index, t, at]
            dst[t, at + 1] = new
            total[t] = total[t] + weight * new
    for t in range(tracers):
        flux[t] = total[t]


def clear_pads(ref):
    levels = ref.shape[1]
    ref[:, 0:1] = jnp.zeros((ref.shape[0], 1) + ref.shape[2:], F32)
    ref[:, levels - 1 : levels] = jnp.zeros((ref.shape[0], 1) + ref.shape[2:], F32)


def forced_in(number):
    return [i for i, steps in enumerate(FORCED) if any(step // WIDTH == number for step in steps)]


def run_steps(number, work, other, outer, coef, forcings, profile, flux, levels):
    def forcing(step):
        for i, ref in zip(forced_in(number), forcings):
            if step in FORCED[i]:
                return ref, FORCED[i].index(step)

    refs = [work, other]
    for i in range(WIDTH):
        extra = outer if i == 0 else None
        advance(number * WIDTH + i, refs[i % 2], refs[(i + 1) % 2], extra, coef, forcing, profile, flux, levels)
    return refs[WIDTH % 2]


def send_rows(number, state, first_out, second_out, rows, levels):
    start, count = window(STEPS - (number + 1) * WIDTH, levels)
    pick = pl.ds(start + 1, count)
    tracers = state.shape[0]
    even = is_even()
    for t in range(tracers):
        upper, lower = state[t, pick, rows - 2 : rows, :], state[t, pick, 0:2, :]
        first_out[t] = jnp.where(even, upper, lower)
        second_out[t] = jnp.where(even, lower, upper)
        upper, lower = state[t, pick, rows - 3 : rows - 2, :], state[t, pick, 2:3, :]
        entry, half = tracers + t // 2, slice(t % 2, t % 2 + 1)
        first_out[entry, :, half, :] = jnp.where(even, upper, lower)
        second_out[entry, :, half, :] = jnp.where(even, lower, upper)


def place_outer(ref, plane, pick, first, second, entry, half):
    even = is_even()
    one, two = first[entry, :, half : half + 1, :], second[entry, :, half : half + 1, :]
    ref[plane, pick, 5:6, :] = jnp.where(even, one, two)
    ref[plane, pick, 6:7, :] = jnp.where(even, two, one)


def first_kernel(moves, levels, *refs):
    number = len(moves())
    groups = [refs[3 * i : 3 * i + 3] for i in range(1 + number)]
    refs = refs[3 * (1 + number) :]
    count = len(forced_in(0))
    forcings, profile = refs[:count], refs[count]
    state_out, coef_out, flux, first_out, second_out, work, other, outer, raw = refs[count + 1 :]
    planes, _, rows, lanes = groups[0][0].shape
    tracers = planes - 5
    mixing, east, west, north, south = range(tracers, planes)
    raw[...] = jnp.zeros_like(raw)
    flux[...] = jnp.zeros_like(flux)
    clear_pads(work)
    clear_pads(other)
    clear_pads(outer)
    even = is_even()
    starts = [window(0, levels)[0]] + [slot for _, _, slot in moves()]
    for (body, first, second), start in zip(groups, starts):
        pick = pl.ds(start + 1, body.shape[1])
        for p in range(planes):
            ref, plane = (work, p) if p < tracers else (raw, p - tracers)
            ref[plane, pick, 0:rows, :] = body[p]
        near = list(range(tracers)) + [mixing, north, south, east, west]
        for entry, p in enumerate(near):
            ref, plane = (work, p) if p < tracers else (raw, p - tracers)
            ref[plane, pick, rows : rows + 2, :] = jnp.where(even, first[entry], second[entry])
            ref[plane, pick, 6:8, :] = jnp.where(even, second[entry], first[entry])
        for k in range(tracers):
            place_outer(outer, k, pick, first, second, len(near) + k // 2, k % 2)
        for plane, k in ((5, tracers), (6, tracers + 1)):
            place_outer(raw, plane, pick, first, second, len(near) + k // 2, k % 2)
    coef_out[0] = raw[0]
    coef_out[1] = raw[1]
    coef_out[3] = raw[3]
    coef_out[5] = raw[5]
    ids = lax.broadcasted_iota(jnp.int32, (8, lanes), 0)
    for l in range(raw.shape[1]):
        coef_out[2, l] = pltpu.roll(raw[2, l], 1, 1)
        coef_out[4, l] = jnp.where(ids == 6, raw[6, l], pltpu.roll(raw[4, l], 1, 0))
    last = run_steps(0, work, other, outer, coef_out, forcings, profile, flux, levels)
    state_out[...] = last[...]
    send_rows(0, state_out, first_out, second_out, rows, levels)


def next_kernel(number, levels, rows, state, coef, first, second, *refs):
    count = len(forced_in(number))
    forcings, profile, flux_in = refs[:count], refs[count], refs[count + 1]
    refs = refs[count + 2 :]
    work, other, outer = refs[-3:]
    start, size = window(STEPS - number * WIDTH, levels)
    pick = pl.ds(start + 1, size)
    even = is_even()
    tracers = state.shape[0]
    work[...] = state[...]
    for t in range(tracers):
        work[t, pick, rows : rows + 2, :] = jnp.where(even, first[t], second[t])
        work[t, pick, 6:8, :] = jnp.where(even, second[t], first[t])
    clear_pads(other)
    clear_pads(outer)
    for t in range(tracers):
        place_outer(outer, t, pick, first, second, tracers + t // 2, t % 2)
    if number < ROUNDS - 1:
        state_out, flux, first_out, second_out = refs[:-3]
        flux[...] = flux_in[...]
        last = run_steps(number, work, other, outer, coef, forcings, profile, flux, levels)
        state_out[...] = last[...]
        send_rows(number, state_out, first_out, second_out, rows, levels)
        return
    adjoint, keep, give, flux = refs[:-3]
    flux[...] = flux_in[...]
    last = run_steps(number, work, other, outer, coef, forcings, profile, flux, levels)
    own, _ = window(0, levels)
    columns = adjoint.shape[-1]
    adjoint[...] = last[:, pl.ds(own + 1, levels), 0:rows, 0:columns]
    if lax.axis_size("levels") == 2:
        half = rows // 2
        upper = lax.axis_index("levels") == 1
        low, high = flux[:, 0:half, 0:columns], flux[:, half:rows, 0:columns]
        keep[...] = jnp.where(upper, high, low)
        give[...] = jnp.where(upper, low, high)
    else:
        keep[...] = flux[:, 0:rows, 0:columns]
        give[...] = jnp.zeros_like(give)


def prepare(tracers, levels, rows, columns, got, terms, right, keys, flat, parts):
    sources, groups, _, held = got[0].shape
    lanes = right.shape[0]
    subs = lax.axis_size("sub")
    tile, sub = lax.axis_index("tiles"), lax.axis_index("sub")
    for s in range(sources * len(got)):
        ref = got[s // sources]
        for group in range(groups):
            flat[4 * group : 4 * group + 4, s * held : (s + 1) * held] = ref[s % sources, group]
    owner = flat[tracers : tracers + 1, :]
    target = flat[tracers + 1 : tracers + 2, :]
    cells = rows * columns
    step = jnp.floor((target + 0.5) * (1.0 / cells))
    cell = target - step * cells
    row = jnp.floor((cell + 0.5) * (1.0 / columns))
    col = cell - row * columns
    owner_tile = jnp.floor((owner + 0.5) * (1.0 / subs))
    row = row + (owner_tile - tile.astype(F32)) * rows
    shift = owner - owner_tile * subs - sub.astype(F32)
    col = col + jnp.where(shift < 0, shift + subs, shift) * columns
    east_side = col < columns + STEPS
    west_side = col >= subs * columns - STEPS
    lane = jnp.where(east_side, col, jnp.where(west_side, col - subs * columns + lanes, -1.0))
    close = (row >= 1 - WIDTH) & (row <= rows + WIDTH - 2)
    key = jnp.where(close, step * 8 + jnp.where(row < 0, row + 8, row), -1.0)
    for start in range(0, lanes, LANES):
        ids = lax.broadcasted_iota(jnp.int32, (LANES, lane.shape[1]), 0).astype(F32) + start
        right[start : start + LANES] = jnp.where(ids == lane, 1.0, 0.0).astype(BF16)
    for t in range(tracers):
        value = flat[...] * flat[t : t + 1, :]
        high = value.astype(BF16).astype(F32)
        parts[0, t] = high
        parts[1, t] = value - high
    first, count = window(STEPS - 1, levels)
    batch = flat.shape[1]
    for i in range(count):
        for t in range(tracers):
            row_id = pl.ds(tracers + 2 + first + i, 1)
            both = [jnp.broadcast_to(parts[k, t, row_id, :], (8, batch)) for k in range(2)]
            terms[i * tracers + t] = jnp.concatenate(both, axis=0).astype(BF16)
    keys[...] = jnp.broadcast_to(key, keys.shape)


def prepare_kernel(tracers, levels, rows, columns, *refs):
    prepare(tracers, levels, rows, columns, refs[:-5], *refs[-5:])


def forcing_kernel(steps, tracers, levels, rows, columns, *refs):
    if len(refs) > 4:
        out, terms, right, keys = refs[-6:-2]
        prepare(tracers, levels, rows, columns, refs[:-6], terms, right, keys, *refs[-2:])
    else:
        terms, right, keys, out = refs
    first, _ = window(STEPS - 1, levels)
    batch = keys.shape[1]
    ids = lax.broadcasted_iota(jnp.int32, (8, batch), 0).astype(F32)
    for i, now in enumerate(steps):
        begin, size = window(STEPS - 1 - now, levels)
        last = now % WIDTH == WIDTH - 1 and 2 * rows == 8
        if last and now - WIDTH in steps:
            continue
        mate = now + WIDTH if last and now + WIDTH in steps else None
        wanted = ids + now * 8.0
        if mate is not None:
            wanted = jnp.where(ids < rows, wanted, ids - rows + mate * 8.0)
        hit = jnp.where(keys[...] == wanted, 1.0, 0.0)
        mask = jnp.concatenate([hit, hit], axis=0).astype(BF16)
        pick = pl.ds((begin - first) * tracers, size * tracers)
        left = (terms[pick] * mask[None]).reshape(size * tracers * 16, batch)
        product = lax.dot_general(
            left, right[...], (((1,), (1,)), ((), ())), preferred_element_type=F32
        )
        for l in range(size):
            for t in range(tracers):
                base = (l * tracers + t) * 16
                value = product[base : base + 8] + product[base + 8 : base + 16]
                places = [((i, t, begin + l), value)]
                if mate is not None:
                    places.append(((steps.index(mate), t, begin + l), pltpu.roll(value, rows, 0)))
                for place, part in places:
                    if pl.num_programs(0) == 1:
                        out[place] = part
                    else:
                        out[place] = jnp.where(pl.program_id(0) == 0, 0.0, out[place]) + part


def per_device(
    final_adjoint,
    lon_courant,
    lat_courant,
    upwind_flags,
    vertical_mixing,
    level_profile,
    sounding_owner,
    sounding_target,
    misfit,
    averaging_kernel,
):
    tracers, levels, rows, columns = final_adjoint.shape
    held = misfit.shape[1]
    bands, subs, tiles = (lax.axis_size(name) for name in ("levels", "sub", "tiles"))
    planes = tracers + 5
    lanes = -(-(columns + 2 * STEPS) // LANES) * LANES
    wide = window(STEPS, levels)[1]
    moves = functools.partial(level_moves, levels)
    number = len(moves())
    shape = lambda *dims: jax.ShapeDtypeStruct(dims, F32)
    sub_pairs = [(i, (i + 1) % subs) for i in range(subs)]

    def call(body, limit, flops=0, **kwargs):
        return pl.pallas_call(
            body,
            compiler_params=pltpu.CompilerParams(vmem_limit_bytes=int(limit * MIB)),
            cost_estimate=pl.CostEstimate(flops=flops, bytes_accessed=MIB, transcendentals=0),
            **kwargs,
        )

    def room(*arrays):
        return [pltpu.VMEM(x.shape, x.dtype) for x in arrays]

    beside = [lax.ppermute(averaging_kernel, "levels", pairs) for pairs, _, _ in moves()]
    fields = (final_adjoint, lon_courant, lat_courant, upwind_flags, vertical_mixing)
    fields += (misfit, averaging_kernel, sounding_owner.reshape(1, held), sounding_target)
    groups = -(-(tracers + 2 + wide) // 4)
    flat_rows = -(-groups // 2) * 8
    own, edge, payload = call(
        functools.partial(edges_kernel, moves),
        60,
        out_shape=[shape(planes, levels, rows, lanes), shape(planes, levels, rows, LANES)]
        + [shape(flat_rows, held)],
        in_specs=[HBM] * 9,
        out_specs=[VMEM] * 3,
        scratch_shapes=room(*fields)
        + [pltpu.VMEM((planes, levels, 8, lanes), F32), pltpu.SemaphoreType.DMA((9,))],
        name="edges",
    )(*fields)
    edge = lax.ppermute(edge, "sub", sub_pairs)
    swapped = lax.ppermute(payload, "sub", sub_pairs)
    own, payload = call(
        stage_kernel,
        8,
        flops=10**9,
        out_shape=[shape(*own.shape), shape(*payload.shape)],
        in_specs=[VMEM] * 2,
        out_specs=[VMEM] * 2,
        name="stage",
    )(own, payload)
    edge, beside, swapped, own, payload = lax.optimization_barrier((edge, beside, swapped, own, payload))
    crossed = [lax.ppermute(part, "sub", sub_pairs) for part in beside]
    depth = tracers + 5 + (tracers + 3) // 2
    body, first, second, *parts = call(
        functools.partial(spread_kernel, moves, columns),
        8,
        out_shape=[shape(planes, levels, rows, lanes)]
        + [shape(depth, levels, 2, lanes)] * 2
        + [shape(planes, STEPS, rows, lanes)] * number,
        in_specs=[VMEM] * 2,
        out_specs=[VMEM] * (3 + number),
        name="spread",
    )(own, edge)
    parts = [lax.ppermute(part, "levels", pairs) for part, (pairs, _, _) in zip(parts, moves())]
    both = call(
        functools.partial(payload_kernel, number, levels, tracers),
        8,
        out_shape=shape(2, groups, 4, held),
        in_specs=[VMEM] * (2 + 2 * number),
        out_specs=VMEM,
        scratch_shapes=[pltpu.VMEM((flat_rows, held), F32)],
        name="payload",
    )(payload, *beside, swapped, *crossed)
    if tiles == 4:
        got = [both] + [lax.ppermute(both, "tiles", [(i, i ^ k) for i in range(tiles)]) for k in (1, 2, 3)]
    else:
        got = [lax.all_gather(both, "tiles", tiled=True)]

    blocks = [body, swap_tiles(first, 0), swap_tiles(second, 1)]

    held_here = got[0].shape[0]
    sources = held_here if len(got) > 1 else max(1, min(held_here, CHUNK // held))
    batch = sources * len(got) * held
    count = window(STEPS - 1, levels)[1] * tracers
    sizes = (tracers, levels, rows, columns)
    prepared = [((count, 16, batch), BF16), ((lanes, batch), BF16), ((8, batch), F32)]
    working = [pltpu.VMEM((flat_rows, batch), F32), pltpu.VMEM((2, tracers, flat_rows, batch), F32)]
    if held_here == sources:
        got = call(
            functools.partial(prepare_kernel, *sizes),
            16,
            out_shape=[jax.ShapeDtypeStruct(*x) for x in prepared],
            in_specs=[VMEM] * len(got),
            out_specs=[VMEM] * 3,
            scratch_shapes=working,
            name="prepare",
        )(*got)
        parts, got = lax.optimization_barrier((parts, got))
    if number:
        far = call(
            functools.partial(far_kernel, number),
            8,
            out_shape=[shape(depth, STEPS, 2, lanes)] * (2 * number),
            in_specs=[VMEM] * number,
            out_specs=[VMEM] * (2 * number),
            name="far",
        )(*parts)
    for i in range(number):
        blocks += [parts[i], swap_tiles(far[2 * i], 0), swap_tiles(far[2 * i + 1], 1)]

    def forcing_of(steps):
        force_shape = (len(steps), tracers, wide, 8, lanes)
        scratch = []
        block = pl.BlockSpec((sources, groups, 4, held), lambda i: (i, 0, 0, 0))
        specs, limit = [block], 60
        if len(got) == 3:
            specs = [pl.BlockSpec(x.shape, lambda i, rank=x.ndim: (0,) * rank) for x in got]
            limit = 24
        else:
            scratch += [pltpu.VMEM(*x) for x in prepared] + working
        return call(
            functools.partial(forcing_kernel, steps, *sizes),
            limit,
            flops=2 * len(steps) * count * 16 * batch * lanes,
            out_shape=shape(*force_shape),
            grid=(held_here // sources,),
            in_specs=specs,
            out_specs=pl.BlockSpec(force_shape, lambda i: (0, 0, 0, 0, 0)),
            scratch_shapes=scratch,
            name="forcing" + str(steps[0]),
        )(*got)

    forcings = [forcing_of(steps) for steps in FORCED]
    state_shape = (tracers, wide + 2, 8, lanes)
    coef_shape = (6, wide + 2, 8, lanes)
    flux_shape = (tracers, 8, lanes)

    def messages(round_id):
        count = window(STEPS - round_id * WIDTH, levels)[1]
        return [shape(tracers + (tracers + 1) // 2, count, 2, lanes)] * 2

    scratch = [pltpu.VMEM(state_shape, F32)] * 3
    state, coef, flux, first, second = call(
        functools.partial(first_kernel, moves, levels),
        16,
        out_shape=[shape(*state_shape), shape(*coef_shape), shape(*flux_shape), *messages(1)],
        in_specs=[VMEM] * (len(blocks) + len(forced_in(0))) + [SMEM],
        out_specs=[VMEM] * 5,
        scratch_shapes=scratch + [pltpu.VMEM((7, wide + 2, 8, lanes), F32)],
        name="round0",
    )(*blocks, *[forcings[i] for i in forced_in(0)], level_profile)
    half = rows // 2 if bands == 2 else rows
    for round_id in range(1, ROUNDS):
        first, second = swap_tiles(first, 0), swap_tiles(second, 1)
        if round_id < ROUNDS - 1:
            outs = [shape(*state_shape), shape(*flux_shape), *messages(round_id + 1)]
            extra = []
        else:
            part = shape(tracers, half, columns)
            outs = [shape(tracers, levels, rows, columns), part, part]
            extra = [pltpu.VMEM(flux_shape, F32)]
        results = call(
            functools.partial(next_kernel, round_id, levels, rows),
            16,
            out_shape=outs,
            in_specs=[VMEM] * (4 + len(forced_in(round_id))) + [SMEM, VMEM],
            out_specs=[VMEM] * len(outs),
            scratch_shapes=extra + scratch,
            name="round" + str(round_id),
        )(state, coef, first, second, *[forcings[i] for i in forced_in(round_id)], level_profile, flux)
        if round_id < ROUNDS - 1:
            state, flux, first, second = results
    adjoint, keep, give = results
    if bands == 2:
        flux_gradient = keep + lax.ppermute(give, "levels", [(0, 1), (1, 0)])
    else:
        flux_gradient = lax.psum_scatter(keep, "levels", scatter_dimension=1, tiled=True)
    return adjoint, flux_gradient


def solution(mesh):
    return jax.shard_map(
        per_device,
        mesh=mesh,
        in_specs=(
            P("groups", "levels", "tiles", "sub"),
            P(("groups", "levels"), "tiles", "sub"),
            P(("groups", "levels"), "tiles", "sub"),
            P(None, ("groups", "levels"), "tiles", "sub"),
            P(("groups", "levels"), "tiles", "sub"),
            P("levels"),
            P(("groups", "tiles", "sub"), None),
            P(("groups", "tiles", "sub")),
            P(None, ("groups", "tiles", "sub")),
            P("levels", ("groups", "tiles", "sub")),
        ),
        out_specs=(P("groups", "levels", "tiles", "sub"), P("groups", ("tiles", "levels"), "sub")),
        check_vma=False,
    )
```

```python
import functools

import jax
import jax.numpy as jnp
from jax import lax
from jax.experimental import pallas as pl
from jax.experimental.pallas import tpu as pltpu
from jax.sharding import PartitionSpec as P

STEPS = 6
WIDTH = 3
FORCED = ((0, 1, 2, 5), (3, 4))
ROUNDS = STEPS // WIDTH
LANES = 128
CHUNK = 3072
F32 = jnp.float32
BF16 = jnp.bfloat16
VMEM = pl.BlockSpec(memory_space=pltpu.VMEM)
SMEM = pl.BlockSpec(memory_space=pltpu.SMEM)
HBM = pl.BlockSpec(memory_space=pltpu.HBM)
MIB = 1024 * 1024


def window(margin, levels):
    count = lax.axis_size("levels")
    if count == 1:
        return 0, levels
    if count == 2:
        return lax.axis_index("levels") * (STEPS - margin), levels + margin
    return STEPS - margin, levels + 2 * margin


def level_moves(levels):
    count = lax.axis_size("levels")
    band = lax.axis_index("levels")
    if count == 1:
        return []
    if count == 2:
        return [([(0, 1), (1, 0)], (levels - STEPS) * (1 - band), levels * (1 - band))]
    up = [(i, i + 1) for i in range(count - 1)]
    down = [(i + 1, i) for i in range(count - 1)]
    return [(up, levels - STEPS, 0), (down, 0, STEPS + levels)]


def swap_tiles(value, odd):
    tiles = lax.axis_size("tiles")
    pairs = []
    for low in range(odd, tiles - 1, 2):
        pairs += [(low, low + 1), (low + 1, low)]
    return lax.ppermute(value, "tiles", pairs)


def is_even():
    return lax.rem(lax.axis_index("tiles"), 2) == 0


def own_planes(adj, lon, lat, flags, mix):
    tracers, levels, rows, _ = adj.shape
    last_band = lax.axis_index("levels") == lax.axis_size("levels") - 1
    last_tile = lax.axis_index("tiles") == lax.axis_size("tiles") - 1
    shape = lon.shape
    level_ids = lax.broadcasted_iota(jnp.int32, shape, 0)
    row_ids = lax.broadcasted_iota(jnp.int32, shape, 1)
    top = (level_ids == levels - 1) & last_band
    shut = (row_ids == rows - 1) & last_tile
    first = flags[0].astype(F32)
    second = flags[1].astype(F32)
    lat_open = jnp.where(shut, 0.0, lat[...])
    planes = [adj[t] for t in range(tracers)]
    planes.append(jnp.where(top, 0.0, mix[...]))
    planes.append(lon[...] * first)
    planes.append(lon[...] * (1.0 - first))
    planes.append(lat_open * second)
    planes.append(lat_open * (1.0 - second))
    return planes


def fetch(sources, targets, sems):
    copies = [pltpu.make_async_copy(x, y, sems.at[i]) for i, (x, y) in enumerate(zip(sources, targets))]
    for copy in copies:
        copy.start()
    for copy in copies:
        copy.wait()


def soundings_of(number, flat, misfit, kernel, owner, target):
    tracers, levels = misfit.shape[0], kernel.shape[0]
    base = tracers + 2
    flat[...] = jnp.zeros_like(flat)
    flat[0:tracers] = misfit[...]
    flat[tracers : tracers + 1] = owner[...].astype(F32)
    flat[tracers + 1 : base] = target[...].astype(F32).reshape(1, target.shape[0])
    if number == 1:

        @pl.when(lax.axis_index("levels") == 0)
        def _():
            flat[base : base + levels] = kernel[...]

        @pl.when(lax.axis_index("levels") == 1)
        def _():
            flat[base + STEPS : base + STEPS + levels] = kernel[...]
    else:
        start = base + (STEPS if number else 0)
        flat[start : start + levels] = kernel[...]


def edges_kernel(moves, *refs):
    inputs, own_out, edge_out, base = refs[:9], refs[9], refs[10], refs[11]
    held, buf, sems = refs[-11:-2], refs[-2], refs[-1]
    fetch(inputs, held, sems)
    soundings_of(len(moves()), base, *held[5:])
    held = held[:5]
    _, levels, rows, columns = held[0].shape
    width = edge_out.shape[-1]
    tail = columns // LANES * LANES
    gap = columns - tail
    buf[...] = jnp.zeros_like(buf)
    for p, plane in enumerate(own_planes(*held)):
        buf[p, :, 0:rows, 0:columns] = plane
    own_out[...] = buf[:, :, 0:rows, :]
    lane = lax.broadcasted_iota(jnp.int32, (8, LANES), 1)
    for p in range(buf.shape[0]):
        for l in range(levels):
            start = pltpu.roll(buf[p, l, :, 0:LANES], gap, 1)
            end = pltpu.roll(buf[p, l, :, tail : tail + LANES], width - gap, 1)
            both = jnp.where(
                lane >= width - STEPS,
                end,
                jnp.where((lane >= gap) & (lane < gap + STEPS), start, 0.0),
            )
            edge_out[p, l] = both[0:rows]

def payload_kernel(number, levels, tracers, *refs):
    out, flat = refs[-2:]
    base = tracers + 2
    for half in range(2):
        part = refs[half * (1 + number) : (half + 1) * (1 + number)]
        flat[...] = part[0][...]
        if number == 1:

            @pl.when(lax.axis_index("levels") == 0)
            def _(part=part):
                flat[base + levels : base + levels + STEPS] = part[1][0:STEPS]

            @pl.when(lax.axis_index("levels") == 1)
            def _(part=part):
                flat[base : base + STEPS] = part[1][levels - STEPS : levels]

        if number == 2:
            flat[base : base + STEPS] = part[1][levels - STEPS : levels]
            flat[base + STEPS + levels : base + 2 * STEPS + levels] = part[2][0:STEPS]
        for group in range(out.shape[1]):
            out[half, group] = flat[4 * group : 4 * group + 4]


def with_edges(plane, edge, columns):
    tail = columns // LANES * LANES
    lane = lax.broadcasted_iota(jnp.int32, plane.shape[:-1] + (LANES,), 2)
    return jnp.where(lane < columns - tail, plane[..., tail : tail + LANES], edge)


def tile_messages(body, first_out, second_out):
    planes, _, rows, _ = body.shape
    tracers = planes - 5
    mixing, east, west, north, south = range(tracers, planes)

    def rows_of(out, first, third):
        near = list(range(tracers)) + [mixing, north, south, east, west]
        for entry, p in enumerate(near):
            out[entry] = body[p, :, first : first + 2, :]
        for k, p in enumerate(list(range(tracers)) + [mixing, south, south]):
            half = slice(k % 2, k % 2 + 1)
            out[len(near) + k // 2, :, half, :] = body[p, :, third : third + 1, :]

    @pl.when(is_even())
    def _():
        rows_of(first_out, rows - 2, rows - 3)
        rows_of(second_out, 0, 2)

    @pl.when(jnp.logical_not(is_even()))
    def _():
        rows_of(first_out, 0, 2)
        rows_of(second_out, rows - 2, rows - 3)


def spread_kernel(moves, columns, own, edge, body, first_out, second_out, *outs):
    tail = columns // LANES * LANES
    body[:, :, :, 0:tail] = own[:, :, :, 0:tail]
    for p in range(own.shape[0]):
        body[p, :, :, tail : tail + LANES] = with_edges(own[p], edge[p], columns)
    for out, (_, start, _) in zip(outs, moves()):
        out[...] = body[:, pl.ds(start, STEPS)]
    tile_messages(body, first_out, second_out)


def stage_kernel(own, payload, own_out, payload_out):
    own_out[...] = own[...]
    payload_out[...] = payload[...]


def far_kernel(number, *refs):
    for i in range(number):
        tile_messages(refs[i], refs[number + 2 * i], refs[number + 2 * i + 1])


def advance(step, src, dst, outer, coef, forcing, profile, flux, levels):
    tracers = src.shape[0]
    first, count = window(STEPS - 1 - step, levels)
    own, _ = window(0, levels)
    lanes = src.shape[-1]
    ids = lax.broadcasted_iota(jnp.int32, src.shape[-2:], 0)
    force, index = forcing(step)
    total = [flux[t] for t in range(tracers)]
    for i in range(count):
        at = first + i
        up, down = coef[0, at + 1], coef[0, at]
        east, west, north, south = (coef[c, at + 1] for c in range(1, 5))
        if outer is not None:
            up_outer, down_outer = coef[5, at + 1], coef[5, at]
            stay_outer = 1.0 - up_outer - down_outer
        stay = 1.0 - up - down
        keep = 1.0 - east - west - north - south
        own_id = at - own
        inside = (own_id >= 0) & (own_id < levels)
        weight = jnp.where(inside, profile[jnp.clip(own_id, 0, levels - 1)], 0.0)
        for t in range(tracers):
            a = src[t, at + 1]
            b = stay * a + up * src[t, at + 2] + down * src[t, at]
            moved = keep * b + east * pltpu.roll(b, lanes - 1, 1) + west * pltpu.roll(b, 1, 1)
            above, below = pltpu.roll(b, 7, 0), pltpu.roll(b, 1, 0)
            if outer is not None:
                a = outer[t, at + 1]
                b_outer = stay_outer * a + up_outer * outer[t, at + 2] + down_outer * outer[t, at]
                above = jnp.where(ids == 5, b_outer, above)
                below = jnp.where(ids == 6, b_outer, below)
            moved = moved + north * above + south * below
            new = moved + force[index, t, at]
            dst[t, at + 1] = new
            total[t] = total[t] + weight * new
    for t in range(tracers):
        flux[t] = total[t]


def clear_pads(ref):
    levels = ref.shape[1]
    ref[:, 0:1] = jnp.zeros((ref.shape[0], 1) + ref.shape[2:], F32)
    ref[:, levels - 1 : levels] = jnp.zeros((ref.shape[0], 1) + ref.shape[2:], F32)


def forced_in(number):
    return [i for i, steps in enumerate(FORCED) if any(step // WIDTH == number for step in steps)]


def run_steps(number, work, other, outer, coef, forcings, profile, flux, levels):
    def forcing(step):
        for i, ref in zip(forced_in(number), forcings):
            if step in FORCED[i]:
                return ref, FORCED[i].index(step)

    refs = [work, other]
    for i in range(WIDTH):
        extra = outer if i == 0 else None
        advance(number * WIDTH + i, refs[i % 2], refs[(i + 1) % 2], extra, coef, forcing, profile, flux, levels)
    return refs[WIDTH % 2]


def send_rows(number, state, first_out, second_out, rows, levels):
    start, count = window(STEPS - (number + 1) * WIDTH, levels)
    pick = pl.ds(start + 1, count)
    tracers = state.shape[0]
    even = is_even()
    for t in range(tracers):
        upper, lower = state[t, pick, rows - 2 : rows, :], state[t, pick, 0:2, :]
        first_out[t] = jnp.where(even, upper, lower)
        second_out[t] = jnp.where(even, lower, upper)
        upper, lower = state[t, pick, rows - 3 : rows - 2, :], state[t, pick, 2:3, :]
        entry, half = tracers + t // 2, slice(t % 2, t % 2 + 1)
        first_out[entry, :, half, :] = jnp.where(even, upper, lower)
        second_out[entry, :, half, :] = jnp.where(even, lower, upper)


def place_outer(ref, plane, pick, first, second, entry, half):
    even = is_even()
    one, two = first[entry, :, half : half + 1, :], second[entry, :, half : half + 1, :]
    ref[plane, pick, 5:6, :] = jnp.where(even, one, two)
    ref[plane, pick, 6:7, :] = jnp.where(even, two, one)


def first_kernel(moves, levels, *refs):
    number = len(moves())
    groups = [refs[3 * i : 3 * i + 3] for i in range(1 + number)]
    refs = refs[3 * (1 + number) :]
    count = len(forced_in(0))
    forcings, profile = refs[:count], refs[count]
    state_out, coef_out, flux, first_out, second_out, work, outer, raw = refs[count + 1 :]
    planes, _, rows, lanes = groups[0][0].shape
    tracers = planes - 5
    mixing, east, west, north, south = range(tracers, planes)
    raw[...] = jnp.zeros_like(raw)
    flux[...] = jnp.zeros_like(flux)
    clear_pads(work)
    clear_pads(state_out)
    clear_pads(outer)
    even = is_even()
    starts = [window(0, levels)[0]] + [slot for _, _, slot in moves()]
    for (body, first, second), start in zip(groups, starts):
        pick = pl.ds(start + 1, body.shape[1])
        for p in range(planes):
            ref, plane = (work, p) if p < tracers else (raw, p - tracers)
            ref[plane, pick, 0:rows, :] = body[p]
        near = list(range(tracers)) + [mixing, north, south, east, west]
        for entry, p in enumerate(near):
            ref, plane = (work, p) if p < tracers else (raw, p - tracers)
            ref[plane, pick, rows : rows + 2, :] = jnp.where(even, first[entry], second[entry])
            ref[plane, pick, 6:8, :] = jnp.where(even, second[entry], first[entry])
        for k in range(tracers):
            place_outer(outer, k, pick, first, second, len(near) + k // 2, k % 2)
        for plane, k in ((5, tracers), (6, tracers + 1)):
            place_outer(raw, plane, pick, first, second, len(near) + k // 2, k % 2)
    coef_out[0] = raw[0]
    coef_out[1] = raw[1]
    coef_out[3] = raw[3]
    coef_out[5] = raw[5]
    ids = lax.broadcasted_iota(jnp.int32, (8, lanes), 0)
    for l in range(raw.shape[1]):
        coef_out[2, l] = pltpu.roll(raw[2, l], 1, 1)
        coef_out[4, l] = jnp.where(ids == 6, raw[6, l], pltpu.roll(raw[4, l], 1, 0))
    run_steps(0, work, state_out, outer, coef_out, forcings, profile, flux, levels)
    send_rows(0, state_out, first_out, second_out, rows, levels)


def next_kernel(number, levels, rows, state, coef, first, second, *refs):
    count = len(forced_in(number))
    forcings, profile, flux_in = refs[:count], refs[count], refs[count + 1]
    refs = refs[count + 2 :]
    work, other, outer = refs[-3:]
    start, size = window(STEPS - number * WIDTH, levels)
    pick = pl.ds(start + 1, size)
    even = is_even()
    tracers = state.shape[0]
    work[...] = state[...]
    for t in range(tracers):
        work[t, pick, rows : rows + 2, :] = jnp.where(even, first[t], second[t])
        work[t, pick, 6:8, :] = jnp.where(even, second[t], first[t])
    clear_pads(other)
    clear_pads(outer)
    for t in range(tracers):
        place_outer(outer, t, pick, first, second, tracers + t // 2, t % 2)
    if number < ROUNDS - 1:
        state_out, flux, first_out, second_out = refs[:-3]
        flux[...] = flux_in[...]
        last = run_steps(number, work, other, outer, coef, forcings, profile, flux, levels)
        state_out[...] = last[...]
        send_rows(number, state_out, first_out, second_out, rows, levels)
        return
    adjoint, keep, give, flux = refs[:-3]
    flux[...] = flux_in[...]
    last = run_steps(number, work, other, outer, coef, forcings, profile, flux, levels)
    own, _ = window(0, levels)
    columns = adjoint.shape[-1]
    adjoint[...] = last[:, pl.ds(own + 1, levels), 0:rows, 0:columns]
    if lax.axis_size("levels") == 2:
        half = rows // 2
        upper = lax.axis_index("levels") == 1
        low, high = flux[:, 0:half, 0:columns], flux[:, half:rows, 0:columns]
        keep[...] = jnp.where(upper, high, low)
        give[...] = jnp.where(upper, low, high)
    else:
        keep[...] = flux[:, 0:rows, 0:columns]
        give[...] = jnp.zeros_like(give)


def prepare(tracers, levels, rows, columns, got, terms, right, keys, flat, parts):
    sources, groups, _, held = got[0].shape
    lanes = right.shape[0]
    subs = lax.axis_size("sub")
    tile, sub = lax.axis_index("tiles"), lax.axis_index("sub")
    for s in range(sources * len(got)):
        ref = got[s // sources]
        for group in range(groups):
            flat[4 * group : 4 * group + 4, s * held : (s + 1) * held] = ref[s % sources, group]
    owner = flat[tracers : tracers + 1, :]
    target = flat[tracers + 1 : tracers + 2, :]
    cells = rows * columns
    step = jnp.floor((target + 0.5) * (1.0 / cells))
    cell = target - step * cells
    row = jnp.floor((cell + 0.5) * (1.0 / columns))
    col = cell - row * columns
    owner_tile = jnp.floor((owner + 0.5) * (1.0 / subs))
    row = row + (owner_tile - tile.astype(F32)) * rows
    shift = owner - owner_tile * subs - sub.astype(F32)
    col = col + jnp.where(shift < 0, shift + subs, shift) * columns
    east_side = col < columns + STEPS
    west_side = col >= subs * columns - STEPS
    lane = jnp.where(east_side, col, jnp.where(west_side, col - subs * columns + lanes, -1.0))
    close = (row >= 1 - WIDTH) & (row <= rows + WIDTH - 2)
    key = jnp.where(close, step * 8 + jnp.where(row < 0, row + 8, row), -1.0)
    for start in range(0, lanes, LANES):
        ids = lax.broadcasted_iota(jnp.int32, (LANES, lane.shape[1]), 0).astype(F32) + start
        right[start : start + LANES] = jnp.where(ids == lane, 1.0, 0.0).astype(BF16)
    for t in range(tracers):
        value = flat[...] * flat[t : t + 1, :]
        high = value.astype(BF16).astype(F32)
        parts[0, t] = high
        parts[1, t] = value - high
    first, count = window(STEPS - 1, levels)
    batch = flat.shape[1]
    for i in range(count):
        for t in range(tracers):
            row_id = pl.ds(tracers + 2 + first + i, 1)
            both = [jnp.broadcast_to(parts[k, t, row_id, :], (8, batch)) for k in range(2)]
            terms[i * tracers + t] = jnp.concatenate(both, axis=0).astype(BF16)
    keys[...] = jnp.broadcast_to(key, keys.shape)


def prepare_kernel(tracers, levels, rows, columns, *refs):
    prepare(tracers, levels, rows, columns, refs[:-5], *refs[-5:])


def forcing_kernel(steps, tracers, levels, rows, columns, *refs):
    if len(refs) > 4:
        out, terms, right, keys = refs[-6:-2]
        prepare(tracers, levels, rows, columns, refs[:-6], terms, right, keys, *refs[-2:])
    else:
        terms, right, keys, out = refs
    first, _ = window(STEPS - 1, levels)
    batch = keys.shape[1]
    ids = lax.broadcasted_iota(jnp.int32, (8, batch), 0).astype(F32)
    for i, now in enumerate(steps):
        begin, size = window(STEPS - 1 - now, levels)
        last = now % WIDTH == WIDTH - 1 and 2 * rows == 8
        if last and now - WIDTH in steps:
            continue
        mate = now + WIDTH if last and now + WIDTH in steps else None
        wanted = ids + now * 8.0
        if mate is not None:
            wanted = jnp.where(ids < rows, wanted, ids - rows + mate * 8.0)
        hit = jnp.where(keys[...] == wanted, 1.0, 0.0)
        mask = jnp.concatenate([hit, hit], axis=0).astype(BF16)
        pick = pl.ds((begin - first) * tracers, size * tracers)
        left = (terms[pick] * mask[None]).reshape(size * tracers * 16, batch)
        product = lax.dot_general(
            left, right[...], (((1,), (1,)), ((), ())), preferred_element_type=F32
        )
        for l in range(size):
            for t in range(tracers):
                base = (l * tracers + t) * 16
                value = product[base : base + 8] + product[base + 8 : base + 16]
                places = [((i, t, begin + l), value)]
                if mate is not None:
                    places.append(((steps.index(mate), t, begin + l), pltpu.roll(value, rows, 0)))
                for place, part in places:
                    if pl.num_programs(0) == 1:
                        out[place] = part
                    else:
                        out[place] = jnp.where(pl.program_id(0) == 0, 0.0, out[place]) + part


def per_device(
    final_adjoint,
    lon_courant,
    lat_courant,
    upwind_flags,
    vertical_mixing,
    level_profile,
    sounding_owner,
    sounding_target,
    misfit,
    averaging_kernel,
):
    tracers, levels, rows, columns = final_adjoint.shape
    held = misfit.shape[1]
    bands, subs, tiles = (lax.axis_size(name) for name in ("levels", "sub", "tiles"))
    planes = tracers + 5
    lanes = -(-(columns + 2 * STEPS) // LANES) * LANES
    wide = window(STEPS, levels)[1]
    moves = functools.partial(level_moves, levels)
    number = len(moves())
    shape = lambda *dims: jax.ShapeDtypeStruct(dims, F32)
    sub_pairs = [(i, (i + 1) % subs) for i in range(subs)]

    def call(body, limit, flops=0, **kwargs):
        return pl.pallas_call(
            body,
            compiler_params=pltpu.CompilerParams(vmem_limit_bytes=int(limit * MIB)),
            cost_estimate=pl.CostEstimate(flops=flops, bytes_accessed=MIB, transcendentals=0),
            **kwargs,
        )

    def room(*arrays):
        return [pltpu.VMEM(x.shape, x.dtype) for x in arrays]

    beside = [lax.ppermute(averaging_kernel, "levels", pairs) for pairs, _, _ in moves()]
    fields = (final_adjoint, lon_courant, lat_courant, upwind_flags, vertical_mixing)
    fields += (misfit, averaging_kernel, sounding_owner.reshape(1, held), sounding_target)
    groups = -(-(tracers + 2 + wide) // 4)
    flat_rows = -(-groups // 2) * 8
    own, edge, payload = call(
        functools.partial(edges_kernel, moves),
        60,
        out_shape=[shape(planes, levels, rows, lanes), shape(planes, levels, rows, LANES)]
        + [shape(flat_rows, held)],
        in_specs=[HBM] * 9,
        out_specs=[VMEM] * 3,
        scratch_shapes=room(*fields)
        + [pltpu.VMEM((planes, levels, 8, lanes), F32), pltpu.SemaphoreType.DMA((9,))],
        name="edges",
    )(*fields)
    edge = lax.ppermute(edge, "sub", sub_pairs)
    swapped = lax.ppermute(payload, "sub", sub_pairs)
    own, payload = call(
        stage_kernel,
        8,
        flops=10**9,
        out_shape=[shape(*own.shape), shape(*payload.shape)],
        in_specs=[VMEM] * 2,
        out_specs=[VMEM] * 2,
        name="stage",
    )(own, payload)
    edge, beside, swapped, own, payload = lax.optimization_barrier((edge, beside, swapped, own, payload))
    crossed = [lax.ppermute(part, "sub", sub_pairs) for part in beside]
    depth = tracers + 5 + (tracers + 3) // 2
    body, first, second, *parts = call(
        functools.partial(spread_kernel, moves, columns),
        8,
        out_shape=[shape(planes, levels, rows, lanes)]
        + [shape(depth, levels, 2, lanes)] * 2
        + [shape(planes, STEPS, rows, lanes)] * number,
        in_specs=[VMEM] * 2,
        out_specs=[VMEM] * (3 + number),
        name="spread",
    )(own, edge)
    parts = [lax.ppermute(part, "levels", pairs) for part, (pairs, _, _) in zip(parts, moves())]
    both = call(
        functools.partial(payload_kernel, number, levels, tracers),
        8,
        out_shape=shape(2, groups, 4, held),
        in_specs=[VMEM] * (2 + 2 * number),
        out_specs=VMEM,
        scratch_shapes=[pltpu.VMEM((flat_rows, held), F32)],
        name="payload",
    )(payload, *beside, swapped, *crossed)
    if tiles == 4:
        got = [both] + [lax.ppermute(both, "tiles", [(i, i ^ k) for i in range(tiles)]) for k in (1, 2, 3)]
    else:
        got = [lax.all_gather(both, "tiles", tiled=True)]

    blocks = [body, swap_tiles(first, 0), swap_tiles(second, 1)]

    held_here = got[0].shape[0]
    sources = held_here if len(got) > 1 else max(1, min(held_here, CHUNK // held))
    batch = sources * len(got) * held
    count = window(STEPS - 1, levels)[1] * tracers
    sizes = (tracers, levels, rows, columns)
    prepared = [((count, 16, batch), BF16), ((lanes, batch), BF16), ((8, batch), F32)]
    working = [pltpu.VMEM((flat_rows, batch), F32), pltpu.VMEM((2, tracers, flat_rows, batch), F32)]
    if held_here == sources:
        got = call(
            functools.partial(prepare_kernel, *sizes),
            16,
            out_shape=[jax.ShapeDtypeStruct(*x) for x in prepared],
            in_specs=[VMEM] * len(got),
            out_specs=[VMEM] * 3,
            scratch_shapes=working,
            name="prepare",
        )(*got)
        parts, got = lax.optimization_barrier((parts, got))
    if number:
        far = call(
            functools.partial(far_kernel, number),
            8,
            out_shape=[shape(depth, STEPS, 2, lanes)] * (2 * number),
            in_specs=[VMEM] * number,
            out_specs=[VMEM] * (2 * number),
            name="far",
        )(*parts)
    for i in range(number):
        blocks += [parts[i], swap_tiles(far[2 * i], 0), swap_tiles(far[2 * i + 1], 1)]

    def forcing_of(steps):
        force_shape = (len(steps), tracers, wide, 8, lanes)
        scratch = []
        block = pl.BlockSpec((sources, groups, 4, held), lambda i: (i, 0, 0, 0))
        specs, limit = [block], 60
        if len(got) == 3:
            specs = [pl.BlockSpec(x.shape, lambda i, rank=x.ndim: (0,) * rank) for x in got]
            limit = 24
        else:
            scratch += [pltpu.VMEM(*x) for x in prepared] + working
        return call(
            functools.partial(forcing_kernel, steps, *sizes),
            limit,
            flops=2 * len(steps) * count * 16 * batch * lanes,
            out_shape=shape(*force_shape),
            grid=(held_here // sources,),
            in_specs=specs,
            out_specs=pl.BlockSpec(force_shape, lambda i: (0, 0, 0, 0, 0)),
            scratch_shapes=scratch,
            name="forcing" + str(steps[0]),
        )(*got)

    forcings = [forcing_of(steps) for steps in FORCED]
    state_shape = (tracers, wide + 2, 8, lanes)
    coef_shape = (6, wide + 2, 8, lanes)
    flux_shape = (tracers, 8, lanes)

    def messages(round_id):
        count = window(STEPS - round_id * WIDTH, levels)[1]
        return [shape(tracers + (tracers + 1) // 2, count, 2, lanes)] * 2

    scratch = [pltpu.VMEM(state_shape, F32)] * 3
    state, coef, flux, first, second = call(
        functools.partial(first_kernel, moves, levels),
        16,
        out_shape=[shape(*state_shape), shape(*coef_shape), shape(*flux_shape), *messages(1)],
        in_specs=[VMEM] * (len(blocks) + len(forced_in(0))) + [SMEM],
        out_specs=[VMEM] * 5,
        scratch_shapes=scratch[:2] + [pltpu.VMEM((7, wide + 2, 8, lanes), F32)],
        name="round0",
    )(*blocks, *[forcings[i] for i in forced_in(0)], level_profile)
    half = rows // 2 if bands == 2 else rows
    for round_id in range(1, ROUNDS):
        first, second = swap_tiles(first, 0), swap_tiles(second, 1)
        if round_id < ROUNDS - 1:
            outs = [shape(*state_shape), shape(*flux_shape), *messages(round_id + 1)]
            extra = []
        else:
            part = shape(tracers, half, columns)
            outs = [shape(tracers, levels, rows, columns), part, part]
            extra = [pltpu.VMEM(flux_shape, F32)]
        results = call(
            functools.partial(next_kernel, round_id, levels, rows),
            16,
            out_shape=outs,
            in_specs=[VMEM] * (4 + len(forced_in(round_id))) + [SMEM, VMEM],
            out_specs=[VMEM] * len(outs),
            scratch_shapes=extra + scratch,
            name="round" + str(round_id),
        )(state, coef, first, second, *[forcings[i] for i in forced_in(round_id)], level_profile, flux)
        if round_id < ROUNDS - 1:
            state, flux, first, second = results
    adjoint, keep, give = results
    if bands == 2:
        flux_gradient = keep + lax.ppermute(give, "levels", [(0, 1), (1, 0)])
    else:
        flux_gradient = lax.psum_scatter(keep, "levels", scatter_dimension=1, tiled=True)
    return adjoint, flux_gradient


def solution(mesh):
    return jax.shard_map(
        per_device,
        mesh=mesh,
        in_specs=(
            P("groups", "levels", "tiles", "sub"),
            P(("groups", "levels"), "tiles", "sub"),
            P(("groups", "levels"), "tiles", "sub"),
            P(None, ("groups", "levels"), "tiles", "sub"),
            P(("groups", "levels"), "tiles", "sub"),
            P("levels"),
            P(("groups", "tiles", "sub"), None),
            P(("groups", "tiles", "sub")),
            P(None, ("groups", "tiles", "sub")),
            P("levels", ("groups", "tiles", "sub")),
        ),
        out_specs=(P("groups", "levels", "tiles", "sub"), P("groups", ("tiles", "levels"), "sub")),
        check_vma=False,
    )
```
